32 devices in a mesh: dp: 8 (over z, x), mp: 4 (over y, core).
Axes of the slice: x: 2, y: 2, z: 4, core: 2. Of those that a mesh axis runs over, the one named last changes fastest.
Arguments:
- latents: bfloat16 [16, 1024, 32], P('dp', 'mp'), may hold values from -6 to 6
- noise: bfloat16 [16, 1024, 32], P('dp', 'mp'), may hold values from -6 to 6
- captions: bfloat16 [16, 512, 2304], P('dp', 'mp'), may hold values from -6 to 6
- res_ids: int32 [16], P('dp'), may hold values from 0 to 1, as said below
- timesteps: int32 [16, 4], P('dp'), may hold values from 0 to 999
- caption_lengths: int32 [16, 4], P('dp'), may hold values from 0 to 300, as said below
- in_proj: float32 [1152, 6, 1152], P('dp', None, 'mp'), may hold values from -0.1875 to 0.1875
- out_proj: float32 [2, 1152, 1152], P(None, 'mp', 'dp'), may hold values from -0.75 to 0.75
- w_up: float32 [1152, 2, 2880], P('dp', None, 'mp'), may hold values from -0.1875 to 0.1875
- w_down: float32 [2880, 1152], P('mp', 'dp'), may hold values from -0.109375 to 0.109375
- cond: float32 [11776, 1152], P(('dp', 'mp')), may hold values from -0.1875 to 0.1875
- conv: float32 [2, 10, 2880], replicated, may hold values from -0.4 to 0.4
- tables: float32 [73, 1152], replicated
- mom_in: float32 [1152, 6, 1152], P('dp', None, 'mp'), may hold values from -9.536743e-07 to 9.536743e-07
- mom_out: float32 [2, 1152, 1152], P(None, 'mp', 'dp'), may hold values from -9.536743e-07 to 9.536743e-07
- mom_up: float32 [1152, 2, 2880], P('dp', None, 'mp'), may hold values from -9.536743e-07 to 9.536743e-07
- mom_down: float32 [2880, 1152], P('mp', 'dp'), may hold values from -9.536743e-07 to 9.536743e-07
- mom_cond: float32 [11776, 1152], P(('dp', 'mp')), may hold values from -9.536743e-07 to 9.536743e-07
- mom_conv: float32 [2, 10, 2880], replicated, may hold values from -2.861023e-06 to 2.861023e-06
- mom_tables: float32 [73, 1152], replicated, may hold values from -2.861023e-06 to 2.861023e-06
- avg_in: float32 [1152, 6, 1152], P('dp', None, 'mp'), may hold values from -0.1875 to 0.1875
- avg_out: float32 [2, 1152, 1152], P(None, 'mp', 'dp'), may hold values from -0.75 to 0.75
- avg_up: float32 [1152, 2, 2880], P('dp', None, 'mp'), may hold values from -0.1875 to 0.1875
- avg_down: float32 [2880, 1152], P('mp', 'dp'), may hold values from -0.109375 to 0.109375
- avg_cond: float32 [11776, 1152], P(('dp', 'mp')), may hold values from -0.1875 to 0.1875
- avg_conv: float32 [2, 10, 2880], replicated, may hold values from -0.4 to 0.4
- avg_tables: float32 [73, 1152], replicated, may hold values from -1.75 to 1.75
Outputs:
- loss: float32 [], replicated
- grad_norm: float32 [], replicated
- new_in_proj: float32 [1152, 6, 1152], P('dp', None, 'mp')
- new_out_proj: float32 [2, 1152, 1152], P(None, 'mp', 'dp')
- new_w_up: float32 [1152, 2, 2880], P('dp', None, 'mp')
- new_w_down: float32 [2880, 1152], P('mp', 'dp')
- new_cond: float32 [11776, 1152], P(('dp', 'mp'))
- new_conv: float32 [2, 10, 2880], replicated
- new_tables: float32 [73, 1152], replicated
- new_mom_in: float32 [1152, 6, 1152], P('dp', None, 'mp')
- new_mom_out: float32 [2, 1152, 1152], P(None, 'mp', 'dp')
- new_mom_up: float32 [1152, 2, 2880], P('dp', None, 'mp')
- new_mom_down: float32 [2880, 1152], P('mp', 'dp')
- new_mom_cond: float32 [11776, 1152], P(('dp', 'mp'))
- clipped_conv: float32 [2, 10, 2880], replicated
- new_mom_tables: float32 [73, 1152], replicated
- new_avg_in: float32 [1152, 6, 1152], P('dp', None, 'mp')
- new_avg_out: float32 [2, 1152, 1152], P(None, 'mp', 'dp')
- new_avg_up: float32 [1152, 2, 2880], P('dp', None, 'mp')
- new_avg_down: float32 [2880, 1152], P('mp', 'dp')
- new_avg_cond: float32 [11776, 1152], P(('dp', 'mp'))
- new_avg_conv: float32 [2, 10, 2880], replicated
- new_avg_tables: float32 [73, 1152], replicated
The draws below stay inside these ranges and needn't reach their ends.
Inputs may be any that keep to these rules, and one draw needn't show every extreme that they name: `res_ids`: 0 or 1; both occur. `caption_lengths`: for res 0 all four slots have lengths of 1 to 128; for res 1 slot 0 has 75 to 300 and the others 0; some caption has exactly 300 tokens.
All inputs are finite; a program needn't handle non-finite values.
Results may differ from the reference program's by a relative error of at most 0.0059.
Values may be sent and summed in bfloat16 or wider, within the bound.
A program may use at most 512 MiB of HBM per device.

```python
import math
import jax
import jax.numpy as jnp
from jax import lax

D = 1152
HEADS = 36
XHEADS = 16
FF = 2880
CAPD = 2304
CIN = 32
FREQ = 256
CANVAS = 32
TXT = 512
CAPLEN = 300
HEAD_DIM = 32
XHEAD_DIM = 72
CANVASES = 16
PARAMS = 34277760


def canvas_layout(key):
    base = jax.random.fold_in(key, 7)
    first_key, second_key, third_key = jax.random.split(base, 3)
    resolution = jax.random.randint(first_key, (CANVASES,), 0, 2)
    resolution = resolution.at[0].set(1).at[1].set(0)
    single_len = jax.random.randint(second_key, (CANVASES, 1), CAPLEN // 4, CAPLEN + 1)
    single_len = single_len.at[0, 0].set(CAPLEN)
    many_len = jax.random.randint(third_key, (CANVASES, 4), 1, TXT // 4 + 1)
    single = jnp.concatenate([single_len, jnp.zeros((CANVASES, 3), jnp.int32)], axis=1)
    lengths = jnp.where(resolution[:, None] == 0, many_len, single)
    return (resolution.astype(jnp.int32), lengths.astype(jnp.int32))


def draw_res_ids(key, part):
    return canvas_layout(key)[0]


def draw_caption_lengths(key, part):
    return canvas_layout(key)[1]


def draw_tables(key, part):
    row_ids = jnp.arange(9 + 2 * CIN)[:, None]
    values = jax.random.normal(key, (9 + 2 * CIN, D), jnp.float32)
    scales = jnp.where(row_ids < 8, 0.5, jnp.where(row_ids < 9, 0.1, jnp.where(row_ids < 9 + CIN, CIN ** (-0.5), 0.5 * D ** (-0.5))))
    values = values * scales
    return jnp.where(row_ids == 8, 1.0 + values, values).astype(jnp.float32)


def with_ends(values, key, low, largest):
    extent = values.shape
    place = [jax.random.randint(jax.random.fold_in(key, axis), (), 0, extent[axis]) for axis in range(len(extent))]
    values = values.at[tuple(place)].set(low)
    longest = extent.index(max(extent))
    place[longest] = (place[longest] + 1) % extent[longest]
    return values.at[tuple(place)].set(largest)


def level_of(stream_key, extent, cuts, smallest, high):
    level = 1.0
    for axis_at, parts in cuts:
        steps = jax.random.uniform(jax.random.fold_in(jax.random.fold_in(stream_key, 6), axis_at), (parts,), jnp.float32, smallest / len(cuts), high / len(cuts))
        level = level * jnp.repeat(jnp.exp(steps), extent[axis_at] // parts).reshape((-1,) + (1,) * (len(extent) - 1 - axis_at))
    return level


def bell_draw(rng, extent, deviation, limit, shards=(), held_as=jnp.bfloat16):
    drawn = deviation * jax.random.normal(rng, extent, jnp.float32)
    if shards:
        drawn = drawn * level_of(rng, extent, shards, -0.22, 0.18)
    return jnp.clip(drawn, -limit, limit).astype(held_as)


def setup_inputs(seed: int = 0) -> dict:
    key_list = jax.random.split(jax.random.key(seed), 28)
    latents = bell_draw(key_list[0], (CANVASES, CANVAS * CANVAS, CIN), 1.0, 6.0, ((0, 8), (1, 4)))
    noise = bell_draw(key_list[1], (CANVASES, CANVAS * CANVAS, CIN), 1.0, 6.0, ((0, 8), (1, 4)))
    captions = bell_draw(key_list[2], (CANVASES, TXT, CAPD), 1.0, 6.0, ((0, 8), (1, 4)))
    res_ids = draw_res_ids(jax.random.fold_in(key_list[27], 71), 0)
    timesteps = with_ends(jax.random.randint(key_list[4], (CANVASES, 4), 0, 1000), jax.random.fold_in(key_list[4], 1), 0, 999).astype(jnp.int32)
    caption_lengths = draw_caption_lengths(jax.random.fold_in(key_list[27], 71), 0)
    in_proj = bell_draw(key_list[6], (D, 6, D), D ** -0.5, 0.1875, ((0, 8), (2, 4)), jnp.float32)
    out_proj = bell_draw(key_list[7], (2, D, D), (D // 16) ** -0.5, 0.75, ((1, 4), (2, 8)), jnp.float32)
    w_up = bell_draw(key_list[8], (D, 2, FF), D ** -0.5, 0.1875, ((0, 8), (2, 4)), jnp.float32)
    w_down = bell_draw(key_list[9], (FF, D), FF ** -0.5, 0.109375, ((0, 4), (1, 8)), jnp.float32)
    cond = bell_draw(key_list[10], (FREQ + CAPD + 8 * D, D), D ** -0.5, 0.1875, ((0, 32),), jnp.float32)
    conv = jnp.clip(jax.random.uniform(key_list[11], (2, 10, FF), jnp.float32, -0.4, 0.4), -0.4, 0.4)
    tables = draw_tables(jax.random.fold_in(key_list[27], 71), 0)
    mom_in = bell_draw(key_list[13], (D, 6, D), (0.001 / PARAMS ** 0.5), 9.5367431640625e-07, ((0, 8), (2, 4)), jnp.float32)
    mom_out = bell_draw(key_list[14], (2, D, D), (0.001 / PARAMS ** 0.5), 9.5367431640625e-07, ((1, 4), (2, 8)), jnp.float32)
    mom_up = bell_draw(key_list[15], (D, 2, FF), (0.001 / PARAMS ** 0.5), 9.5367431640625e-07, ((0, 8), (2, 4)), jnp.float32)
    mom_down = bell_draw(key_list[16], (FF, D), (0.001 / PARAMS ** 0.5), 9.5367431640625e-07, ((0, 4), (1, 8)), jnp.float32)
    mom_cond = bell_draw(key_list[17], (FREQ + CAPD + 8 * D, D), (0.001 / PARAMS ** 0.5), 9.5367431640625e-07, ((0, 32),), jnp.float32)
    mom_conv = bell_draw(key_list[18], (2, 10, FF), (0.003 / PARAMS ** 0.5), 2.86102294921875e-06, (), jnp.float32)
    mom_tables = bell_draw(key_list[19], (9 + 2 * CIN, D), (0.003 / PARAMS ** 0.5), 2.86102294921875e-06, (), jnp.float32)
    avg_in = bell_draw(key_list[20], (D, 6, D), D ** -0.5, 0.1875, ((0, 8), (2, 4)), jnp.float32)
    avg_out = bell_draw(key_list[21], (2, D, D), (D // 16) ** -0.5, 0.75, ((1, 4), (2, 8)), jnp.float32)
    avg_up = bell_draw(key_list[22], (D, 2, FF), D ** -0.5, 0.1875, ((0, 8), (2, 4)), jnp.float32)
    avg_down = bell_draw(key_list[23], (FF, D), FF ** -0.5, 0.109375, ((0, 4), (1, 8)), jnp.float32)
    avg_cond = bell_draw(key_list[24], (FREQ + CAPD + 8 * D, D), D ** -0.5, 0.1875, ((0, 32),), jnp.float32)
    avg_conv = jnp.clip(jax.random.uniform(key_list[25], (2, 10, FF), jnp.float32, -0.4, 0.4), -0.4, 0.4)
    avg_tables = bell_draw(key_list[26], (9 + 2 * CIN, D), 0.3, 1.75, (), jnp.float32)
    return dict(latents=latents, noise=noise, captions=captions, res_ids=res_ids, timesteps=timesteps, caption_lengths=caption_lengths, in_proj=in_proj, out_proj=out_proj, w_up=w_up, w_down=w_down, cond=cond, conv=conv, tables=tables, mom_in=mom_in, mom_out=mom_out, mom_up=mom_up, mom_down=mom_down, mom_cond=mom_cond, mom_conv=mom_conv, mom_tables=mom_tables, avg_in=avg_in, avg_out=avg_out, avg_up=avg_up, avg_down=avg_down, avg_cond=avg_cond, avg_conv=avg_conv, avg_tables=avg_tables)


@jax.custom_vjp
def low(v):
    return lax.optimization_barrier(v.astype(jnp.bfloat16)).astype(jnp.float32)

@jax.custom_vjp
def low_back(v):
    return v

def low_keep(v):
    return (low(v), None)

def low_pass(kept, grad):
    return (grad,)

def back_keep(v):
    return (v, None)

def back_low(kept, grad):
    return (low(grad),)
low.defvjp(low_keep, low_pass)
low_back.defvjp(back_keep, back_low)
HIGH = lax.Precision.HIGHEST
EPS = 1e-06
CLIP = 0.001
MOMENTUM = 0.9
AVERAGE_RATE = 0.1
STEP_SCALE = 0.01
TMAX = 1000.0
MASKED = -1e+30

def exact_dot(left, right):
    return jnp.dot(left, right, precision=HIGH, preferred_element_type=jnp.float32)

def layer_norm(value):
    centred = value - lax.optimization_barrier(jnp.mean(value, -1, keepdims=True))
    return centred * lax.rsqrt(lax.optimization_barrier(jnp.mean(centred * centred, -1, keepdims=True)) + EPS)

def modulate(value, shift, scale):
    return layer_norm(value) * (1.0 + scale) + shift

def rms_norm(value, gain):
    return value * lax.rsqrt(lax.optimization_barrier(jnp.mean(value * value, -1, keepdims=True)) + EPS) * gain

def time_embed(steps_t):
    half_size = FREQ // 2
    freqs = jnp.exp(-math.log(10000.0) * jnp.arange(half_size, dtype=jnp.float32) / half_size)
    angles = steps_t.astype(jnp.float32)[:, None] * freqs[None, :]
    return jnp.concatenate([jnp.cos(angles), jnp.sin(angles)], axis=1)

def geometry(resolution, lengths):
    position = jnp.arange(CANVAS * CANVAS, dtype=jnp.int32)
    half_side = CANVAS // 2
    quadrant = position // CANVAS // half_side * 2 + position % CANVAS // half_side
    segment = jnp.where(resolution == 0, quadrant, 0).astype(jnp.int32)
    length_ends = jnp.cumsum(lengths).astype(jnp.int32)
    text_pos = jnp.arange(TXT, dtype=jnp.int32)
    text_segment = lax.optimization_barrier(jnp.sum((text_pos[:, None] >= length_ends[None, :]).astype(jnp.int32), axis=1))
    return (segment, text_segment)

def depthwise(activity, kernel, segment):
    channels = activity.shape[2]
    grid_act = activity.reshape(CANVAS, CANVAS, 2, channels)
    grid_seg = segment.reshape(CANVAS, CANVAS)
    padded = jnp.pad(grid_act, ((1, 1), (1, 1), (0, 0), (0, 0)))
    seg_pad = jnp.pad(grid_seg, 1, constant_values=-1)
    total = jnp.zeros_like(grid_act) + kernel[:, 9][None, None]
    for row_off in range(3):
        for col_off in range(3):
            nearby = padded[row_off:row_off + CANVAS, col_off:col_off + CANVAS]
            same_img = (seg_pad[row_off:row_off + CANVAS, col_off:col_off + CANVAS] == grid_seg).astype(jnp.float32)
            total = total + nearby * same_img[:, :, None, None] * kernel[:, row_off * 3 + col_off][None, None]
    return total.reshape(activity.shape)

def conv_glu(segment, upper, kernel):
    mixed = depthwise(jax.nn.silu(upper), kernel, segment)
    return mixed[:, 0] * jax.nn.silu(mixed[:, 1])

def linear_attention(onehot, query, keys, values):
    state = jnp.einsum('ps,phd,phe->shde', onehot, keys, values, precision=HIGH)
    key_sum = jnp.einsum('ps,phd->shd', onehot, keys, precision=HIGH)
    numer = jnp.einsum('ps,phd,shde->phe', onehot, query, state, precision=HIGH)
    denom = jnp.einsum('ps,phd,shd->ph', onehot, query, key_sum, precision=HIGH) + 1.0
    return numer / denom[:, :, None]

def canvas_loss(weights, latent, noise_c, caption, resolution, steps_t, lengths, count):
    in_proj, out_proj, w_up, w_down, cond, conv, tables = weights
    tokens_all = CANVAS * CANVAS
    segment, text_segment = geometry(resolution, lengths)
    onehot = (segment[:, None] == jnp.arange(4, dtype=jnp.int32)[None, :]).astype(jnp.float32)
    sigma = exact_dot(onehot, steps_t.astype(jnp.float32)[:, None] / TMAX)
    mixed_in = (1.0 - sigma) * latent + sigma * noise_c
    target = noise_c - latent
    w_in = low(in_proj)
    w_out = low(out_proj)
    w_upper = low(w_up)
    w_lower = low(w_down)
    w_cond = low(cond)
    cap_at = FREQ + D
    block_at = FREQ + CAPD + 2 * D
    time_hidden = exact_dot(low(time_embed(steps_t)), w_cond[:FREQ])
    time_emb = exact_dot(low(jax.nn.silu(time_hidden)), w_cond[FREQ:FREQ + D])
    time_mod = exact_dot(low(jax.nn.silu(time_emb)), w_cond[block_at:].T)
    mods = tables[0:6][None] + exact_dot(onehot, time_mod).reshape(tokens_all, 6, D)
    cap_hidden = low_back(exact_dot(caption, w_cond[cap_at:cap_at + CAPD]))
    cap_act = low(jax.nn.gelu(cap_hidden, approximate=True))
    text_raw = low_back(exact_dot(cap_act, w_cond[cap_at + CAPD:block_at]))
    text_norm = low(rms_norm(text_raw, tables[8]))
    text_kv = low(low_back(jnp.einsum('td,dke->tke', text_norm, w_in[:, 4:6], precision=HIGH)))
    embed = exact_dot(mixed_in, tables[9:9 + CIN])
    normed_a = low(modulate(embed, mods[:, 0], mods[:, 1]))
    qkv_raw = low_back(jnp.einsum('pd,dke->pke', normed_a, w_in[:, 0:3], precision=HIGH))
    qkv = low(jax.nn.relu(qkv_raw)).reshape(tokens_all, 3, HEADS, HEAD_DIM)
    attn = low(linear_attention(onehot, qkv[:, 0], qkv[:, 1], qkv[:, 2]).reshape(tokens_all, D))
    state = embed + mods[:, 2] * low_back(exact_dot(attn, w_out[0]))
    query = low(low_back(exact_dot(low(state), w_in[:, 3]))).reshape(tokens_all, XHEADS, XHEAD_DIM)
    keys = text_kv[:, 0].reshape(TXT, XHEADS, XHEAD_DIM)
    values = text_kv[:, 1].reshape(TXT, XHEADS, XHEAD_DIM)
    match = segment[:, None] == text_segment[None, :]
    scores = low_back(jnp.einsum('phd,thd->hpt', query, keys, precision=HIGH) * XHEAD_DIM ** (-0.5))
    scores = jnp.where(match[None], scores, MASKED)
    probs = low(jax.nn.softmax(scores, axis=-1))
    cross = low(low_back(jnp.einsum('hpt,thd->phd', probs, values, precision=HIGH).reshape(tokens_all, D)))
    state = state + low_back(exact_dot(cross, w_out[1]))
    normed_f = low(modulate(state, mods[:, 3], mods[:, 4]))
    upper = low_back(jnp.einsum('pd,dkf->pkf', normed_f, w_upper, precision=HIGH))
    gated = low(conv_glu(segment, upper, conv))
    state = state + mods[:, 5] * low_back(exact_dot(gated, w_lower))
    shift_scale = tables[6:8][None] + exact_dot(onehot, time_emb)[:, None]
    final = modulate(state, shift_scale[:, 0], shift_scale[:, 1])
    output = jnp.einsum('pd,cd->pc', final, tables[9 + CIN:], precision=HIGH)
    image_tokens = jnp.where(resolution == 0, (CANVAS // 2) ** 2, tokens_all).astype(jnp.float32)
    error = output - target
    return jnp.sum(error * error) / (CIN * image_tokens * count)

def update(weight, grad, moment, average, factor, rate):
    clipped = factor * grad
    moment_new = MOMENTUM * moment + clipped
    weight_new = weight - rate * (clipped + MOMENTUM * moment_new)
    average_new = average + AVERAGE_RATE * (weight_new - average)
    return (weight_new, moment_new, average_new)

def reference(latents, noise, captions, res_ids, timesteps, caption_lengths, in_proj, out_proj, w_up, w_down, cond, conv, tables, mom_in, mom_out, mom_up, mom_down, mom_cond, mom_conv, mom_tables, avg_in, avg_out, avg_up, avg_down, avg_cond, avg_conv, avg_tables):
    count = jnp.sum(jnp.where(res_ids == 0, 4.0, 1.0)).astype(jnp.float32)
    masters = (in_proj, out_proj, w_up, w_down, cond, conv, tables)
    items = (latents.astype(jnp.float32), noise.astype(jnp.float32), captions.astype(jnp.float32), res_ids, timesteps, caption_lengths)
    checked = jax.checkpoint(canvas_loss)

    def total_loss(weights):

        def one_canvas(running, item):
            latent, noise_c, caption, resolution, steps_t, lengths = item
            return (running + checked(weights, latent, noise_c, caption, resolution, steps_t, lengths, count), None)
        result, _ = lax.scan(one_canvas, jnp.zeros((), jnp.float32), items)
        return result
    loss, pull = jax.vjp(total_loss, masters)
    grads = pull(jnp.ones_like(loss))[0]
    norm = jnp.sqrt(sum((jnp.sum(grad * grad) for grad in grads)))
    factor = CLIP / jnp.maximum(norm, CLIP)
    rate = STEP_SCALE * math.sqrt(PARAMS) / CLIP
    moments = (mom_in, mom_out, mom_up, mom_down, mom_cond, mom_conv, mom_tables)
    averages = (avg_in, avg_out, avg_up, avg_down, avg_cond, avg_conv, avg_tables)
    new_sets = [update(masters[index], grads[index], moments[index], averages[index], factor, rate) for index in range(7)]
    clipped_conv = factor * grads[5]
    return (loss, norm, new_sets[0][0], new_sets[1][0], new_sets[2][0], new_sets[3][0], new_sets[4][0], new_sets[5][0], new_sets[6][0], new_sets[0][1], new_sets[1][1], new_sets[2][1], new_sets[3][1], new_sets[4][1], clipped_conv, new_sets[6][1], new_sets[0][2], new_sets[1][2], new_sets[2][2], new_sets[3][2], new_sets[4][2], new_sets[5][2], new_sets[6][2])
```

```python
from functools import partial
import math

import jax
import jax.numpy as jnp
from jax import lax
from jax.experimental import pallas as pl
from jax.experimental.pallas import tpu as pltpu
from jax.sharding import PartitionSpec as P

D = 1152
FF = 2880
CAPD = 2304
CIN = 32
FREQ = 256
SIDE = 32
TXT = 512
HEAD = 32
XHEAD = 72
XHEADS = 16
PARAMS = 34277760
FFB = 768
FFP = 4 * FFB
TIME_ROWS = FREQ + D
CAP_ROWS = CAPD + D
BLOCK_AT = TIME_ROWS + CAP_ROWS

HIGH = lax.Precision.HIGHEST
EPS = 1e-06
CLIP = 0.001
MOMENTUM = 0.9
AVERAGE_RATE = 0.1
STEP_SCALE = 0.01
TMAX = 1000.0
MASKED = -1e30
AXES = ("dp", "mp")
F32 = jnp.float32
BF16 = jnp.bfloat16


def bf(value):
    return value.astype(BF16)


def wide(value):
    return value.astype(F32)


def dot(left, right, dims, precision=None):
    return lax.dot_general(
        left, right, (dims, ((), ())), precision=precision, preferred_element_type=F32
    )


def mm(left, right, precision=None):
    return dot(left, right, ((1,), (0,)), precision)


def mm_nt(left, right, precision=None):
    return dot(left, right, ((1,), (1,)), precision)


def mm_tn(left, right, precision=None):
    return dot(left, right, ((0,), (0,)), precision)


class Place:
    def __init__(self, n_dp, n_mp):
        self.n_dp, self.n_mp, self.n = n_dp, n_mp, n_dp * n_mp
        self.dp, self.mp = lax.axis_index("dp"), lax.axis_index("mp")
        self.me = self.dp * n_mp + self.mp
        self.y, self.c = self.mp // 2, self.mp % 2
        self.dp_bits = int(math.log2(n_dp))

    def bit(self, mask):
        return (self.me // mask) % 2

    def swap(self, value, mask):
        return lax.ppermute(value, AXES, [(i, i ^ mask) for i in range(self.n)])

    @property
    def far_masks(self):
        return [self.n_mp << b for b in range(1, self.dp_bits)]

    @property
    def x_mask(self):
        return self.n_mp


def ordered(bit, mine, theirs, axis):
    low = jnp.where(bit == 0, mine, theirs)
    high = jnp.where(bit == 0, theirs, mine)
    return jnp.concatenate([low, high], axis=axis)


def gather_far(place, block, axis):
    block = jnp.expand_dims(block, axis)
    for mask in place.far_masks:
        block = ordered(place.bit(mask), block, place.swap(block, mask), axis)
    return block


def gather_near(place, block, order):
    held = {0: block}
    for mask in order:
        held.update({key | mask: place.swap(value, mask) for key, value in held.items()})
    return held


def near_bits(place, key):
    flip = [1 if key & mask else 0 for mask in (place.x_mask, 2, 1)]
    own = (place.bit(place.x_mask), place.y, place.c)
    return [jnp.where(f == 1, 1 - o, o) for f, o in zip(flip, own)]


def gather_rows_all(place, block, order):
    rows, cols = block.shape
    held = gather_near(place, gather_far(place, block, 0), order)
    half = place.n_dp // 2
    out = jnp.zeros((half, 2, 2, 2, rows, cols), block.dtype)
    for key, value in held.items():
        x, y, c = near_bits(place, key)
        out = lax.dynamic_update_slice(out, value[:, None, None, None], (0, x, y, c, 0, 0))
    return out.reshape(place.n * rows, cols)


def spread_table(place, owner_rows, low, chunk):
    rounds = -(-owner_rows // chunk) + 1
    tables = []
    for step in range(rounds):
        pairs = []
        for owner in range(place.n):
            target = (owner_rows * owner - low) // chunk + step
            start = low + chunk * target - owner_rows * owner
            if 0 <= target < place.n and -chunk < start < owner_rows:
                pairs.append((owner, target))
        tables.append(pairs)
    return tables


def chunk_of(place, rows):
    chunk = -(-rows // place.n)
    return -(-chunk // 8) * 8


def spread_rows(place, held, low, rows):
    owner_rows = held.shape[0]
    chunk = chunk_of(place, rows)
    padded = jnp.pad(held, ((chunk, chunk), (0, 0)))
    first = (owner_rows * place.me - low) // chunk
    total = None
    for step, pairs in enumerate(spread_table(place, owner_rows, low, chunk)):
        start = low + chunk * (first + step) - owner_rows * place.me + chunk
        piece = lax.dynamic_slice_in_dim(padded, start, chunk, 0)
        got = lax.ppermute(piece, AXES, pairs)
        total = got if total is None else total + got
    return total


def collect_rows(place, block, owner_rows, low, rows):
    chunk = block.shape[0]
    first = (owner_rows * place.me - low) // chunk
    got = [
        lax.ppermute(block, AXES, [(target, owner) for owner, target in pairs])
        for pairs in spread_table(place, owner_rows, low, chunk)
    ]
    start = owner_rows * place.me - low - chunk * first
    mine = lax.dynamic_slice_in_dim(jnp.concatenate(got, axis=0), start, owner_rows, 0)
    row = owner_rows * place.me + jnp.arange(owner_rows, dtype=jnp.int32)[:, None]
    return jnp.where((row >= low) & (row < low + rows), mine, 0.0)


def halve(place, grad, stages):
    for axis, mask in stages:
        bit = place.bit(mask)
        half = grad.shape[axis] // 2
        away = lax.dynamic_slice_in_dim(grad, (1 - bit) * half, half, axis)
        keep = lax.dynamic_slice_in_dim(grad, bit * half, half, axis)
        grad = keep + wide(place.swap(bf(away), mask))
    return grad


def layer_norm(value):
    centred = value - jnp.mean(value, -1, keepdims=True)
    inverse = lax.rsqrt(jnp.mean(centred * centred, -1, keepdims=True) + EPS)
    return centred * inverse, inverse


def layer_norm_back(grad, normed, inverse):
    along = jnp.mean(grad * normed, -1, keepdims=True)
    return inverse * (grad - jnp.mean(grad, -1, keepdims=True) - normed * along)


def silu_grad(value):
    gate = jax.nn.sigmoid(value)
    return gate * (1.0 + value * (1.0 - gate))


def time_embed(steps_t):
    half_size = FREQ // 2
    freqs = jnp.exp(-math.log(10000.0) * jnp.arange(half_size, dtype=F32) / half_size)
    angles = wide(steps_t)[:, None] * freqs[None, :]
    return jnp.concatenate([jnp.cos(angles), jnp.sin(angles)], axis=1)


def to_ff(value):
    blocks = value.reshape(value.shape[:-1] + (4, FF // 4))
    pad = [(0, 0)] * (blocks.ndim - 1) + [(0, FFB - FF // 4)]
    blocks = jnp.pad(blocks, pad)
    blocks = jnp.stack([blocks[..., m, :] for m in (0, 2, 1, 3)], axis=-2)
    return blocks.reshape(value.shape[:-1] + (FFP,))


def from_ff(value):
    blocks = value.reshape(value.shape[:-1] + (4, FFB))[..., : FF // 4]
    blocks = jnp.stack([blocks[..., m, :] for m in (0, 2, 1, 3)], axis=-2)
    return blocks.reshape(value.shape[:-1] + (FF,))


def unit_split(place, units):
    units = units.reshape((2, 4) + units.shape[1:])

    def part(number):
        return lax.dynamic_index_in_dim(units, number, 1, False)

    got = [part(place.mp)] + [place.swap(part(place.mp ^ m), m) for m in (1, 2, 3)]
    stacked = jnp.stack(got)
    return jnp.concatenate(
        [lax.dynamic_index_in_dim(stacked, place.mp ^ m, 0, False) for m in range(4)], axis=-1
    )


def unit_join(place, block):
    cols = D // 4

    def part(number):
        return lax.dynamic_slice_in_dim(block, number * cols, cols, 2)

    got = [part(place.mp)] + [place.swap(part(place.mp ^ m), m) for m in (1, 2, 3)]
    stacked = jnp.stack(got)
    order = [lax.dynamic_index_in_dim(stacked, place.mp ^ m, 0, False) for m in range(4)]
    return jnp.stack(order, axis=1).reshape((8,) + order[0].shape[1:])


def as_units(in_w, out_w):
    inp = [in_w[:, k] for k in range(6)]
    outp = [out_w[j].T for j in range(2)]
    return jnp.stack([inp[0], inp[1], inp[2], outp[0], inp[3], outp[1], inp[4], inp[5]])


def from_units(units):
    g_in = jnp.stack([units[u] for u in (0, 1, 2, 4, 6, 7)], axis=1)
    g_out = jnp.stack([units[3].T, units[5].T])
    return g_in, g_out


class Flow:
    def __init__(self, place, sends, stages):
        self.place, self.stages = place, list(stages)
        self.keep = None
        self.moving = place.swap(sends, 1)
        self.sends = None

    def launch(self):
        self.moving = self.place.swap(self.sends, self.mask)
        self.sends = None

    def land(self):
        total = self.keep + wide(self.moving)
        self.moving = None
        if not self.stages:
            self.keep = total
            return
        kind, axis, self.mask = self.stages.pop(0)
        if kind == "rel":
            away = lax.slice_in_dim(total, 1, 2, axis=axis)
            self.keep = lax.slice_in_dim(total, 0, 1, axis=axis)
        else:
            bit = self.place.bit(self.mask)
            away = lax.dynamic_slice_in_dim(total, 1 - bit, 1, axis)
            self.keep = lax.dynamic_slice_in_dim(total, bit, 1, axis)
        self.sends = bf(away)

    def drain(self):
        while self.moving is not None:
            self.land()
            if self.sends is not None:
                self.launch()
        return self.keep


def tick(value, flows):
    moving = [flow for flow in flows if flow.moving is not None]
    value, landed = lax.optimization_barrier((value, [flow.moving for flow in moving]))
    for flow, arrived in zip(moving, landed):
        flow.moving = arrived
        flow.land()
    ready = [flow for flow in moving if flow.sends is not None]
    value, sends = lax.optimization_barrier((value, [flow.sends for flow in ready]))
    for flow, out in zip(ready, sends):
        flow.sends = out
        flow.launch()
    return value


CB = 256
ROW = SIDE
LIMIT = 48 * 1024 * 1024


def whole_spec(shape):
    return pl.BlockSpec(shape, lambda *_: (0,) * len(shape))


def ffn_forward_kernel(
    x_ref, w0_ref, w1_ref, wd_ref, taps_ref, left_ref, right_ref, on_ref,
    u_ref, z_ref, g_ref, out_ref, act, act_l, act_r
):
    rows = g_ref.shape[0] // ROW
    zero = jnp.zeros((ROW, CB), F32)
    x = x_ref[...]
    u_ref[0] = mm(x, w0_ref[...].reshape(D, CB))
    u_ref[1] = mm(x, w1_ref[...].reshape(D, CB))
    on = on_ref[0, 0]
    for k in range(2):
        for ref in (act, act_l, act_r):
            ref[k, pl.ds(0, ROW)] = zero

    def fill(r, scale):
        for k in range(2):
            u = u_ref[k, pl.ds(pl.multiple_of(r * ROW, ROW), ROW)]
            a = u * jax.nn.sigmoid(u) * scale
            at = pl.ds(pl.multiple_of(r * ROW + ROW, ROW), ROW)
            act[k, at] = a
            act_l[k, at] = pltpu.roll(a, 1, 0) * left_ref[...]
            act_r[k, at] = pltpu.roll(a, ROW - 1, 0) * right_ref[...]

    @pl.loop(0, rows)
    def _(r):
        fill(r, 1.0)

    fill(rows, on)

    @pl.loop(0, rows)
    def _(r):
        z = []
        for k in range(2):
            total = jnp.broadcast_to(taps_ref[k, pl.ds(9, 1)], (ROW, CB))
            for dr in range(3):
                at = pl.ds(pl.multiple_of(r * ROW + dr * ROW, ROW), ROW)
                for dc, ref in enumerate((act_l, act, act_r)):
                    total = total + ref[k, at] * taps_ref[k, pl.ds(dr * 3 + dc, 1)]
            z_ref[k, pl.ds(pl.multiple_of(r * ROW, ROW), ROW)] = total
            z.append(total)
        gated = z[0] * (z[1] * jax.nn.sigmoid(z[1]))
        g_ref[pl.ds(pl.multiple_of(r * ROW, ROW), ROW)] = bf(gated)

    part = mm_nt(g_ref[...], wd_ref[...].reshape(D, CB))

    @pl.when(pl.program_id(0) == 0)
    def _():
        out_ref[...] = part

    @pl.when(pl.program_id(0) > 0)
    def _():
        out_ref[...] += part


def ff_spec(ffw, k):
    groups, blocks, rows, lanes = ffw.shape
    per = lanes // CB

    def index(j):
        at = j // per
        return (0, at % 2 * 2 + at // 2 if blocks == 4 else 0, k, j % per)

    return pl.BlockSpec((groups, 1, rows // 3, CB), index)


def ffn_forward(x_ext, ffw, taps, left_ok, right_ok, on):
    n_ext = x_ext.shape[0]
    n_tok = n_ext - ROW
    weight = partial(ff_spec, ffw)
    pads = pltpu.VMEM((2, n_ext + ROW, CB), F32)
    return pl.pallas_call(
        ffn_forward_kernel,
        grid=(FFP // CB,),
        in_specs=[
            whole_spec((n_ext, D)), weight(0), weight(1), weight(2),
            pl.BlockSpec((2, 10, CB), lambda j: (0, 0, j)),
            whole_spec((ROW, CB)), whole_spec((ROW, CB)),
            pl.BlockSpec((1, 1), lambda j: (0, 0), memory_space=pltpu.SMEM),
        ],
        out_specs=[
            pl.BlockSpec((2, n_ext, CB), lambda j: (0, 0, j)),
            pl.BlockSpec((2, n_tok, CB), lambda j: (0, 0, j)),
            pl.BlockSpec((n_tok, CB), lambda j: (0, j)),
            whole_spec((n_tok, D)),
        ],
        out_shape=[
            jax.ShapeDtypeStruct((2, n_ext, FFP), F32),
            jax.ShapeDtypeStruct((2, n_tok, FFP), F32),
            jax.ShapeDtypeStruct((n_tok, FFP), BF16),
            jax.ShapeDtypeStruct((n_tok, D), F32),
        ],
        scratch_shapes=[pads, pads, pads],
        compiler_params=pltpu.CompilerParams(
            dimension_semantics=("arbitrary",), vmem_limit_bytes=LIMIT
        ),
        cost_estimate=pl.CostEstimate(
            flops=2 * n_ext * D * FFP * 3, bytes_accessed=50 * 2**20, transcendentals=n_ext * FFP * 3
        ),
    )(x_ext, ffw, ffw, ffw, taps, left_ok, right_ok, on)


def ffn_backward_kernel(
    d_ref, wd_ref, w0_ref, w1_ref, u_ref, z_ref, zh_ref, taps_ref, left_ref, right_ref, on_ref,
    du_ref, dt_ref, dn_ref, dg_buf, dz, dz_l, dz_r, acc
):
    n_tok = z_ref.shape[1]
    rows = n_tok // ROW
    zero = jnp.zeros((ROW, CB), F32)
    dg_buf[...] = mm(d_ref[...], wd_ref[...].reshape(D, CB))
    for k in range(2):
        for ref in (dz, dz_l, dz_r):
            ref[k, pl.ds(0, ROW)] = zero
    acc[...] = jnp.zeros_like(acc)

    def fill(r, z0, z1, scale, count):
        dg = dg_buf[pl.ds(pl.multiple_of(r * ROW, ROW), ROW)]
        gate = jax.nn.sigmoid(z1)
        soft = z1 * gate
        at = pl.ds(pl.multiple_of(r * ROW + ROW, ROW), ROW)
        d_both = (dg * soft, dg * z0 * (gate + soft * (1.0 - gate)))
        for k in range(2):
            value = d_both[k] * scale
            dz[k, at] = value
            dz_l[k, at] = pltpu.roll(value * left_ref[...], ROW - 1, 0)
            dz_r[k, at] = pltpu.roll(value * right_ref[...], 1, 0)
            if count:
                acc[k, 9] += fold(value)

    def fold(value):
        return value[0:8] + value[8:16] + value[16:24] + value[24:32]

    @pl.loop(0, rows)
    def _(r):
        at = pl.ds(pl.multiple_of(r * ROW, ROW), ROW)
        fill(r, z_ref[0, at], z_ref[1, at], 1.0, True)

    fill(rows, zh_ref[0], zh_ref[1], on_ref[0, 0], False)

    def back(r, taps_on):
        at = pl.ds(pl.multiple_of(r * ROW, ROW), ROW)
        for k in range(2):
            u = u_ref[k, at]
            gate = jax.nn.sigmoid(u)
            a = u * gate
            total = zero
            for dr in range(3):
                near = pl.ds(pl.multiple_of(r * ROW + (2 - dr) * ROW, ROW), ROW)
                for dc, ref in enumerate((dz_l, dz, dz_r)):
                    value = ref[k, near]
                    total = total + value * taps_ref[k, pl.ds(dr * 3 + dc, 1)]
                    if dr in taps_on:
                        acc[k, dr * 3 + dc] += fold(value * a)
            du_ref[k, at] = bf(total * (gate + a * (1.0 - gate)))

    @pl.loop(0, rows - 1)
    def _(r):
        back(r, (0, 1, 2))

    back(rows - 1, (1, 2))
    for k in range(2):
        u = u_ref[k, pl.ds(n_tok, ROW)]
        a = u * jax.nn.sigmoid(u) * on_ref[0, 0]
        for dc, ref in enumerate((dz_l, dz, dz_r)):
            acc[k, 6 + dc] += fold(ref[k, pl.ds(n_tok, ROW)] * a)
        for t in range(10):
            dt_ref[k, pl.ds(t, 1)] = jnp.sum(acc[k, t], axis=0, keepdims=True)

    part = mm_nt(du_ref[0], w0_ref[...].reshape(D, CB))
    part = part + mm_nt(du_ref[1], w1_ref[...].reshape(D, CB))

    @pl.when(pl.program_id(0) == 0)
    def _():
        dn_ref[...] = part

    @pl.when(pl.program_id(0) > 0)
    def _():
        dn_ref[...] += part


def ffn_backward(d_ext, ffw, upper, z, z_halo, taps, left_ok, right_ok, on):
    n_ext = d_ext.shape[0]
    n_tok = n_ext - ROW
    pads = pltpu.VMEM((2, n_ext + ROW, CB), F32)
    return pl.pallas_call(
        ffn_backward_kernel,
        grid=(FFP // CB,),
        in_specs=[
            whole_spec((n_ext, D)),
            ff_spec(ffw, 2), ff_spec(ffw, 0), ff_spec(ffw, 1),
            pl.BlockSpec((2, n_ext, CB), lambda j: (0, 0, j)),
            pl.BlockSpec((2, n_tok, CB), lambda j: (0, 0, j)),
            pl.BlockSpec((2, ROW, CB), lambda j: (0, 0, j)),
            pl.BlockSpec((2, 10, CB), lambda j: (0, 0, j)),
            whole_spec((ROW, CB)), whole_spec((ROW, CB)),
            pl.BlockSpec((1, 1), lambda j: (0, 0), memory_space=pltpu.SMEM),
        ],
        out_specs=[
            pl.BlockSpec((2, n_tok, CB), lambda j: (0, 0, j)),
            pl.BlockSpec((2, 10, CB), lambda j: (0, 0, j)),
            whole_spec((n_tok, D)),
        ],
        out_shape=[
            jax.ShapeDtypeStruct((2, n_tok, FFP), BF16),
            jax.ShapeDtypeStruct((2, 10, FFP), F32),
            jax.ShapeDtypeStruct((n_tok, D), F32),
        ],
        scratch_shapes=[
            pltpu.VMEM((n_ext, CB), F32), pads, pads, pads, pltpu.VMEM((2, 10, 8, CB), F32)
        ],
        compiler_params=pltpu.CompilerParams(
            dimension_semantics=("arbitrary",), vmem_limit_bytes=LIMIT
        ),
        cost_estimate=pl.CostEstimate(
            flops=2 * n_ext * D * FFP * 3, bytes_accessed=50 * 2**20, transcendentals=n_ext * FFP * 3
        ),
    )(d_ext, ffw, ffw, ffw, upper, z, z_halo, taps, left_ok, right_ok, on)


def ff_grad_kernel(spot_ref, left_ref, right_ref, out_ref):
    out_ref[0, 0] = mm_tn(left_ref[...], right_ref[0]).astype(out_ref.dtype)


def ff_grad(spot, left, right, away, dtype):
    n_tok = left.shape[0]
    count = right.shape[0]

    def lanes(k, r, spot_ref):
        return (k, 0, (spot_ref[1] + away) % 2 * 2 + (spot_ref[0] + r) % 2)

    return pl.pallas_call(
        ff_grad_kernel,
        grid_spec=pltpu.PrefetchScalarGridSpec(
            num_scalar_prefetch=1,
            grid=(count, 2),
            in_specs=[
                pl.BlockSpec((n_tok, D), lambda k, r, spot_ref: (0, 0)),
                pl.BlockSpec((1, n_tok, FFB), lanes),
            ],
            out_specs=pl.BlockSpec((1, 1, D, FFB), lambda k, r, spot_ref: (k, r, 0, 0)),
        ),
        out_shape=jax.ShapeDtypeStruct((count, 2, D, FFB), dtype),
        compiler_params=pltpu.CompilerParams(
            dimension_semantics=("arbitrary", "arbitrary"), vmem_limit_bytes=LIMIT
        ),
        cost_estimate=pl.CostEstimate(
            flops=4 * count * n_tok * D * FFB, bytes_accessed=6 * count * D * FFB, transcendentals=0
        ),
    )(spot, left, right)


def unit_grad_kernel(pairs, away, spot_ref, *refs):
    out_ref = refs[-1]
    unit = (spot_ref[0] + pl.program_id(0)) % 2 * 2 + (spot_ref[1] + away) % 2
    step = D // 3
    for number, (left, right) in enumerate(pairs):

        @pl.when(unit == number)
        def _():
            for i in range(3):
                rows = pl.ds(i * step, step)
                value = mm_tn(refs[left][:, rows], refs[right][...])
                out_ref[0, rows] = value.astype(out_ref.dtype)


def unit_grad(spot, arrays, pairs, away, dtype):
    n_tok = arrays[0].shape[0]
    return pl.pallas_call(
        partial(unit_grad_kernel, pairs, away),
        grid_spec=pltpu.PrefetchScalarGridSpec(
            num_scalar_prefetch=1,
            grid=(2,),
            in_specs=[pl.BlockSpec(a.shape, lambda r, spot_ref: (0, 0)) for a in arrays],
            out_specs=pl.BlockSpec((1, D, D), lambda r, spot_ref: (r, 0, 0)),
        ),
        out_shape=jax.ShapeDtypeStruct((2, D, D), dtype),
        compiler_params=pltpu.CompilerParams(
            dimension_semantics=("arbitrary",), vmem_limit_bytes=LIMIT
        ),
        cost_estimate=pl.CostEstimate(
            flops=4 * n_tok * D * D, bytes_accessed=16 * D * D, transcendentals=0
        ),
    )(spot, *arrays)


WIN = 256
QROWS = 512
BROWS = 256


def head_window(h):
    start = jnp.minimum(h * XHEAD // 128 * 128, D - WIN)
    lane = lax.broadcasted_iota(jnp.int32, (1, WIN), 1)
    mask = (lane >= h * XHEAD - start) & (lane < h * XHEAD - start + XHEAD)
    return pl.ds(pl.multiple_of(start, 128), WIN), mask


def cross_probs(q, keys, token_seg, text_seg):
    scores = mm_nt(q, keys) * XHEAD ** (-0.5)
    scores = jnp.where(token_seg == text_seg, scores, MASKED)
    top = jnp.max(scores, axis=-1, keepdims=True)
    probs = jnp.exp(scores - top)
    return probs * (1.0 / jnp.sum(probs, axis=-1, keepdims=True))


def cross_forward_kernel(q_ref, k_ref, v_ref, tok_ref, txt_ref, out_ref):
    win, mask = head_window(pl.program_id(0))
    keys, values = k_ref[:, win], v_ref[:, win]

    @pl.loop(0, q_ref.shape[0] // QROWS)
    def _(i):
        at = pl.ds(pl.multiple_of(i * QROWS, QROWS), QROWS)
        q = jnp.where(mask, q_ref[at, win], jnp.zeros((), BF16))
        probs = bf(cross_probs(q, keys, tok_ref[at, 0:1], txt_ref[...]))
        out_ref[at, win] = jnp.where(mask, bf(mm(probs, values)), out_ref[at, win])


def cross_forward(q, keys, values, token_seg, text_seg):
    n_tok = q.shape[0]
    n_txt = keys.shape[0]
    return pl.pallas_call(
        cross_forward_kernel,
        grid=(XHEADS,),
        in_specs=[
            whole_spec((n_tok, D)), whole_spec((n_txt, D)), whole_spec((n_txt, D)),
            whole_spec((n_tok, 1)), whole_spec((1, n_txt)),
        ],
        out_specs=whole_spec((n_tok, D)),
        out_shape=jax.ShapeDtypeStruct((n_tok, D), BF16),
        compiler_params=pltpu.CompilerParams(
            dimension_semantics=("arbitrary",), vmem_limit_bytes=LIMIT
        ),
        cost_estimate=pl.CostEstimate(
            flops=4 * n_tok * n_txt * WIN * XHEADS, bytes_accessed=5 * 2**20,
            transcendentals=n_tok * n_txt * XHEADS
        ),
    )(q, keys, values, token_seg, text_seg)


def cross_backward_kernel(
    q_ref, k_ref, v_ref, dc_ref, tok_ref, txt_ref, dq_ref, dk_ref, dv_ref, dk_acc, dv_acc
):
    win, mask = head_window(pl.program_id(0))
    keys, values = k_ref[:, win], v_ref[:, win]
    scale = XHEAD ** (-0.5)
    none = jnp.zeros((), BF16)
    dk_acc[...] = jnp.zeros_like(dk_acc)
    dv_acc[...] = jnp.zeros_like(dv_acc)

    @pl.loop(0, q_ref.shape[0] // BROWS)
    def _(i):
        at = pl.ds(pl.multiple_of(i * BROWS, BROWS), BROWS)
        q = jnp.where(mask, q_ref[at, win], none)
        dc = jnp.where(mask, dc_ref[at, win], none)
        probs = cross_probs(q, keys, tok_ref[at, 0:1], txt_ref[...])
        d_probs = mm_nt(dc, values)
        along = jnp.sum(probs * d_probs, axis=-1, keepdims=True)
        d_scores = bf(probs * (d_probs - along))
        dq_ref[at, win] = jnp.where(mask, bf(mm(d_scores, keys) * scale), dq_ref[at, win])
        dk_acc[...] += mm_tn(d_scores, q)
        dv_acc[...] += mm_tn(bf(probs), dc)

    dk_ref[:, win] = jnp.where(mask, dk_acc[...] * scale, dk_ref[:, win])
    dv_ref[:, win] = jnp.where(mask, dv_acc[...], dv_ref[:, win])


def cross_backward(q, keys, values, d_cross, token_seg, text_seg):
    n_tok = q.shape[0]
    n_txt = keys.shape[0]
    return pl.pallas_call(
        cross_backward_kernel,
        grid=(XHEADS,),
        in_specs=[
            whole_spec((n_tok, D)), whole_spec((n_txt, D)), whole_spec((n_txt, D)),
            whole_spec((n_tok, D)), whole_spec((n_tok, 1)), whole_spec((1, n_txt)),
        ],
        out_specs=[whole_spec((n_tok, D)), whole_spec((n_txt, D)), whole_spec((n_txt, D))],
        out_shape=[
            jax.ShapeDtypeStruct((n_tok, D), BF16),
            jax.ShapeDtypeStruct((n_txt, D), F32),
            jax.ShapeDtypeStruct((n_txt, D), F32),
        ],
        scratch_shapes=[pltpu.VMEM((n_txt, WIN), F32), pltpu.VMEM((n_txt, WIN), F32)],
        compiler_params=pltpu.CompilerParams(
            dimension_semantics=("arbitrary",), vmem_limit_bytes=LIMIT
        ),
        cost_estimate=pl.CostEstimate(
            flops=10 * n_tok * n_txt * WIN * XHEADS, bytes_accessed=12 * 2**20,
            transcendentals=n_tok * n_txt * XHEADS
        ),
    )(q, keys, values, d_cross, token_seg, text_seg)


GL = 128
GROUPS = D // GL


def parts(value):
    high = bf(value)
    return high, bf(value - wide(high))


def group_heads():
    row = lax.broadcasted_iota(jnp.int32, (GL, GL), 0) // HEAD
    col = lax.broadcasted_iota(jnp.int32, (GL, GL), 1) // HEAD
    return wide(row == col)


def both_segments(value, second):
    value = wide(value)
    late = value * second
    return bf(value - late), bf(late)


def state_kernel(k_ref, v_ref, sec_ref, kv_ref, ks_ref):
    same = group_heads()
    k0, k1 = both_segments(k_ref[...], sec_ref[...])
    kv_ref[0, 0] = mm_tn(k0, v_ref[...]) * same
    kv_ref[0, 1] = mm_tn(k1, v_ref[...]) * same
    ks_ref[0, 0] = jnp.broadcast_to(jnp.sum(wide(k0), axis=0, keepdims=True), (8, GL))
    ks_ref[0, 1] = jnp.broadcast_to(jnp.sum(wide(k1), axis=0, keepdims=True), (8, GL))


def attend(q_ref, sec_ref, kv_ref, ks_ref, same):
    q0, q1 = both_segments(q_ref[...], sec_ref[...])
    numer = 0.0
    denom = 1.0
    for i, q in enumerate((q0, q1)):
        for part in parts(kv_ref[0, i]):
            numer = numer + mm(q, part)
        sums = jnp.transpose(jnp.broadcast_to(ks_ref[0, i, 0:1], (GL, GL))) * same
        for part in parts(sums):
            denom = denom + mm(q, part)
    return q0, q1, numer, denom


def attend_kernel(q_ref, sec_ref, kv_ref, ks_ref, out_ref):
    _, _, numer, denom = attend(q_ref, sec_ref, kv_ref, ks_ref, group_heads())
    out_ref[...] = bf(numer / denom)


def attend_back_kernel(q_ref, da_ref, sec_ref, kv_ref, ks_ref, dq_ref, dkv_ref, dks_ref):
    same = group_heads()
    second = sec_ref[...]
    q0, q1, numer, denom = attend(q_ref, sec_ref, kv_ref, ks_ref, same)
    inverse = 1.0 / denom
    d_num = da_ref[...] * inverse
    high, low = parts(d_num * numer)
    ones = bf(same)
    d_den = -(mm(high, ones) + mm(low, ones)) * inverse
    d_parts = parts(d_num)
    back = []
    for i, q in enumerate((q0, q1)):
        total = 0.0
        grad = 0.0
        for part in d_parts:
            total = total + mm_tn(q, part)
        for part in parts(kv_ref[0, i]):
            for left in d_parts:
                grad = grad + mm_nt(left, part)
        dkv_ref[0, i] = total * same
        dks_ref[0, i] = jnp.broadcast_to(
            jnp.sum(wide(q) * d_den, axis=0, keepdims=True), (8, GL)
        )
        back.append(grad + d_den * ks_ref[0, i, 0:1])
    dq = jnp.where(second > 0, back[1], back[0])
    dq_ref[...] = bf(jnp.where(wide(q_ref[...]) > 0, dq, 0.0))


def state_back_kernel(k_ref, v_ref, sec_ref, dkv_ref, dks_ref, dk_ref, dv_ref):
    second = sec_ref[...] > 0
    k, v = k_ref[...], v_ref[...]
    dk, dv = [], []
    for i in range(2):
        grad_k = dks_ref[0, i, 0:1]
        grad_v = 0.0
        for part in parts(dkv_ref[0, i]):
            grad_k = grad_k + mm_nt(v, part)
            grad_v = grad_v + mm(k, part)
        dk.append(grad_k)
        dv.append(grad_v)
    dk_ref[...] = bf(jnp.where(wide(k) > 0, jnp.where(second, dk[1], dk[0]), 0.0))
    dv_ref[...] = bf(jnp.where(wide(v) > 0, jnp.where(second, dv[1], dv[0]), 0.0))


def by_group(kernel, n_tok, ins, outs, out_types):
    specs = dict(
        tok=pl.BlockSpec((n_tok, GL), lambda g: (0, g)),
        seg=whole_spec((n_tok, GL)),
        kv=pl.BlockSpec((1, 2, GL, GL), lambda g: (g, 0, 0, 0)),
        ks=pl.BlockSpec((1, 2, 8, GL), lambda g: (g, 0, 0, 0)),
    )
    shapes = dict(tok=(n_tok, D), kv=(GROUPS, 2, GL, GL), ks=(GROUPS, 2, 8, GL))
    return pl.pallas_call(
        kernel,
        grid=(GROUPS,),
        in_specs=[specs[i] for i in ins],
        out_specs=[specs[o] for o in outs],
        out_shape=[jax.ShapeDtypeStruct(shapes[o], t) for o, t in zip(outs, out_types)],
        compiler_params=pltpu.CompilerParams(
            dimension_semantics=("arbitrary",), vmem_limit_bytes=LIMIT
        ),
        cost_estimate=pl.CostEstimate(
            flops=16 * n_tok * D * GL, bytes_accessed=8 * 2**20, transcendentals=0
        ),
    )


def update(weight, grad, moment, average, factor, rate):
    clipped = factor * grad
    moment_new = MOMENTUM * moment + clipped
    weight_new = weight - rate * (clipped + MOMENTUM * moment_new)
    average_new = average + AVERAGE_RATE * (weight_new - average)
    return (weight_new, moment_new, average_new)


def local(
    n_dp, n_mp,
    latents, noise, captions, res_ids, timesteps, caption_lengths,
    in_proj, out_proj, w_up, w_down, cond, conv, tables,
    mom_in, mom_out, mom_up, mom_down, mom_cond, mom_conv, mom_tables,
    avg_in, avg_out, avg_up, avg_down, avg_cond, avg_conv, avg_tables,
):
    place = Place(n_dp, n_mp)
    y, c = place.y, place.c
    half_dp = n_dp // 2
    dl = D // n_dp
    spot = jnp.stack([y, c]).astype(jnp.int32)
    owner_rows = cond.shape[0]

    cond_b = bf(cond)
    units_b = unit_split(place, as_units(bf(in_proj), bf(out_proj)))
    cap_chunk = chunk_of(place, CAP_ROWS)
    cap_mine = spread_rows(place, cond_b, TIME_ROWS, CAP_ROWS)
    packed = jnp.concatenate([units_b.reshape(-1, D), cap_mine], axis=0)
    ff_b = jnp.stack([bf(w_up[:, 0]), bf(w_up[:, 1]), bf(w_down).T])
    ff_b = jnp.pad(ff_b, ((0, 0), (0, 0), (0, FFB - ff_b.shape[2])))
    packed, ff_b, cond_time = lax.optimization_barrier((packed, ff_b, cond_b))
    got = lax.all_gather(packed, AXES, axis=0)
    by_place = got.reshape((n_dp, 2, 2) + packed.shape)
    w_q, w_k, w_v, w_o0, w_xq, w_o1, w_xk, w_xv = [
        by_place[:, i, j, part * dl : (part + 1) * dl].reshape(D, D)
        for part in (0, 1) for i in (0, 1) for j in (0, 1)
    ]
    cap_w = got[:, 2 * dl :].reshape(-1, D)
    w_cap1, w_cap2 = cap_w[:CAPD], cap_w[CAPD:CAP_ROWS]
    ffw = lax.all_gather(ff_b.reshape(3 * dl, FFB), AXES, axis=0)
    if dl % 16 == 0:
        ffw = ffw.reshape(n_dp, 4, 3 * dl, FFB)
    else:
        ffw = ffw.reshape(n_dp, 2, 2, 3, dl, FFB).transpose(3, 0, 4, 2, 1, 5)
        ffw = ffw.reshape(1, 1, 3 * D, FFP)

    spread_time = spread_rows(place, cond_time, 0, TIME_ROWS)
    w_time = gather_rows_all(place, spread_time, (place.x_mask, 2, 1))[:TIME_ROWS]
    facts = jnp.concatenate([timesteps, res_ids[:, None]], axis=1)
    for b in range(place.dp_bits):
        mask = n_mp << b
        facts = ordered(place.bit(mask), facts, place.swap(facts, mask), 0)
    steps_all = facts[:, :4].reshape(-1)
    count = jnp.sum(jnp.where(facts[:, 4] == 0, 4.0, 1.0))
    slots = steps_all.shape[0]

    resolution = lax.dynamic_index_in_dim(res_ids, y, 0, False)
    lengths = lax.dynamic_index_in_dim(caption_lengths, y, 0, False)
    steps_t = lax.dynamic_index_in_dim(timesteps, y, 0, False)
    pair = jnp.stack([latents, noise])
    quarters = jnp.stack([pair] + [place.swap(pair, mask) for mask in (1, 2, 3)])
    parts = [lax.dynamic_index_in_dim(quarters, (2 * c + j) ^ place.mp, 0, False) for j in (0, 1)]
    tokens = jnp.concatenate(
        [lax.dynamic_index_in_dim(part, y, 1, False) for part in parts], axis=1
    )
    n_tok = tokens.shape[1]
    rows = n_tok // SIDE
    grid = tokens.reshape(2, rows, SIDE, CIN)
    tokens = jnp.where(c == 1, grid[:, ::-1], grid).reshape(2, n_tok, CIN)
    clean, noisy = wide(tokens[0]), wide(tokens[1])
    col = jnp.arange(n_tok, dtype=jnp.int32)[:, None] % SIDE
    second = (col >= SIDE // 2) & (resolution == 0)
    seg0 = jnp.where(resolution == 0, 2 * c, 0)
    seg1 = jnp.where(resolution == 0, 2 * c + 1, 0)
    token_seg = jnp.where(second, seg1, seg0)

    def pick(table):
        first = lax.dynamic_index_in_dim(table, seg0, 0, True)
        other = lax.dynamic_index_in_dim(table, seg1, 0, True)
        return jnp.where(second, other, first)

    def by_segment(value):
        late = jnp.sum(jnp.where(second, value, 0.0), axis=0)
        early = jnp.sum(jnp.where(second, 0.0, value), axis=0)
        slot = jnp.arange(4, dtype=jnp.int32)[:, None]
        table = jnp.where(slot == seg0, early, 0.0) + jnp.where(slot == seg1, late, 0.0)
        return table, early + late

    sigma = pick(wide(steps_t)[:, None] / TMAX)
    mixed_in = (1.0 - sigma) * clean + sigma * noisy
    target = noisy - clean
    image_tokens = jnp.where(resolution == 0, (SIDE // 2) ** 2, SIDE * SIDE).astype(F32)
    loss_weight = 1.0 / (CIN * image_tokens * count)

    freq_b = bf(time_embed(steps_all))
    time_hidden = mm(freq_b, w_time[:FREQ])
    hidden_b = bf(jax.nn.silu(time_hidden))
    time_emb = mm(hidden_b, w_time[FREQ:])
    silu_b = bf(jax.nn.silu(time_emb))
    mod_mine = mm_nt(silu_b, cond_b).reshape(n_dp, 2, 1, 4 * owner_rows)
    mod_send = jnp.broadcast_to(mod_mine, (n_dp, 2, 2, 4 * owner_rows))
    mod_got = lax.all_to_all(mod_send.reshape(place.n, 4 * owner_rows), AXES, 0, 0)
    time_mod = mod_got.reshape(place.n, 4, owner_rows).transpose(1, 0, 2).reshape(4, -1)
    time_mod = time_mod[:, BLOCK_AT:].reshape(4, 6, D)
    mod_table = tables[None, :6] + time_mod
    mods = [pick(mod_table[:, k]) for k in range(6)]
    canvas = place.dp * 2 + y
    emb_mine = lax.dynamic_slice_in_dim(time_emb, canvas * 4, 4, 0)
    emb_tok = pick(emb_mine)

    own_cap = lax.dynamic_index_in_dim(captions, y, 0, False)
    their_cap = lax.dynamic_index_in_dim(captions, 1 - y, 0, False)
    caption = jnp.concatenate([own_cap, place.swap(their_cap, 2)], axis=0)
    quarter = own_cap.shape[0]
    within = jnp.arange(quarter, dtype=jnp.int32)
    text_at = jnp.concatenate([(place.mp ^ m) * quarter + within for m in (0, 2, 1, 3)])
    ends = jnp.cumsum(lengths)
    text_segment = jnp.sum((text_at[:, None] >= ends[None, :]).astype(jnp.int32), axis=1)
    cap_hidden = mm(caption, w_cap1)
    cap_act, gelu_pull = jax.vjp(partial(jax.nn.gelu, approximate=True), cap_hidden)
    cap_act_b = bf(cap_act)
    text_raw = mm(cap_act_b, w_cap2)
    gain = tables[8]
    text_inv = lax.rsqrt(jnp.mean(text_raw * text_raw, -1, keepdims=True) + EPS)
    text_hat = text_raw * text_inv
    text_b = bf(text_hat * gain)
    text_k = bf(mm(text_b, w_xk))
    text_v = bf(mm(text_b, w_xv))
    keys = jnp.concatenate([text_k, place.swap(text_k, 1)], axis=0)
    values = jnp.concatenate([text_v, place.swap(text_v, 1)], axis=0)

    embed = mm(mixed_in, tables[9 : 9 + CIN], HIGH)
    hat_a, inv_a = layer_norm(embed)
    normed_a = bf(hat_a * (1.0 + mods[1]) + mods[0])
    q = bf(jax.nn.relu(mm(normed_a, w_q)))
    k = bf(jax.nn.relu(mm(normed_a, w_k)))
    v = bf(jax.nn.relu(mm(normed_a, w_v)))
    whole_image = wide(resolution == 1)
    second_wide = jnp.broadcast_to(wide(second), (n_tok, GL))

    def shared(state, sums):
        first = jnp.concatenate([state[:, 0], sums[:, 0]], axis=1)
        first = first + whole_image * place.swap(first, 1)
        state = jnp.stack([first[:, :GL], state[:, 1]], axis=1)
        return state, jnp.stack([first[:, GL:], sums[:, 1]], axis=1)

    group_call = partial(by_group, n_tok=n_tok)
    state, key_sum = group_call(
        state_kernel, ins=("tok", "tok", "seg"), outs=("kv", "ks"), out_types=(F32, F32)
    )(k, v, second_wide)
    state, key_sum = shared(state, key_sum)
    (attn_b,) = group_call(
        attend_kernel, ins=("tok", "seg", "kv", "ks"), outs=("tok",), out_types=(BF16,)
    )(q, second_wide, state, key_sum)
    branch_a = mm_nt(attn_b, w_o0)
    state_a = embed + mods[2] * branch_a

    state_b = bf(state_a)
    xq = bf(mm(state_b, w_xq))
    cross_b = cross_forward(xq, keys, values, token_seg, text_segment[None, :])
    state_c = state_a + mm_nt(cross_b, w_o1)

    hat_f, inv_f = layer_norm(state_c)
    normed_f = bf(hat_f * (1.0 + mods[4]) + mods[3])
    taps = to_ff(conv)
    flipped = jnp.concatenate([taps[:, 6:9], taps[:, 3:6], taps[:, 0:3], taps[:, 9:]], axis=1)
    taps = jnp.where(c == 1, flipped, taps)
    column = jnp.arange(SIDE, dtype=jnp.int32)[:, None]
    middle = SIDE // 2
    left_ok = (column != 0) & ((resolution == 1) | (column != middle))
    right_ok = (column != SIDE - 1) & ((resolution == 1) | (column != middle - 1))
    left_ok = jnp.broadcast_to(wide(left_ok), (SIDE, CB))
    right_ok = jnp.broadcast_to(wide(right_ok), (SIDE, CB))
    halo_on = whole_image.reshape(1, 1)
    edge = n_tok - SIDE
    x_ext = jnp.concatenate([normed_f, place.swap(normed_f[edge:], 1)], axis=0)
    upper, z, gated_b, branch_f = ffn_forward(
        x_ext, ffw, taps, left_ok, right_ok, halo_on
    )
    z_halo = place.swap(z[:, edge:], 1)
    state_f = state_c + mods[5] * branch_f

    hat_o, inv_o = layer_norm(state_f)
    shift_o = tables[6] + emb_tok
    scale_o = tables[7] + emb_tok
    final = hat_o * (1.0 + scale_o) + shift_o
    out_rows = tables[9 + CIN :]
    output = mm_nt(final, out_rows, HIGH)
    error = output - target
    loss = jnp.sum(error * error) * loss_weight

    d_output = 2.0 * loss_weight * error
    d_final = mm(d_output, out_rows, HIGH)
    d_out_rows = mm_tn(d_output, final, HIGH)
    d_shift_seg, d_shift_o = by_segment(d_final)
    d_scale_seg, d_scale_o = by_segment(d_final * hat_o)
    d_emb_mine = d_shift_seg + d_scale_seg
    d_state_f = layer_norm_back(d_final * (1.0 + scale_o), hat_o, inv_o)

    split_dp = (2,) * place.dp_bits
    far = [(b, n_mp << (place.dp_bits - 1 - b)) for b in range(place.dp_bits - 2, -1, -1)]

    def stages(lead, order):
        table = {
            "x": ("abs", lead + place.dp_bits - 1, place.x_mask),
            "y": ("rel", lead - 1, 2),
        }
        return [table[o] for o in order] + [("abs", lead + axis, mask) for axis, mask in far]

    def ff_flow(left, right, orders):
        shape = (1, 2) + split_dp + (dl, FFB)
        away = ff_grad(spot, left, right, 1, BF16)
        flows = [
            Flow(place, away[i].reshape(shape), stages(2, order)) for i, order in enumerate(orders)
        ]
        left, right, away = lax.optimization_barrier((left, right, away))
        for i, flow in enumerate(flows):
            flow.keep = ff_grad(spot, left, right[i : i + 1], 0, F32).reshape(shape)
        return flows

    def unit_flow(arrays, pairs, order):
        shape = (2,) + split_dp + (dl, D)
        away = unit_grad(spot, arrays, pairs, 1, BF16)
        flow = Flow(place, away.reshape(shape), stages(1, order))
        arrays, away = lax.optimization_barrier((arrays, away))
        flow.keep = unit_grad(spot, arrays, pairs, 0, F32).reshape(shape)
        return flow

    def settle(value, flows):
        value, keeps = lax.optimization_barrier((value, [flow.keep for flow in flows]))
        for flow, keep in zip(flows, keeps):
            flow.keep = keep
        return tick(value, flows)

    d_branch_f = bf(mods[5] * d_state_f)
    d_edge = place.swap(d_branch_f[edge:], 1)
    flow_dn, = ff_flow(d_branch_f, gated_b[None], ["yx"])
    d_ext = jnp.concatenate([d_branch_f, d_edge], axis=0)
    d_ext = settle(d_ext, [flow_dn])
    d_upper, d_taps, d_normed_f = tick(
        ffn_backward(d_ext, ffw, upper, z, z_halo, taps, left_ok, right_ok, halo_on), [flow_dn]
    )
    unflipped = jnp.concatenate(
        [d_taps[:, 6:9], d_taps[:, 3:6], d_taps[:, 0:3], d_taps[:, 9:]], axis=1
    )
    conv_grad = from_ff(jnp.where(c == 1, unflipped, d_taps))
    flow_up = ff_flow(normed_f, d_upper, ["xy", "yx"])
    ffn_flows = [flow_dn] + flow_up
    d_normed_f = settle(d_normed_f, flow_up)
    d_state_c = d_state_f + layer_norm_back(d_normed_f * (1.0 + mods[4]), hat_f, inv_f)
    d_mods = [None] * 6
    d_mods[5] = by_segment(d_state_f * branch_f)
    d_mods[3] = by_segment(d_normed_f)
    d_mods[4] = by_segment(d_normed_f * hat_f)

    d_branch_c = bf(d_state_c)
    d_cross = bf(mm(d_branch_c, w_o1))
    conv_sent = place.swap(conv_grad, 1)
    d_xq_b, d_keys, d_values, conv_sent = tick(
        tuple(cross_backward(xq, keys, values, d_cross, token_seg, text_segment[None, :]))
        + (conv_sent,),
        ffn_flows,
    )
    conv_grad = conv_grad + conv_sent
    half_txt = TXT // 2
    d_kv = jnp.stack([d_keys, d_values])
    d_kv = d_kv[:, :half_txt] + place.swap(d_kv[:, half_txt:], 1)
    d_kv_b = bf(d_kv)
    early = unit_flow(
        [state_b, d_xq_b, d_branch_c, cross_b, text_b, d_kv_b[0], d_kv_b[1]],
        ((0, 1), (2, 3), (4, 5), (4, 6)),
        "yx",
    )
    d_state_a = d_state_c + mm_nt(d_xq_b, w_xq)
    d_state_a = settle(d_state_a, [early])

    d_text = mm_nt(d_kv_b[0], w_xk) + mm_nt(d_kv_b[1], w_xv)
    d_gain = jnp.sum(d_text * text_hat, axis=0)
    d_hat = d_text * gain
    d_text_raw = text_inv * (d_hat - text_hat * jnp.mean(d_hat * text_hat, -1, keepdims=True))
    d_text_raw_b = bf(d_text_raw)
    g_cap2 = mm_tn(cap_act_b, d_text_raw_b)
    d_cap_b = bf(gelu_pull(mm_nt(d_text_raw_b, w_cap2))[0])
    conv_sent = place.swap(conv_grad, 2)
    d_cap_b, conv_sent, d_state_a = tick((d_cap_b, conv_sent, d_state_a), ffn_flows)
    conv_grad = conv_grad + conv_sent
    g_cap1 = mm_tn(caption, d_cap_b)
    g_cap = jnp.concatenate(
        [g_cap1, g_cap2, jnp.zeros((place.n * cap_chunk - CAP_ROWS, D), F32)], axis=0
    ).reshape(split_dp + (2, 2, cap_chunk, D))
    b = place.dp_bits
    cap_flow = Flow(
        place,
        bf(lax.dynamic_slice_in_dim(g_cap, 1 - c, 1, b + 1)),
        [("abs", b - 1, place.x_mask), ("abs", b, 2)] + [("abs",) + pair_ for pair_ in far],
    )
    cap_flow.keep = lax.dynamic_slice_in_dim(g_cap, c, 1, b + 1)
    d_state_a = settle(d_state_a, [cap_flow])

    d_branch_a = bf(mods[2] * d_state_a)
    d_mods[2] = by_segment(d_state_a * branch_a)
    d_attn = mm(d_branch_a, w_o0)
    conv_sent = place.swap(conv_grad, place.x_mask)
    dq_b, d_state, d_sum, conv_sent = tick(
        tuple(group_call(
            attend_back_kernel,
            ins=("tok", "tok", "seg", "kv", "ks"),
            outs=("tok", "kv", "ks"),
            out_types=(BF16, F32, F32),
        )(q, d_attn, second_wide, state, key_sum)) + (conv_sent,),
        ffn_flows + [early],
    )
    conv_grad = conv_grad + conv_sent
    d_state, d_sum = shared(d_state, d_sum)
    dk_b, dv_b = group_call(
        state_back_kernel,
        ins=("tok", "tok", "seg", "kv", "ks"),
        outs=("tok", "tok"),
        out_types=(BF16, BF16),
    )(k, v, second_wide, d_state, d_sum)
    dk_b, dv_b = tick((dk_b, dv_b), flow_up)
    late = unit_flow(
        [normed_a, dq_b, dk_b, dv_b, d_branch_a, attn_b],
        ((0, 1), (0, 2), (0, 3), (4, 5)),
        "xy",
    )
    dq_b, dk_b, dv_b = settle((dq_b, dk_b, dv_b), [late])
    dq_b, dk_b, dv_b = tick((dq_b, dk_b, dv_b), [early, cap_flow])
    d_normed_a = mm_nt(dq_b, w_q) + mm_nt(dk_b, w_k) + mm_nt(dv_b, w_v)
    d_mods[0] = by_segment(d_normed_a)
    d_mods[1] = by_segment(d_normed_a * hat_a)
    d_embed = d_state_a + layer_norm_back(d_normed_a * (1.0 + mods[1]), hat_a, inv_a)
    g_patch = mm_tn(mixed_in, d_embed, HIGH)
    d_rows_six = jnp.stack([total for _, total in d_mods])
    tables_grad = jnp.concatenate(
        [d_rows_six, d_shift_o[None], d_scale_o[None], d_gain[None], g_patch, d_out_rows], axis=0
    )
    for b in range(place.dp_bits + 2):
        tables_grad = tables_grad + place.swap(tables_grad, 1 << b)
        if (1 << b) > place.x_mask:
            conv_grad = conv_grad + place.swap(conv_grad, 1 << b)

    d_mod = jnp.stack([table for table, _ in d_mods], axis=1).reshape(4, 6 * D)
    d_mod = jnp.pad(d_mod, ((0, 0), (BLOCK_AT, 0)))
    d_mod = d_mod.reshape(4, place.n, owner_rows).transpose(1, 0, 2)
    d_mod = lax.all_to_all(d_mod, AXES, 0, 0)
    d_mod = d_mod.reshape(slots // 4, 2, 4, owner_rows).sum(1).reshape(slots, owner_rows)
    g_block = mm_tn(d_mod, wide(silu_b), HIGH)
    d_silu = mm(d_mod, wide(cond_b), HIGH)
    d_silu = d_silu.reshape(split_dp + (2, 4, D))
    for axis, mask in [(place.dp_bits, 2), (place.dp_bits - 1, place.x_mask)] + far:
        bit = place.bit(mask)
        away = lax.dynamic_slice_in_dim(d_silu, 1 - bit, 1, axis)
        d_silu = lax.dynamic_slice_in_dim(d_silu, bit, 1, axis) + place.swap(away, mask)
    d_silu = d_silu.reshape(4, D)
    pair_sum = jnp.stack([d_silu, d_emb_mine])
    d_silu, d_emb = pair_sum + place.swap(pair_sum, 1)
    d_time = d_silu * silu_grad(emb_mine) + d_emb
    d_hidden = mm_nt(d_time, wide(w_time[FREQ:]), HIGH)
    hidden_mine = lax.dynamic_slice_in_dim(time_hidden, canvas * 4, 4, 0)
    d_times = jnp.stack([d_time, d_hidden * silu_grad(hidden_mine)])
    for mask in [2] + [n_mp << b for b in range(place.dp_bits)]:
        d_times = ordered(place.bit(mask), d_times, place.swap(d_times, mask), 1)
    g_time2 = mm_tn(wide(hidden_b), d_times[0], HIGH)
    g_time1 = mm_tn(wide(freq_b), d_times[1], HIGH)
    spots = -(-TIME_ROWS // owner_rows)
    g_time = jnp.concatenate(
        [g_time1, g_time2, jnp.zeros(((spots + 1) * owner_rows - TIME_ROWS, D), F32)], axis=0
    )
    g_time = lax.dynamic_slice_in_dim(
        g_time, jnp.minimum(place.me, spots) * owner_rows, owner_rows, 0
    )

    ff_own = [flow.drain().reshape(dl, FFB)[:, : FF // 4] for flow in ffn_flows]
    early_own = early.drain().reshape(dl, D)
    g_cap = collect_rows(
        place, cap_flow.drain().reshape(cap_chunk, D), owner_rows, TIME_ROWS, CAP_ROWS
    )
    g_cond = g_cap + g_block + g_time
    mine = jnp.stack([late.drain().reshape(dl, D), early_own])
    owned_sq = sum(jnp.sum(grad * grad) for grad in [mine, g_cond] + ff_own)
    g_in, g_out = from_units(unit_join(place, mine))
    g_upper = jnp.stack(ff_own[1:], axis=1)
    g_lower = ff_own[0].T
    owned = (g_in, g_out, g_upper, g_lower, g_cond)

    sums = jnp.stack([owned_sq, loss]).reshape(1, 2)
    for b in range(place.dp_bits + 2):
        sums = sums + place.swap(sums, 1 << b)
    squares, loss = sums[0, 0], sums[0, 1]
    norm = jnp.sqrt(squares + jnp.sum(conv_grad * conv_grad) + jnp.sum(tables_grad * tables_grad))
    factor = CLIP / jnp.maximum(norm, CLIP)
    rate = STEP_SCALE * math.sqrt(PARAMS) / CLIP
    grads = owned + (conv_grad, tables_grad)
    weights = (in_proj, out_proj, w_up, w_down, cond, conv, tables)
    moments = (mom_in, mom_out, mom_up, mom_down, mom_cond, mom_conv, mom_tables)
    averages = (avg_in, avg_out, avg_up, avg_down, avg_cond, avg_conv, avg_tables)
    new = [
        update(weights[i], grads[i], moments[i], averages[i], factor, rate) for i in range(7)
    ]
    moments_out = [new[i][1] for i in range(5)] + [factor * conv_grad, new[6][1]]
    return (loss, norm, *[n[0] for n in new], *moments_out, *[n[2] for n in new])


def solution(mesh):
    tokens = P("dp", "mp", None)
    weights = (
        P("dp", None, "mp"),
        P(None, "mp", "dp"),
        P("dp", None, "mp"),
        P("mp", "dp"),
        P(("dp", "mp"), None),
        P(),
        P(),
    )
    in_specs = (tokens, tokens, tokens, P("dp"), P("dp", None), P("dp", None)) + weights * 3
    out_specs = (P(), P()) + weights * 3
    body = partial(local, mesh.shape["dp"], mesh.shape["mp"])
    return jax.shard_map(body, mesh=mesh, in_specs=in_specs, out_specs=out_specs, check_vma=False)
```

```python
from functools import partial
import math

import jax
import jax.numpy as jnp
from jax import lax
from jax.experimental import pallas as pl
from jax.experimental.pallas import tpu as pltpu
from jax.sharding import PartitionSpec as P

D = 1152
FF = 2880
CAPD = 2304
CIN = 32
FREQ = 256
SIDE = 32
TXT = 512
HEAD = 32
XHEAD = 72
XHEADS = 16
PARAMS = 34277760
FFB = 768
FFP = 4 * FFB
TIME_ROWS = FREQ + D
CAP_ROWS = CAPD + D
BLOCK_AT = TIME_ROWS + CAP_ROWS

HIGH = lax.Precision.HIGHEST
EPS = 1e-06
CLIP = 0.001
MOMENTUM = 0.9
AVERAGE_RATE = 0.1
STEP_SCALE = 0.01
TMAX = 1000.0
MASKED = -1e30
AXES = ("dp", "mp")
F32 = jnp.float32
BF16 = jnp.bfloat16


def bf(value):
    return value.astype(BF16)


def wide(value):
    return value.astype(F32)


def dot(left, right, dims, precision=None):
    return lax.dot_general(
        left, right, (dims, ((), ())), precision=precision, preferred_element_type=F32
    )


def mm(left, right, precision=None):
    return dot(left, right, ((1,), (0,)), precision)


def mm_nt(left, right, precision=None):
    return dot(left, right, ((1,), (1,)), precision)


def mm_tn(left, right, precision=None):
    return dot(left, right, ((0,), (0,)), precision)


class Place:
    def __init__(self, n_dp, n_mp):
        self.n_dp, self.n_mp, self.n = n_dp, n_mp, n_dp * n_mp
        self.dp, self.mp = lax.axis_index("dp"), lax.axis_index("mp")
        self.me = self.dp * n_mp + self.mp
        self.y, self.c = self.mp // 2, self.mp % 2
        self.dp_bits = int(math.log2(n_dp))

    def bit(self, mask):
        return (self.me // mask) % 2

    def swap(self, value, mask):
        return lax.ppermute(value, AXES, [(i, i ^ mask) for i in range(self.n)])

    @property
    def far_masks(self):
        return [self.n_mp << b for b in range(1, self.dp_bits)]

    @property
    def x_mask(self):
        return self.n_mp


def ordered(bit, mine, theirs, axis):
    low = jnp.where(bit == 0, mine, theirs)
    high = jnp.where(bit == 0, theirs, mine)
    return jnp.concatenate([low, high], axis=axis)


def gather_far(place, block, axis):
    block = jnp.expand_dims(block, axis)
    for mask in place.far_masks:
        block = ordered(place.bit(mask), block, place.swap(block, mask), axis)
    return block


def gather_near(place, block, order):
    held = {0: block}
    for mask in order:
        held.update({key | mask: place.swap(value, mask) for key, value in held.items()})
    return held


def near_bits(place, key):
    flip = [1 if key & mask else 0 for mask in (place.x_mask, 2, 1)]
    own = (place.bit(place.x_mask), place.y, place.c)
    return [jnp.where(f == 1, 1 - o, o) for f, o in zip(flip, own)]


def gather_rows_all(place, block, order):
    rows, cols = block.shape
    held = gather_near(place, gather_far(place, block, 0), order)
    half = place.n_dp // 2
    out = jnp.zeros((half, 2, 2, 2, rows, cols), block.dtype)
    for key, value in held.items():
        x, y, c = near_bits(place, key)
        out = lax.dynamic_update_slice(out, value[:, None, None, None], (0, x, y, c, 0, 0))
    return out.reshape(place.n * rows, cols)


def spread_table(place, owner_rows, low, chunk):
    rounds = -(-owner_rows // chunk) + 1
    tables = []
    for step in range(rounds):
        pairs = []
        for owner in range(place.n):
            target = (owner_rows * owner - low) // chunk + step
            start = low + chunk * target - owner_rows * owner
            if 0 <= target < place.n and -chunk < start < owner_rows:
                pairs.append((owner, target))
        tables.append(pairs)
    return tables


def chunk_of(place, rows):
    chunk = -(-rows // place.n)
    unit = 128 if chunk > 64 else 8
    return -(-chunk // unit) * unit


def spread_rows(place, held, low, rows):
    owner_rows = held.shape[0]
    chunk = chunk_of(place, rows)
    padded = jnp.pad(held, ((chunk, chunk), (0, 0)))
    first = (owner_rows * place.me - low) // chunk
    total = None
    for step, pairs in enumerate(spread_table(place, owner_rows, low, chunk)):
        start = low + chunk * (first + step) - owner_rows * place.me + chunk
        piece = lax.dynamic_slice_in_dim(padded, start, chunk, 0)
        got = lax.ppermute(piece, AXES, pairs)
        total = got if total is None else total + got
    return total


def collect_rows(place, block, owner_rows, low, rows):
    chunk = block.shape[0]
    first = (owner_rows * place.me - low) // chunk
    got = [
        wide(lax.ppermute(bf(block), AXES, [(target, owner) for owner, target in pairs]))
        for pairs in spread_table(place, owner_rows, low, chunk)
    ]
    start = owner_rows * place.me - low - chunk * first
    mine = lax.dynamic_slice_in_dim(jnp.concatenate(got, axis=0), start, owner_rows, 0)
    row = owner_rows * place.me + jnp.arange(owner_rows, dtype=jnp.int32)[:, None]
    return jnp.where((row >= low) & (row < low + rows), mine, 0.0)


def halve(place, grad, stages):
    for axis, mask in stages:
        bit = place.bit(mask)
        half = grad.shape[axis] // 2
        away = lax.dynamic_slice_in_dim(grad, (1 - bit) * half, half, axis)
        keep = lax.dynamic_slice_in_dim(grad, bit * half, half, axis)
        grad = keep + wide(place.swap(bf(away), mask))
    return grad


def layer_norm(value):
    centred = value - jnp.mean(value, -1, keepdims=True)
    inverse = lax.rsqrt(jnp.mean(centred * centred, -1, keepdims=True) + EPS)
    return centred * inverse, inverse


def layer_norm_back(grad, normed, inverse):
    along = jnp.mean(grad * normed, -1, keepdims=True)
    return inverse * (grad - jnp.mean(grad, -1, keepdims=True) - normed * along)


def silu_grad(value):
    gate = jax.nn.sigmoid(value)
    return gate * (1.0 + value * (1.0 - gate))


def time_embed(steps_t):
    half_size = FREQ // 2
    freqs = jnp.exp(-math.log(10000.0) * jnp.arange(half_size, dtype=F32) / half_size)
    angles = wide(steps_t)[:, None] * freqs[None, :]
    return jnp.concatenate([jnp.cos(angles), jnp.sin(angles)], axis=1)


def to_ff(value):
    blocks = value.reshape(value.shape[:-1] + (4, FF // 4))
    pad = [(0, 0)] * (blocks.ndim - 1) + [(0, FFB - FF // 4)]
    blocks = jnp.pad(blocks, pad)
    blocks = jnp.stack([blocks[..., m, :] for m in (0, 2, 1, 3)], axis=-2)
    return blocks.reshape(value.shape[:-1] + (FFP,))


def from_ff(value):
    blocks = value.reshape(value.shape[:-1] + (4, FFB))[..., : FF // 4]
    blocks = jnp.stack([blocks[..., m, :] for m in (0, 2, 1, 3)], axis=-2)
    return blocks.reshape(value.shape[:-1] + (FF,))


def unit_split(place, units):
    units = units.reshape((2, 4) + units.shape[1:])

    def part(number):
        return lax.dynamic_index_in_dim(units, number, 1, False)

    got = [part(place.mp)] + [place.swap(part(place.mp ^ m), m) for m in (1, 2, 3)]
    stacked = jnp.stack(got)
    return jnp.concatenate(
        [lax.dynamic_index_in_dim(stacked, place.mp ^ m, 0, False) for m in range(4)], axis=-1
    )


def unit_join(place, block):
    cols = D // 4

    def part(number):
        return lax.dynamic_slice_in_dim(block, number * cols, cols, 2)

    got = [part(place.mp)] + [place.swap(part(place.mp ^ m), m) for m in (1, 2, 3)]
    stacked = jnp.stack(got)
    order = [lax.dynamic_index_in_dim(stacked, place.mp ^ m, 0, False) for m in range(4)]
    return jnp.stack(order, axis=1).reshape((8,) + order[0].shape[1:])


def as_units(in_w, out_w):
    inp = [in_w[:, k] for k in range(6)]
    outp = [out_w[j].T for j in range(2)]
    return jnp.stack([inp[0], inp[1], inp[2], outp[0], inp[3], outp[1], inp[4], inp[5]])


def from_units(units):
    g_in = jnp.stack([units[u] for u in (0, 1, 2, 4, 6, 7)], axis=1)
    g_out = jnp.stack([units[3].T, units[5].T])
    return g_in, g_out


class Flow:
    def __init__(self, place, sends, stages):
        self.place, self.stages = place, list(stages)
        self.keep = None
        self.moving = place.swap(sends, 1)
        self.sends = None

    def launch(self):
        self.moving = self.place.swap(self.sends, self.mask)
        self.sends = None

    def part(self, take):
        return take(self.keep) + wide(take(self.moving))

    def land(self):
        if not self.stages:
            self.keep = self.part(lambda value: value)
            self.moving = None
            return
        kind, axis, self.mask = self.stages.pop(0)
        if kind == "rel":
            away = self.part(lambda value: lax.slice_in_dim(value, 1, 2, axis=axis))
            keep = self.part(lambda value: lax.slice_in_dim(value, 0, 1, axis=axis))
        else:
            bit = self.place.bit(self.mask)
            away = self.part(lambda value: lax.dynamic_slice_in_dim(value, 1 - bit, 1, axis))
            keep = self.part(lambda value: lax.dynamic_slice_in_dim(value, bit, 1, axis))
        self.sends, self.keep, self.moving = bf(away), keep, None

    def split(self, axis, orders):
        flows = []
        for i, order in enumerate(orders):
            flow = Flow.__new__(Flow)
            flow.place, flow.stages, flow.sends = self.place, list(order), None
            flow.keep = lax.slice_in_dim(self.keep, i, i + 1, axis=axis)
            flow.moving = lax.slice_in_dim(self.moving, i, i + 1, axis=axis)
            flows.append(flow)
        return flows

    def drain(self):
        while self.moving is not None:
            self.land()
            if self.sends is not None:
                self.launch()
        return self.keep


def tick(value, flows):
    moving = [flow for flow in flows if flow.moving is not None]
    value, landed = lax.optimization_barrier((value, [flow.moving for flow in moving]))
    for flow, arrived in zip(moving, landed):
        flow.moving = arrived
        flow.land()
    ready = [flow for flow in moving if flow.sends is not None]
    value, sends = lax.optimization_barrier((value, [flow.sends for flow in ready]))
    for flow, out in zip(ready, sends):
        flow.sends = out
        flow.launch()
    return value


CB = 256
ROW = SIDE
LIMIT = 48 * 1024 * 1024
QUICK = pl.CostEstimate(flops=2**20, bytes_accessed=2**16, transcendentals=0)


def whole_spec(shape):
    return pl.BlockSpec(shape, lambda *_: (0,) * len(shape))


def ffn_forward_kernel(
    x_ref, w0_ref, w1_ref, wd_ref, taps_ref, left_ref, right_ref, on_ref,
    u_ref, z_ref, g_ref, out_ref, act, act_l, act_r
):
    rows = g_ref.shape[0] // ROW
    zero = jnp.zeros((ROW, CB), F32)
    x = x_ref[...]
    u_ref[0] = mm(x, w0_ref[...].reshape(D, CB))
    u_ref[1] = mm(x, w1_ref[...].reshape(D, CB))
    on = on_ref[0, 0]
    for k in range(2):
        for ref in (act, act_l, act_r):
            ref[k, pl.ds(0, ROW)] = zero

    def fill(r, scale):
        for k in range(2):
            u = u_ref[k, pl.ds(pl.multiple_of(r * ROW, ROW), ROW)]
            a = u * jax.nn.sigmoid(u) * scale
            at = pl.ds(pl.multiple_of(r * ROW + ROW, ROW), ROW)
            act[k, at] = a
            act_l[k, at] = pltpu.roll(a, 1, 0) * left_ref[...]
            act_r[k, at] = pltpu.roll(a, ROW - 1, 0) * right_ref[...]

    @pl.loop(0, rows)
    def _(r):
        fill(r, 1.0)

    fill(rows, on)

    @pl.loop(0, rows)
    def _(r):
        z = []
        for k in range(2):
            total = jnp.broadcast_to(taps_ref[k, pl.ds(9, 1)], (ROW, CB))
            for dr in range(3):
                at = pl.ds(pl.multiple_of(r * ROW + dr * ROW, ROW), ROW)
                for dc, ref in enumerate((act_l, act, act_r)):
                    total = total + ref[k, at] * taps_ref[k, pl.ds(dr * 3 + dc, 1)]
            z_ref[k, pl.ds(pl.multiple_of(r * ROW, ROW), ROW)] = total
            z.append(total)
        gated = z[0] * (z[1] * jax.nn.sigmoid(z[1]))
        g_ref[pl.ds(pl.multiple_of(r * ROW, ROW), ROW)] = bf(gated)

    part = mm_nt(g_ref[...], wd_ref[...].reshape(D, CB))

    @pl.when(pl.program_id(0) == 0)
    def _():
        out_ref[...] = part

    @pl.when(pl.program_id(0) > 0)
    def _():
        out_ref[...] += part


def ff_spec(ffw, k):
    groups, blocks, rows, lanes = ffw.shape
    per = lanes // CB

    def index(j):
        at = j // per
        return (0, at % 2 * 2 + at // 2 if blocks == 4 else 0, k, j % per)

    return pl.BlockSpec((groups, 1, rows // 3, CB), index)


def ffn_forward(x_ext, ffw, taps, left_ok, right_ok, on):
    n_ext = x_ext.shape[0]
    n_tok = n_ext - ROW
    weight = partial(ff_spec, ffw)
    pads = pltpu.VMEM((2, n_ext + ROW, CB), F32)
    return pl.pallas_call(
        ffn_forward_kernel,
        grid=(FFP // CB,),
        in_specs=[
            whole_spec((n_ext, D)), weight(0), weight(1), weight(2),
            pl.BlockSpec((2, 10, CB), lambda j: (0, 0, j)),
            whole_spec((ROW, CB)), whole_spec((ROW, CB)),
            pl.BlockSpec((1, 1), lambda j: (0, 0), memory_space=pltpu.SMEM),
        ],
        out_specs=[
            pl.BlockSpec((2, n_ext, CB), lambda j: (0, 0, j)),
            pl.BlockSpec((2, n_tok, CB), lambda j: (0, 0, j)),
            pl.BlockSpec((n_tok, CB), lambda j: (0, j)),
            whole_spec((n_tok, D)),
        ],
        out_shape=[
            jax.ShapeDtypeStruct((2, n_ext, FFP), F32),
            jax.ShapeDtypeStruct((2, n_tok, FFP), F32),
            jax.ShapeDtypeStruct((n_tok, FFP), BF16),
            jax.ShapeDtypeStruct((n_tok, D), F32),
        ],
        scratch_shapes=[pads, pads, pads],
        compiler_params=pltpu.CompilerParams(
            dimension_semantics=("arbitrary",), vmem_limit_bytes=LIMIT
        ),
        cost_estimate=QUICK,
    )(x_ext, ffw, ffw, ffw, taps, left_ok, right_ok, on)


def ffn_backward_kernel(
    d_ref, wd_ref, w0_ref, w1_ref, u_ref, z_ref, zh_ref, taps_ref, left_ref, right_ref, on_ref,
    du_ref, dt_ref, dn_ref, dg_buf, dz, dz_l, dz_r, acc
):
    n_tok = z_ref.shape[1]
    rows = n_tok // ROW
    zero = jnp.zeros((ROW, CB), F32)
    dg_buf[...] = mm(d_ref[...], wd_ref[...].reshape(D, CB))
    for k in range(2):
        for ref in (dz, dz_l, dz_r):
            ref[k, pl.ds(0, ROW)] = zero
    acc[...] = jnp.zeros_like(acc)

    def fill(r, z0, z1, scale, count):
        dg = dg_buf[pl.ds(pl.multiple_of(r * ROW, ROW), ROW)]
        gate = jax.nn.sigmoid(z1)
        soft = z1 * gate
        at = pl.ds(pl.multiple_of(r * ROW + ROW, ROW), ROW)
        d_both = (dg * soft, dg * z0 * (gate + soft * (1.0 - gate)))
        for k in range(2):
            value = d_both[k] * scale
            dz[k, at] = value
            dz_l[k, at] = pltpu.roll(value * left_ref[...], ROW - 1, 0)
            dz_r[k, at] = pltpu.roll(value * right_ref[...], 1, 0)
            if count:
                acc[k, 9] += fold(value)

    def fold(value):
        return value[0:8] + value[8:16] + value[16:24] + value[24:32]

    @pl.loop(0, rows)
    def _(r):
        at = pl.ds(pl.multiple_of(r * ROW, ROW), ROW)
        fill(r, z_ref[0, at], z_ref[1, at], 1.0, True)

    fill(rows, zh_ref[0], zh_ref[1], on_ref[0, 0], False)

    def back(r, taps_on):
        at = pl.ds(pl.multiple_of(r * ROW, ROW), ROW)
        for k in range(2):
            u = u_ref[k, at]
            gate = jax.nn.sigmoid(u)
            a = u * gate
            total = zero
            for dr in range(3):
                near = pl.ds(pl.multiple_of(r * ROW + (2 - dr) * ROW, ROW), ROW)
                for dc, ref in enumerate((dz_l, dz, dz_r)):
                    value = ref[k, near]
                    total = total + value * taps_ref[k, pl.ds(dr * 3 + dc, 1)]
                    if dr in taps_on:
                        acc[k, dr * 3 + dc] += fold(value * a)
            du_ref[k, at] = bf(total * (gate + a * (1.0 - gate)))

    @pl.loop(0, rows - 1)
    def _(r):
        back(r, (0, 1, 2))

    back(rows - 1, (1, 2))
    for k in range(2):
        u = u_ref[k, pl.ds(n_tok, ROW)]
        a = u * jax.nn.sigmoid(u) * on_ref[0, 0]
        for dc, ref in enumerate((dz_l, dz, dz_r)):
            acc[k, 6 + dc] += fold(ref[k, pl.ds(n_tok, ROW)] * a)
        for t in range(10):
            dt_ref[k, pl.ds(t, 1)] = jnp.sum(acc[k, t], axis=0, keepdims=True)

    part = mm_nt(du_ref[0], w0_ref[...].reshape(D, CB))
    part = part + mm_nt(du_ref[1], w1_ref[...].reshape(D, CB))

    @pl.when(pl.program_id(0) == 0)
    def _():
        dn_ref[...] = part

    @pl.when(pl.program_id(0) > 0)
    def _():
        dn_ref[...] += part


def ffn_backward(d_ext, ffw, upper, z, z_halo, taps, left_ok, right_ok, on):
    n_ext = d_ext.shape[0]
    n_tok = n_ext - ROW
    pads = pltpu.VMEM((2, n_ext + ROW, CB), F32)
    return pl.pallas_call(
        ffn_backward_kernel,
        grid=(FFP // CB,),
        in_specs=[
            whole_spec((n_ext, D)),
            ff_spec(ffw, 2), ff_spec(ffw, 0), ff_spec(ffw, 1),
            pl.BlockSpec((2, n_ext, CB), lambda j: (0, 0, j)),
            pl.BlockSpec((2, n_tok, CB), lambda j: (0, 0, j)),
            pl.BlockSpec((2, ROW, CB), lambda j: (0, 0, j)),
            pl.BlockSpec((2, 10, CB), lambda j: (0, 0, j)),
            whole_spec((ROW, CB)), whole_spec((ROW, CB)),
            pl.BlockSpec((1, 1), lambda j: (0, 0), memory_space=pltpu.SMEM),
        ],
        out_specs=[
            pl.BlockSpec((2, n_tok, CB), lambda j: (0, 0, j)),
            pl.BlockSpec((2, 10, CB), lambda j: (0, 0, j)),
            whole_spec((n_tok, D)),
        ],
        out_shape=[
            jax.ShapeDtypeStruct((2, n_tok, FFP), BF16),
            jax.ShapeDtypeStruct((2, 10, FFP), F32),
            jax.ShapeDtypeStruct((n_tok, D), F32),
        ],
        scratch_shapes=[
            pltpu.VMEM((n_ext, CB), F32), pads, pads, pads, pltpu.VMEM((2, 10, 8, CB), F32)
        ],
        compiler_params=pltpu.CompilerParams(
            dimension_semantics=("arbitrary",), vmem_limit_bytes=LIMIT
        ),
        cost_estimate=QUICK,
    )(d_ext, ffw, ffw, ffw, upper, z, z_halo, taps, left_ok, right_ok, on)


def ff_grad_kernel(spot_ref, left_ref, right_ref, out_ref):
    out_ref[0, 0] = mm_tn(left_ref[...], right_ref[0]).astype(out_ref.dtype)


def ff_grad(spot, left, right, which, away, dtype):
    n_tok = left.shape[0]
    count = 1

    def lanes(k, r, spot_ref):
        return (which, 0, (spot_ref[1] + away) % 2 * 2 + (spot_ref[0] + r) % 2)

    return pl.pallas_call(
        ff_grad_kernel,
        grid_spec=pltpu.PrefetchScalarGridSpec(
            num_scalar_prefetch=1,
            grid=(count, 2),
            in_specs=[
                pl.BlockSpec((n_tok, D), lambda k, r, spot_ref: (0, 0)),
                pl.BlockSpec((1, n_tok, FFB), lanes),
            ],
            out_specs=pl.BlockSpec((1, 1, D, FFB), lambda k, r, spot_ref: (k, r, 0, 0)),
        ),
        out_shape=jax.ShapeDtypeStruct((count, 2, D, FFB), dtype),
        compiler_params=pltpu.CompilerParams(
            dimension_semantics=("arbitrary", "arbitrary"), vmem_limit_bytes=LIMIT
        ),
        cost_estimate=QUICK,
    )(spot, left, right)


def unit_grad_kernel(pairs, away, spot_ref, *refs):
    out_ref = refs[-1]
    unit = (spot_ref[0] + pl.program_id(0)) % 2 * 2 + (spot_ref[1] + away) % 2
    step = D // 3
    for number, (left, right) in enumerate(pairs):

        @pl.when(unit == number)
        def _():
            for i in range(3):
                rows = pl.ds(i * step, step)
                value = mm_tn(refs[left][:, rows], refs[right][...])
                out_ref[0, rows] = value.astype(out_ref.dtype)


def unit_grad(spot, arrays, pairs, away, dtype):
    n_tok = arrays[0].shape[0]
    return pl.pallas_call(
        partial(unit_grad_kernel, pairs, away),
        grid_spec=pltpu.PrefetchScalarGridSpec(
            num_scalar_prefetch=1,
            grid=(2,),
            in_specs=[pl.BlockSpec(a.shape, lambda r, spot_ref: (0, 0)) for a in arrays],
            out_specs=pl.BlockSpec((1, D, D), lambda r, spot_ref: (r, 0, 0)),
        ),
        out_shape=jax.ShapeDtypeStruct((2, D, D), dtype),
        compiler_params=pltpu.CompilerParams(
            dimension_semantics=("arbitrary",), vmem_limit_bytes=LIMIT
        ),
        cost_estimate=QUICK,
    )(spot, *arrays)


class Course:
    def __init__(self, flow):
        shape = flow.keep.shape
        self.block = shape[-2:]
        self.count = math.prod(shape[:-2])
        self.sends = flow.sends.reshape((self.count,) + self.block)
        self.keep = flow.keep.reshape((self.count,) + self.block)
        self.first = flow.mask
        self.stages = [
            (kind, math.prod(shape[axis + 1 : -2]), mask) for kind, axis, mask in flow.stages
        ]

    def sizes(self):
        return [self.count >> i for i in range(len(self.stages) + 1)]


def finish_kernel(n_mp, courses, top, sum_masks, gather_masks, *refs):
    count = len(courses)
    dp, mp = lax.axis_index("dp"), lax.axis_index("mp")

    def bit(mask):
        return mp // mask % 2 if mask < n_mp else dp // (mask // n_mp) % 2

    def partner(mask):
        if mask < n_mp:
            return {"mp": mp + mask * (1 - 2 * bit(mask))}
        return {"dp": dp + mask // n_mp * (1 - 2 * bit(mask))}

    sends, keeps = refs[:count], refs[count : 2 * count]
    part_ref, mine_ref, scalar_ref = refs[2 * count : 2 * count + 3]
    join_ref, cap_ref, sum_ref, all_ref, total_ref = refs[2 * count + 3 : 2 * count + 8]
    scratch = list(refs[2 * count + 8 :])
    (
        send_sem, recv_sem, sum_send, sum_recv, all_send, all_recv, one_send, one_recv,
        join_send, join_recv
    ) = scratch[-10:]
    sum_got, sum_buf, owns, cap_owns, one_got, one_buf, join_buf = scratch[-17:-10]
    merges = [
        (owns, owns.at[3], scratch[-21], scratch[-20]),
        (cap_owns, cap_ref, scratch[-19], scratch[-18]),
    ]
    outs = [owns.at[0], owns.at[1], cap_owns.at[0], cap_owns.at[1], owns.at[2]]
    accs, gots, packs = [], [], []
    for course in courses:
        accs.append(scratch.pop(0))
        gots.append([scratch.pop(0) for _ in course.sizes()])
        packs.append([None] + [scratch.pop(0) for _ in course.sizes()[1:]])

    def across():
        return {"mp": mp + 1 - 2 * bit(1) + 2 * (1 - 2 * bit(2))}

    barrier = pltpu.get_barrier_semaphore()
    for target in [partner(mask) for mask in sum_masks] + [across()]:
        pl.semaphore_signal(
            barrier, inc=1, device_id=target, device_id_type=pl.DeviceIdType.MESH
        )
    pl.semaphore_wait(barrier, len(sum_masks) + 1)

    def copy(f, stage):
        course = courses[f]
        mask = course.first if stage == 0 else course.stages[stage - 1][2]
        return pltpu.make_async_remote_copy(
            src_ref=sends[f] if stage == 0 else packs[f][stage],
            dst_ref=gots[f][stage],
            send_sem=send_sem.at[f, stage],
            recv_sem=recv_sem.at[f, stage],
            device_id=partner(mask),
            device_id_type=pl.DeviceIdType.MESH,
        )

    def each_rows(rows, act):
        if rows % 16:
            act(slice(None))
        else:

            @pl.loop(0, rows // 16)
            def _(i):
                act(pl.ds(pl.multiple_of(i * 16, 16), 16))

    def spots(strides, at):
        found = [(at, 0)]
        for stride in strides:
            found = [
                (block + value * stride, slot * 2 + value)
                for block, slot in found for value in (0, 1)
            ]
        return found

    def absorb(f, stage, fixed, strides):
        course = courses[f]
        base = keeps[f] if stage == 0 else accs[f]
        got = gots[f][stage]
        rows = course.block[0]
        if stage == len(course.stages):

            def close(at):
                outs[f][at, :] = base[fixed, at, :] + wide(got[0, at, :])

            each_rows(rows, close)
            return None
        kind, cut, mask = course.stages[stage]
        own = bit(mask) if kind == "abs" else 0
        other = 1 - own
        place_of = strides.index(cut)
        weight = 1 << (len(strides) - 1 - place_of)
        rest = [stride for stride in strides if stride != cut]

        for number, (block, slot) in enumerate(spots(rest, fixed)):
            low = slot % weight
            slot = (slot // weight) * 2 * weight + low

            def act(at, block=block, slot=slot, number=number):
                packs[f][stage + 1][number, at, :] = bf(
                    base[block + other * cut, at, :] + wide(got[slot + other * weight, at, :])
                )

            each_rows(rows, act)
        copy(f, stage + 1).start()
        for number, (block, slot) in enumerate(spots(rest, fixed)):
            low = slot % weight
            slot = (slot // weight) * 2 * weight + low

            def act(at, block=block, slot=slot):
                accs[f][block + own * cut, at, :] = (
                    base[block + own * cut, at, :] + wide(got[slot + own * weight, at, :])
                )

            each_rows(rows, act)
        return fixed + own * cut, rest

    def sum_copy(stage):
        return pltpu.make_async_remote_copy(
            src_ref=part_ref if stage == 0 else sum_buf.at[stage - 1],
            dst_ref=sum_got.at[stage],
            send_sem=sum_send.at[stage],
            recv_sem=sum_recv.at[stage],
            device_id=partner(sum_masks[stage]),
            device_id_type=pl.DeviceIdType.MESH,
        )

    def all_copy(stage):
        held = canvas // (1 << stage) * (1 << stage)
        return pltpu.make_async_remote_copy(
            src_ref=mine_ref if stage == 0 else all_ref.at[pl.ds(held, 1 << stage)],
            dst_ref=all_ref.at[pl.ds(held, 1 << stage)],
            send_sem=all_send.at[stage],
            recv_sem=all_recv.at[stage],
            device_id=partner(gather_masks[stage]),
            device_id_type=pl.DeviceIdType.MESH,
        )

    def merge_copy(pair):
        return pltpu.make_async_remote_copy(
            src_ref=merges[pair][2],
            dst_ref=merges[pair][3],
            send_sem=send_sem.at[2 * pair, merge_at[pair] + 1],
            recv_sem=recv_sem.at[2 * pair, merge_at[pair] + 1],
            device_id=partner(top),
            device_id_type=pl.DeviceIdType.MESH,
        )

    def one_copy(stage):
        return pltpu.make_async_remote_copy(
            src_ref=one_buf.at[stage],
            dst_ref=one_got.at[stage],
            send_sem=one_send.at[stage],
            recv_sem=one_recv.at[stage],
            device_id=partner(sum_masks[stage]),
            device_id_type=pl.DeviceIdType.MESH,
        )

    def join_copy(number):
        return pltpu.make_async_remote_copy(
            src_ref=join_buf.at[number],
            dst_ref=join_ref.at[mp],
            send_sem=join_send.at[number],
            recv_sem=join_recv.at[number],
            device_id=across() if number == 2 else partner(number + 1),
            device_id_type=pl.DeviceIdType.MESH,
        )

    def lanes_of(number):
        cols = D // 4

        def cut(ref):
            value = ref[:, :cols]
            for m in range(1, 4):
                value = jnp.where(number == m, ref[:, m * cols : (m + 1) * cols], value)
            return value

        return cut

    merge_at = [len(courses[0].stages), len(courses[2].stages)]
    canvas = dp * 2 + mp // 2
    sum_copy(0).start()
    all_copy(0).start()
    state = []
    turns = (0, 1, 4, 2, 3)
    lag = (0, 0, 1, 1, 0)
    for f, course in enumerate(courses):
        if not lag[f]:
            copy(f, 0).start()
        strides = [course.count >> (i + 1) for i in range(course.count.bit_length() - 1)]
        state.append((0, strides))
    all_ref[pl.ds(canvas, 1)] = mine_ref[...]
    high = bit(top) == 1
    for turn in range(max(len(sum_masks), *[len(course.stages) + 3 for course in courses])):
        for f in turns:
            stage = turn - lag[f]
            if stage == -1:
                copy(f, 0).start()
            elif stage <= len(courses[f].stages):
                copy(f, stage).wait_recv()
                state[f] = absorb(f, stage, *state[f])
            if f % 2 == 1 and stage == merge_at[f // 2]:
                both, _, pack, _ = merges[f // 2]
                pack[...] = bf(jnp.where(high, both[0], both[1]))
                merge_copy(f // 2).start()
        for pair, (both, own, pack, came) in enumerate(merges):
            if turn == merge_at[pair] + lag[2 * pair] + 1:
                merge_copy(pair).wait_recv()
                own[...] = jnp.where(high, both[1], both[0]) + wide(came[...])
        if turn < len(sum_masks):
            sum_copy(turn).wait_recv()
            total = (part_ref[...] if turn == 0 else sum_buf[turn - 1]) + sum_got[turn]
            if turn + 1 < len(sum_masks):
                sum_buf[turn] = total
                sum_copy(turn + 1).start()
            else:
                sum_ref[...] = total
        if turn < len(gather_masks):
            all_copy(turn).wait_recv()
            if turn + 1 < len(gather_masks):
                all_copy(turn + 1).start()
    square = jnp.sum(owns[2] * owns[2]) + jnp.sum(owns[3] * owns[3])
    square = square + jnp.sum(cap_ref[...] * cap_ref[...])
    row = lax.broadcasted_iota(jnp.int32, (8, 128), 0)
    one_buf[0] = scalar_ref[...] + jnp.where(row == 0, square, 0.0)
    one_copy(0).start()
    b0, b1 = bit(1), bit(2)
    for number, (f0, f1) in enumerate(((1, 0), (0, 1), (1, 1))):
        other = b0 + f0 * (1 - 2 * b0) + 2 * (b1 + f1 * (1 - 2 * b1))
        cut = lanes_of(other)
        join_buf[number, 0] = cut(owns.at[3])
        join_buf[number, 1] = cut(owns.at[2])
        join_copy(number).start()
    cut = lanes_of(mp)
    join_ref[mp, 0] = cut(owns.at[3])
    join_ref[mp, 1] = cut(owns.at[2])
    for stage in range(len(sum_masks)):
        one_copy(stage).wait_recv()
        total = one_buf[stage] + one_got[stage]
        if stage + 1 < len(sum_masks):
            one_buf[stage + 1] = total
            one_copy(stage + 1).start()
        else:
            total_ref[...] = total
    for number in range(3):
        join_copy(number).wait_recv()
        join_copy(number).wait_send()
    for stage in range(len(sum_masks)):
        one_copy(stage).wait_send()
        sum_copy(stage).wait_send()
    for stage in range(len(gather_masks)):
        all_copy(stage).wait_send()
    for pair in range(2):
        merge_copy(pair).wait_send()
    for f, course in enumerate(courses):
        for stage in range(len(course.stages) + 1):
            copy(f, stage).wait_send()


def finish(n_mp, flows, top, masks, part, mine, scalars):
    budget = 3000
    height = lambda flow: flow.keep.size // D // flow.keep.shape[-2] * (-(-flow.keep.shape[-2] // 16) * 16)
    while sum(height(flow) for flow in flows) > budget:
        flow = max(flows, key=height)
        flow.launch()
        flow.land()
    courses = [Course(flow) for flow in flows]
    canvases = 1 << len(masks) - 1
    scratch = []
    for course in courses:
        scratch.append(pltpu.VMEM((course.count,) + course.block, F32))
        scratch += [pltpu.VMEM((size,) + course.block, BF16) for size in course.sizes()]
        scratch += [pltpu.VMEM((size,) + course.block, BF16) for size in course.sizes()[1:]]
    most = max(len(course.stages) for course in courses) + 2
    late = courses[0].block
    for block in (late, courses[2].block):
        scratch += [pltpu.VMEM(block, BF16), pltpu.VMEM(block, BF16)]
    scratch += [
        pltpu.VMEM((len(masks),) + part.shape, F32),
        pltpu.VMEM((len(masks) - 1,) + part.shape, F32),
        pltpu.VMEM((4,) + late, F32),
        pltpu.VMEM((2,) + courses[2].block, F32),
        pltpu.VMEM((len(masks), 8, 128), F32),
        pltpu.VMEM((len(masks), 8, 128), F32),
        pltpu.VMEM((3, 2, late[0], D // 4), F32),
    ]
    scratch += [pltpu.SemaphoreType.DMA((len(courses), most))] * 2
    scratch += [pltpu.SemaphoreType.DMA((len(masks),))] * 6
    scratch += [pltpu.SemaphoreType.DMA((3,))] * 2
    plan = [
        Plan(course.count, course.block, course.first, tuple(course.stages)) for course in courses
    ]
    vmem = pl.BlockSpec(memory_space=pltpu.VMEM)
    outs = [(4, 2, late[0], D // 4), courses[2].block, part.shape]
    outs += [(canvases,) + mine.shape[1:], (8, 128)]
    return pl.pallas_call(
        partial(finish_kernel, n_mp, plan, top, masks, masks[1:]),
        in_specs=[pl.BlockSpec(memory_space=pl.ANY)] * len(courses) + [vmem] * (len(courses) + 3),
        out_specs=[vmem] * len(outs),
        out_shape=[jax.ShapeDtypeStruct(shape, F32) for shape in outs],
        scratch_shapes=scratch,
        compiler_params=pltpu.CompilerParams(
            collective_id=0, has_side_effects=True, vmem_limit_bytes=58 * 1024 * 1024
        ),
    )(*[course.sends for course in courses], *[course.keep for course in courses], part, mine, scalars)


class Plan:
    def __init__(self, count, block, first, stages):
        self.count, self.block, self.first, self.stages = count, block, first, stages

    def sizes(self):
        return [self.count >> i for i in range(len(self.stages) + 1)]


def cap_grad_kernel(away, spot_ref, cap_ref, act_ref, dcap_ref, draw_ref, out_ref):
    block = pl.program_id(0) * 2 + (spot_ref[1] + away) % 2
    first, both = cap_ref.shape[1] // GL, (cap_ref.shape[1] + act_ref.shape[1]) // GL

    @pl.when(block < first)
    def _():
        rows = pl.ds(pl.multiple_of(block * GL, GL), GL)
        out_ref[0] = mm_tn(cap_ref[:, rows], dcap_ref[...]).astype(out_ref.dtype)

    @pl.when((block >= first) & (block < both))
    def _():
        rows = pl.ds(pl.multiple_of((block - first) * GL, GL), GL)
        out_ref[0] = mm_tn(act_ref[:, rows], draw_ref[...]).astype(out_ref.dtype)

    @pl.when(block >= both)
    def _():
        out_ref[0] = jnp.zeros((GL, D), out_ref.dtype)


def cap_grad(spot, arrays, blocks, away, dtype):
    return pl.pallas_call(
        partial(cap_grad_kernel, away),
        grid_spec=pltpu.PrefetchScalarGridSpec(
            num_scalar_prefetch=1,
            grid=(blocks // 2,),
            in_specs=[pl.BlockSpec(a.shape, lambda j, spot_ref: (0, 0)) for a in arrays],
            out_specs=pl.BlockSpec((1, GL, D), lambda j, spot_ref: (j, 0, 0)),
        ),
        out_shape=jax.ShapeDtypeStruct((blocks // 2, GL, D), dtype),
        compiler_params=pltpu.CompilerParams(
            dimension_semantics=("arbitrary",), vmem_limit_bytes=LIMIT
        ),
        cost_estimate=QUICK,
    )(spot, *arrays)


WIN = 256
QROWS = 512
BROWS = 256


def head_window(h):
    start = jnp.minimum(h * XHEAD // 128 * 128, D - WIN)
    lane = lax.broadcasted_iota(jnp.int32, (1, WIN), 1)
    mask = (lane >= h * XHEAD - start) & (lane < h * XHEAD - start + XHEAD)
    return pl.ds(pl.multiple_of(start, 128), WIN), mask


def cross_probs(q, keys, token_seg, text_seg):
    scores = mm_nt(q, keys) * XHEAD ** (-0.5)
    scores = jnp.where(token_seg == text_seg, scores, MASKED)
    top = jnp.max(scores, axis=-1, keepdims=True)
    probs = jnp.exp(scores - top)
    return probs * (1.0 / jnp.sum(probs, axis=-1, keepdims=True))


def cross_forward_kernel(q_ref, k_ref, v_ref, tok_ref, txt_ref, out_ref):
    win, mask = head_window(pl.program_id(0))
    keys, values = k_ref[:, win], v_ref[:, win]

    @pl.loop(0, q_ref.shape[0] // QROWS)
    def _(i):
        at = pl.ds(pl.multiple_of(i * QROWS, QROWS), QROWS)
        q = jnp.where(mask, q_ref[at, win], jnp.zeros((), BF16))
        probs = bf(cross_probs(q, keys, tok_ref[at, 0:1], txt_ref[...]))
        out_ref[at, win] = jnp.where(mask, bf(mm(probs, values)), out_ref[at, win])


def cross_forward(q, keys, values, token_seg, text_seg):
    n_tok = q.shape[0]
    n_txt = keys.shape[0]
    return pl.pallas_call(
        cross_forward_kernel,
        grid=(XHEADS,),
        in_specs=[
            whole_spec((n_tok, D)), whole_spec((n_txt, D)), whole_spec((n_txt, D)),
            whole_spec((n_tok, 1)), whole_spec((1, n_txt)),
        ],
        out_specs=whole_spec((n_tok, D)),
        out_shape=jax.ShapeDtypeStruct((n_tok, D), BF16),
        compiler_params=pltpu.CompilerParams(
            dimension_semantics=("arbitrary",), vmem_limit_bytes=LIMIT
        ),
        cost_estimate=QUICK,
    )(q, keys, values, token_seg, text_seg)


def cross_backward_kernel(
    q_ref, k_ref, v_ref, dc_ref, tok_ref, txt_ref, dq_ref, dk_ref, dv_ref, dk_acc, dv_acc
):
    win, mask = head_window(pl.program_id(0))
    keys, values = k_ref[:, win], v_ref[:, win]
    scale = XHEAD ** (-0.5)
    none = jnp.zeros((), BF16)
    dk_acc[...] = jnp.zeros_like(dk_acc)
    dv_acc[...] = jnp.zeros_like(dv_acc)

    @pl.loop(0, q_ref.shape[0] // BROWS)
    def _(i):
        at = pl.ds(pl.multiple_of(i * BROWS, BROWS), BROWS)
        q = jnp.where(mask, q_ref[at, win], none)
        dc = jnp.where(mask, dc_ref[at, win], none)
        probs = cross_probs(q, keys, tok_ref[at, 0:1], txt_ref[...])
        d_probs = mm_nt(dc, values)
        along = jnp.sum(probs * d_probs, axis=-1, keepdims=True)
        d_scores = bf(probs * (d_probs - along))
        dq_ref[at, win] = jnp.where(mask, bf(mm(d_scores, keys) * scale), dq_ref[at, win])
        dk_acc[...] += mm_tn(d_scores, q)
        dv_acc[...] += mm_tn(bf(probs), dc)

    dk_ref[:, win] = jnp.where(mask, dk_acc[...] * scale, dk_ref[:, win])
    dv_ref[:, win] = jnp.where(mask, dv_acc[...], dv_ref[:, win])


def cross_backward(q, keys, values, d_cross, token_seg, text_seg):
    n_tok = q.shape[0]
    n_txt = keys.shape[0]
    return pl.pallas_call(
        cross_backward_kernel,
        grid=(XHEADS,),
        in_specs=[
            whole_spec((n_tok, D)), whole_spec((n_txt, D)), whole_spec((n_txt, D)),
            whole_spec((n_tok, D)), whole_spec((n_tok, 1)), whole_spec((1, n_txt)),
        ],
        out_specs=[whole_spec((n_tok, D)), whole_spec((n_txt, D)), whole_spec((n_txt, D))],
        out_shape=[
            jax.ShapeDtypeStruct((n_tok, D), BF16),
            jax.ShapeDtypeStruct((n_txt, D), F32),
            jax.ShapeDtypeStruct((n_txt, D), F32),
        ],
        scratch_shapes=[pltpu.VMEM((n_txt, WIN), F32), pltpu.VMEM((n_txt, WIN), F32)],
        compiler_params=pltpu.CompilerParams(
            dimension_semantics=("arbitrary",), vmem_limit_bytes=LIMIT
        ),
        cost_estimate=QUICK,
    )(q, keys, values, d_cross, token_seg, text_seg)


GL = 128
GROUPS = D // GL


def parts(value):
    high = bf(value)
    return high, bf(value - wide(high))


def group_heads():
    row = lax.broadcasted_iota(jnp.int32, (GL, GL), 0) // HEAD
    col = lax.broadcasted_iota(jnp.int32, (GL, GL), 1) // HEAD
    return wide(row == col)


def both_segments(value, second):
    value = wide(value)
    late = value * second
    return bf(value - late), bf(late)


def state_kernel(k_ref, v_ref, sec_ref, kv_ref, ks_ref):
    same = group_heads()
    k0, k1 = both_segments(k_ref[...], sec_ref[...])
    kv_ref[0, 0] = mm_tn(k0, v_ref[...]) * same
    kv_ref[0, 1] = mm_tn(k1, v_ref[...]) * same
    ks_ref[0, 0] = jnp.broadcast_to(jnp.sum(wide(k0), axis=0, keepdims=True), (8, GL))
    ks_ref[0, 1] = jnp.broadcast_to(jnp.sum(wide(k1), axis=0, keepdims=True), (8, GL))


def attend(q_ref, sec_ref, kv_ref, ks_ref, same):
    q0, q1 = both_segments(q_ref[...], sec_ref[...])
    numer = 0.0
    denom = 1.0
    for i, q in enumerate((q0, q1)):
        for part in parts(kv_ref[0, i]):
            numer = numer + mm(q, part)
        sums = jnp.transpose(jnp.broadcast_to(ks_ref[0, i, 0:1], (GL, GL))) * same
        for part in parts(sums):
            denom = denom + mm(q, part)
    return q0, q1, numer, denom


def attend_kernel(q_ref, sec_ref, kv_ref, ks_ref, out_ref):
    _, _, numer, denom = attend(q_ref, sec_ref, kv_ref, ks_ref, group_heads())
    out_ref[...] = bf(numer / denom)


def attend_back_kernel(q_ref, da_ref, sec_ref, kv_ref, ks_ref, dq_ref, dkv_ref, dks_ref):
    same = group_heads()
    second = sec_ref[...]
    q0, q1, numer, denom = attend(q_ref, sec_ref, kv_ref, ks_ref, same)
    inverse = 1.0 / denom
    d_num = da_ref[...] * inverse
    high, low = parts(d_num * numer)
    ones = bf(same)
    d_den = -(mm(high, ones) + mm(low, ones)) * inverse
    d_parts = parts(d_num)
    back = []
    for i, q in enumerate((q0, q1)):
        total = 0.0
        grad = 0.0
        for part in d_parts:
            total = total + mm_tn(q, part)
        for part in parts(kv_ref[0, i]):
            for left in d_parts:
                grad = grad + mm_nt(left, part)
        dkv_ref[0, i] = total * same
        dks_ref[0, i] = jnp.broadcast_to(
            jnp.sum(wide(q) * d_den, axis=0, keepdims=True), (8, GL)
        )
        back.append(grad + d_den * ks_ref[0, i, 0:1])
    dq = jnp.where(second > 0, back[1], back[0])
    dq_ref[...] = bf(jnp.where(wide(q_ref[...]) > 0, dq, 0.0))


def state_back_kernel(k_ref, v_ref, sec_ref, dkv_ref, dks_ref, dk_ref, dv_ref):
    second = sec_ref[...] > 0
    k, v = k_ref[...], v_ref[...]
    dk, dv = [], []
    for i in range(2):
        grad_k = dks_ref[0, i, 0:1]
        grad_v = 0.0
        for part in parts(dkv_ref[0, i]):
            grad_k = grad_k + mm_nt(v, part)
            grad_v = grad_v + mm(k, part)
        dk.append(grad_k)
        dv.append(grad_v)
    dk_ref[...] = bf(jnp.where(wide(k) > 0, jnp.where(second, dk[1], dk[0]), 0.0))
    dv_ref[...] = bf(jnp.where(wide(v) > 0, jnp.where(second, dv[1], dv[0]), 0.0))


def by_group(kernel, n_tok, ins, outs, out_types):
    specs = dict(
        tok=pl.BlockSpec((n_tok, GL), lambda g: (0, g)),
        seg=whole_spec((n_tok, GL)),
        kv=pl.BlockSpec((1, 2, GL, GL), lambda g: (g, 0, 0, 0)),
        ks=pl.BlockSpec((1, 2, 8, GL), lambda g: (g, 0, 0, 0)),
    )
    shapes = dict(tok=(n_tok, D), kv=(GROUPS, 2, GL, GL), ks=(GROUPS, 2, 8, GL))
    return pl.pallas_call(
        kernel,
        grid=(GROUPS,),
        in_specs=[specs[i] for i in ins],
        out_specs=[specs[o] for o in outs],
        out_shape=[jax.ShapeDtypeStruct(shapes[o], t) for o, t in zip(outs, out_types)],
        compiler_params=pltpu.CompilerParams(
            dimension_semantics=("arbitrary",), vmem_limit_bytes=LIMIT
        ),
        cost_estimate=QUICK,
    )


def update(weight, grad, moment, average, factor, rate):
    clipped = factor * grad
    moment_new = MOMENTUM * moment + clipped
    weight_new = weight - rate * (clipped + MOMENTUM * moment_new)
    average_new = average + AVERAGE_RATE * (weight_new - average)
    return (weight_new, moment_new, average_new)


def local(
    n_dp, n_mp,
    latents, noise, captions, res_ids, timesteps, caption_lengths,
    in_proj, out_proj, w_up, w_down, cond, conv, tables,
    mom_in, mom_out, mom_up, mom_down, mom_cond, mom_conv, mom_tables,
    avg_in, avg_out, avg_up, avg_down, avg_cond, avg_conv, avg_tables,
):
    place = Place(n_dp, n_mp)
    y, c = place.y, place.c
    half_dp = n_dp // 2
    dl = D // n_dp
    spot = jnp.stack([y, c]).astype(jnp.int32)
    owner_rows = cond.shape[0]

    cond_b = bf(cond)
    units_b = unit_split(place, as_units(bf(in_proj), bf(out_proj)))
    cap_chunk = chunk_of(place, CAP_ROWS)
    cap_mine = spread_rows(place, cond_b, TIME_ROWS, CAP_ROWS)
    packed = jnp.concatenate([units_b.reshape(-1, D), cap_mine], axis=0)
    ff_b = jnp.stack([bf(w_up[:, 0]), bf(w_up[:, 1]), bf(w_down).T])
    ff_b = jnp.pad(ff_b, ((0, 0), (0, 0), (0, FFB - ff_b.shape[2])))
    packed, ff_b, cond_time = lax.optimization_barrier((packed, ff_b, cond_b))
    got = lax.all_gather(packed, AXES, axis=0)
    by_place = got.reshape((n_dp, 2, 2) + packed.shape)
    w_q, w_k, w_v, w_o0, w_xq, w_o1, w_xk, w_xv = [
        by_place[:, i, j, part * dl : (part + 1) * dl].reshape(D, D)
        for part in (0, 1) for i in (0, 1) for j in (0, 1)
    ]
    cap_w = got[:, 2 * dl :].reshape(-1, D)
    w_cap1, w_cap2 = cap_w[:CAPD], cap_w[CAPD:CAP_ROWS]
    ffw = lax.all_gather(ff_b.reshape(3 * dl, FFB), AXES, axis=0)
    if dl % 16 == 0:
        ffw = ffw.reshape(n_dp, 4, 3 * dl, FFB)
    else:
        ffw = ffw.reshape(n_dp, 2, 2, 3, dl, FFB).transpose(3, 0, 4, 2, 1, 5)
        ffw = ffw.reshape(1, 1, 3 * D, FFP)

    spread_time = spread_rows(place, cond_time, 0, TIME_ROWS)
    w_time = gather_rows_all(place, spread_time, (place.x_mask, 2, 1))[:TIME_ROWS]
    facts = jnp.concatenate([timesteps, res_ids[:, None]], axis=1)
    for b in range(place.dp_bits):
        mask = n_mp << b
        facts = ordered(place.bit(mask), facts, place.swap(facts, mask), 0)
    steps_all = facts[:, :4].reshape(-1)
    count = jnp.sum(jnp.where(facts[:, 4] == 0, 4.0, 1.0))
    slots = steps_all.shape[0]

    resolution = lax.dynamic_index_in_dim(res_ids, y, 0, False)
    lengths = lax.dynamic_index_in_dim(caption_lengths, y, 0, False)
    steps_t = lax.dynamic_index_in_dim(timesteps, y, 0, False)
    pair = jnp.stack([latents, noise])
    quarters = jnp.stack([pair] + [place.swap(pair, mask) for mask in (1, 2, 3)])
    parts = [lax.dynamic_index_in_dim(quarters, (2 * c + j) ^ place.mp, 0, False) for j in (0, 1)]
    tokens = jnp.concatenate(
        [lax.dynamic_index_in_dim(part, y, 1, False) for part in parts], axis=1
    )
    n_tok = tokens.shape[1]
    rows = n_tok // SIDE
    grid = tokens.reshape(2, rows, SIDE, CIN)
    tokens = jnp.where(c == 1, grid[:, ::-1], grid).reshape(2, n_tok, CIN)
    clean, noisy = wide(tokens[0]), wide(tokens[1])
    col = jnp.arange(n_tok, dtype=jnp.int32)[:, None] % SIDE
    second = (col >= SIDE // 2) & (resolution == 0)
    seg0 = jnp.where(resolution == 0, 2 * c, 0)
    seg1 = jnp.where(resolution == 0, 2 * c + 1, 0)
    token_seg = jnp.where(second, seg1, seg0)

    def pick(table):
        first = lax.dynamic_index_in_dim(table, seg0, 0, True)
        other = lax.dynamic_index_in_dim(table, seg1, 0, True)
        return jnp.where(second, other, first)

    def by_segment(value):
        late = jnp.sum(jnp.where(second, value, 0.0), axis=0)
        early = jnp.sum(jnp.where(second, 0.0, value), axis=0)
        slot = jnp.arange(4, dtype=jnp.int32)[:, None]
        table = jnp.where(slot == seg0, early, 0.0) + jnp.where(slot == seg1, late, 0.0)
        return table, early + late

    sigma = pick(wide(steps_t)[:, None] / TMAX)
    mixed_in = (1.0 - sigma) * clean + sigma * noisy
    target = noisy - clean
    image_tokens = jnp.where(resolution == 0, (SIDE // 2) ** 2, SIDE * SIDE).astype(F32)
    loss_weight = 1.0 / (CIN * image_tokens * count)

    freq_b = bf(time_embed(steps_all))
    time_hidden = mm(freq_b, w_time[:FREQ])
    hidden_b = bf(jax.nn.silu(time_hidden))
    time_emb = mm(hidden_b, w_time[FREQ:])
    silu_b = bf(jax.nn.silu(time_emb))
    mod_mine = mm_nt(silu_b, cond_b).reshape(n_dp, 2, 1, 4 * owner_rows)
    mod_send = jnp.broadcast_to(mod_mine, (n_dp, 2, 2, 4 * owner_rows))
    mod_got = lax.all_to_all(mod_send.reshape(place.n, 4 * owner_rows), AXES, 0, 0)
    time_mod = mod_got.reshape(place.n, 4, owner_rows).transpose(1, 0, 2).reshape(4, -1)
    time_mod = time_mod[:, BLOCK_AT:].reshape(4, 6, D)
    mod_table = tables[None, :6] + time_mod
    mods = [pick(mod_table[:, k]) for k in range(6)]
    canvas = place.dp * 2 + y
    emb_mine = lax.dynamic_slice_in_dim(time_emb, canvas * 4, 4, 0)
    emb_tok = pick(emb_mine)

    own_cap = lax.dynamic_index_in_dim(captions, y, 0, False)
    their_cap = lax.dynamic_index_in_dim(captions, 1 - y, 0, False)
    caption = jnp.concatenate([own_cap, place.swap(their_cap, 2)], axis=0)
    quarter = own_cap.shape[0]
    within = jnp.arange(quarter, dtype=jnp.int32)
    text_at = jnp.concatenate([(place.mp ^ m) * quarter + within for m in (0, 2, 1, 3)])
    ends = jnp.cumsum(lengths)
    text_segment = jnp.sum((text_at[:, None] >= ends[None, :]).astype(jnp.int32), axis=1)
    cap_hidden = mm(caption, w_cap1)
    cap_act, gelu_pull = jax.vjp(partial(jax.nn.gelu, approximate=True), cap_hidden)
    cap_act_b = bf(cap_act)
    text_raw = mm(cap_act_b, w_cap2)
    gain = tables[8]
    text_inv = lax.rsqrt(jnp.mean(text_raw * text_raw, -1, keepdims=True) + EPS)
    text_hat = text_raw * text_inv
    text_b = bf(text_hat * gain)
    text_k = bf(mm(text_b, w_xk))
    text_v = bf(mm(text_b, w_xv))
    keys = jnp.concatenate([text_k, place.swap(text_k, 1)], axis=0)
    values = jnp.concatenate([text_v, place.swap(text_v, 1)], axis=0)

    embed = mm(mixed_in, tables[9 : 9 + CIN], HIGH)
    hat_a, inv_a = layer_norm(embed)
    normed_a = bf(hat_a * (1.0 + mods[1]) + mods[0])
    q = bf(jax.nn.relu(mm(normed_a, w_q)))
    k = bf(jax.nn.relu(mm(normed_a, w_k)))
    v = bf(jax.nn.relu(mm(normed_a, w_v)))
    whole_image = wide(resolution == 1)
    second_wide = jnp.broadcast_to(wide(second), (n_tok, GL))

    def shared(state, sums):
        first = jnp.concatenate([state[:, 0], sums[:, 0]], axis=1)
        first = first + whole_image * place.swap(first, 1)
        state = jnp.stack([first[:, :GL], state[:, 1]], axis=1)
        return state, jnp.stack([first[:, GL:], sums[:, 1]], axis=1)

    group_call = partial(by_group, n_tok=n_tok)
    state, key_sum = group_call(
        state_kernel, ins=("tok", "tok", "seg"), outs=("kv", "ks"), out_types=(F32, F32)
    )(k, v, second_wide)
    state, key_sum = shared(state, key_sum)
    (attn_b,) = group_call(
        attend_kernel, ins=("tok", "seg", "kv", "ks"), outs=("tok",), out_types=(BF16,)
    )(q, second_wide, state, key_sum)
    branch_a = mm_nt(attn_b, w_o0)
    state_a = embed + mods[2] * branch_a

    state_b = bf(state_a)
    xq = bf(mm(state_b, w_xq))
    cross_b = cross_forward(xq, keys, values, token_seg, text_segment[None, :])
    state_c = state_a + mm_nt(cross_b, w_o1)

    hat_f, inv_f = layer_norm(state_c)
    normed_f = bf(hat_f * (1.0 + mods[4]) + mods[3])
    taps = to_ff(conv)
    flipped = jnp.concatenate([taps[:, 6:9], taps[:, 3:6], taps[:, 0:3], taps[:, 9:]], axis=1)
    taps = jnp.where(c == 1, flipped, taps)
    column = jnp.arange(SIDE, dtype=jnp.int32)[:, None]
    middle = SIDE // 2
    left_ok = (column != 0) & ((resolution == 1) | (column != middle))
    right_ok = (column != SIDE - 1) & ((resolution == 1) | (column != middle - 1))
    left_ok = jnp.broadcast_to(wide(left_ok), (SIDE, CB))
    right_ok = jnp.broadcast_to(wide(right_ok), (SIDE, CB))
    halo_on = whole_image.reshape(1, 1)
    edge = n_tok - SIDE
    x_ext = jnp.concatenate([normed_f, place.swap(normed_f[edge:], 1)], axis=0)
    upper, z, gated_b, branch_f = ffn_forward(
        x_ext, ffw, taps, left_ok, right_ok, halo_on
    )
    z_halo = place.swap(z[:, edge:], 1)
    state_f = state_c + mods[5] * branch_f

    hat_o, inv_o = layer_norm(state_f)
    shift_o = tables[6] + emb_tok
    scale_o = tables[7] + emb_tok
    final = hat_o * (1.0 + scale_o) + shift_o
    out_rows = tables[9 + CIN :]
    output = mm_nt(final, out_rows, HIGH)
    error = output - target
    loss = jnp.sum(error * error) * loss_weight

    d_output = 2.0 * loss_weight * error
    d_final = mm(d_output, out_rows, HIGH)
    d_out_rows = mm_tn(d_output, final, HIGH)
    d_shift_seg, d_shift_o = by_segment(d_final)
    d_scale_seg, d_scale_o = by_segment(d_final * hat_o)
    d_emb_mine = d_shift_seg + d_scale_seg
    d_emb = d_emb_mine + place.swap(d_emb_mine, 1)
    d_state_f = layer_norm_back(d_final * (1.0 + scale_o), hat_o, inv_o)

    split_dp = (2,) * place.dp_bits
    far = [(b, n_mp << (place.dp_bits - 1 - b)) for b in range(place.dp_bits - 2, -1, -1)]

    def stages(lead, order):
        table = {
            "x": ("abs", lead + place.dp_bits - 1, place.x_mask),
            "y": ("rel", lead - 1, 2),
        }
        rest = [("abs", lead + axis, mask) for axis, mask in far]
        return [table[o] if o in table else rest.pop(0) for o in order] + rest

    def ff_flow(left, right, orders):
        shape = (1, 2) + split_dp + (dl, FFB)
        flows = []
        for i, order in enumerate(orders):
            away = ff_grad(spot, left, right, i, 1, BF16)
            flows.append(Flow(place, away.reshape(shape), stages(2, order)))
            left, right, away = lax.optimization_barrier((left, right, away))
        for i, flow in enumerate(flows):
            flow.keep = ff_grad(spot, left, right, i, 0, F32).reshape(shape)
        return flows

    def unit_flow(arrays, pairs, order):
        shape = (2,) + split_dp + (dl, D)
        away = unit_grad(spot, arrays, pairs, 1, BF16)
        flow = Flow(place, away.reshape(shape), stages(1, order))
        arrays, away = lax.optimization_barrier((arrays, away))
        flow.keep = unit_grad(spot, arrays, pairs, 0, F32).reshape(shape)
        return flow

    def settle(value, flows):
        value, keeps = lax.optimization_barrier((value, [flow.keep for flow in flows]))
        for flow, keep in zip(flows, keeps):
            flow.keep = keep
        return tick(value, flows)

    d_branch_f = bf(mods[5] * d_state_f)
    d_edge = place.swap(d_branch_f[edge:], 1)
    flow_dn, = ff_flow(d_branch_f, gated_b[None], ["yx"])
    d_ext = jnp.concatenate([d_branch_f, d_edge], axis=0)
    d_ext = settle(d_ext, [flow_dn])
    d_upper, d_taps, d_normed_f = tick(
        ffn_backward(d_ext, ffw, upper, z, z_halo, taps, left_ok, right_ok, halo_on), [flow_dn]
    )
    unflipped = jnp.concatenate(
        [d_taps[:, 6:9], d_taps[:, 3:6], d_taps[:, 0:3], d_taps[:, 9:]], axis=1
    )
    conv_grad = from_ff(jnp.where(c == 1, unflipped, d_taps))
    flow_up = ff_flow(normed_f, d_upper, ["xy", "yx"])
    ffn_flows = [flow_dn] + flow_up
    soon = jnp.concatenate([conv_grad.reshape(-1, D), d_out_rows], axis=0)
    soon_masks = [1, 2] + [n_mp << b for b in range(place.dp_bits)]
    soon_sent = place.swap(soon, soon_masks[0])
    d_normed_f, soon_sent = settle((d_normed_f, soon_sent), flow_up)
    soon = soon + soon_sent
    d_state_c = d_state_f + layer_norm_back(d_normed_f * (1.0 + mods[4]), hat_f, inv_f)
    d_mods = [None] * 6
    d_mods[5] = by_segment(d_state_f * branch_f)
    d_mods[3] = by_segment(d_normed_f)
    d_mods[4] = by_segment(d_normed_f * hat_f)

    d_branch_c = bf(d_state_c)
    d_cross = bf(mm(d_branch_c, w_o1))
    soon_sent = place.swap(soon, soon_masks[1])
    (d_xq_b, d_keys, d_values), soon_sent = tick(
        (
            cross_backward(xq, keys, values, d_cross, token_seg, text_segment[None, :]),
            soon_sent,
        ),
        ffn_flows,
    )
    soon = soon + soon_sent
    half_txt = TXT // 2
    d_kv = jnp.stack([d_keys, d_values])
    d_kv = d_kv[:, :half_txt] + place.swap(d_kv[:, half_txt:], 1)
    d_kv_b = bf(d_kv)
    early = unit_flow(
        [state_b, d_xq_b, d_branch_c, cross_b, text_b, d_kv_b[0], d_kv_b[1]],
        ((0, 1), (2, 3), (4, 5), (4, 6)),
        "yzx",
    )
    d_state_a = d_state_c + mm_nt(d_xq_b, w_xq)
    soon_sent = place.swap(soon, soon_masks[2])
    d_state_a, d_kv_b, soon_sent = settle((d_state_a, d_kv_b, soon_sent), [early])
    soon = soon + soon_sent

    d_branch_a = bf(mods[2] * d_state_a)
    d_mods[2] = by_segment(d_state_a * branch_a)
    d_attn = mm(d_branch_a, w_o0)
    soon_sent = place.swap(soon, soon_masks[3])
    (dq_b, d_state, d_sum), soon_sent = tick(
        (group_call(
            attend_back_kernel,
            ins=("tok", "tok", "seg", "kv", "ks"),
            outs=("tok", "kv", "ks"),
            out_types=(BF16, F32, F32),
        )(q, d_attn, second_wide, state, key_sum), soon_sent),
        ffn_flows,
    )
    soon = soon + soon_sent
    d_state, d_sum = shared(d_state, d_sum)
    dk_b, dv_b = group_call(
        state_back_kernel,
        ins=("tok", "tok", "seg", "kv", "ks"),
        outs=("tok", "tok"),
        out_types=(BF16, BF16),
    )(k, v, second_wide, d_state, d_sum)
    d_normed_a = mm_nt(dq_b, w_q) + mm_nt(dk_b, w_k) + mm_nt(dv_b, w_v)
    d_mods[0] = by_segment(d_normed_a)
    d_mods[1] = by_segment(d_normed_a * hat_a)

    d_mod = jnp.stack([table for table, _ in d_mods], axis=1).reshape(4, 6 * D)
    d_mod = jnp.pad(d_mod, ((0, 0), (BLOCK_AT, 0)))
    d_mod = d_mod.reshape(4, place.n, owner_rows).transpose(1, 0, 2)
    d_mod, dq_b, dk_b, dv_b = lax.optimization_barrier((d_mod, dq_b, dk_b, dv_b))
    d_mod = lax.all_to_all(d_mod, AXES, 0, 0)
    late = unit_flow(
        [normed_a, dq_b, dk_b, dv_b, d_branch_a, attn_b],
        ((0, 1), (0, 2), (0, 3), (4, 5)),
        "xy",
    )
    d_embed = d_state_a + layer_norm_back(d_normed_a * (1.0 + mods[1]), hat_a, inv_a)
    g_patch = mm_tn(mixed_in, d_embed, HIGH)
    d_mod, d_kv_b, g_patch, late.keep, late.moving, early.moving = lax.optimization_barrier(
        (d_mod, d_kv_b, g_patch, late.keep, late.moving, early.moving)
    )
    near_far = [stage for stage in stages(1, "") if stage[1] != 1]
    late_flows = late.split(
        1, [stages(1, order)[:2] + near_far for order in ("xy", "yx")]
    )
    d_mod, d_kv_b = tick((d_mod, d_kv_b), ffn_flows)
    for flow in late_flows + [early]:
        flow.land()
    for mask in soon_masks[4:]:
        soon = soon + place.swap(soon, mask)
    conv_grad = soon[: conv_grad.size // D].reshape(conv_grad.shape)
    d_out_rows = soon[conv_grad.size // D :]
    d_mod = d_mod.reshape(slots // 4, 2, 4, owner_rows).sum(1).reshape(slots, owner_rows)
    d_silu = mm(d_mod, wide(cond_b), HIGH)
    g_block = mm_tn(d_mod, wide(silu_b), HIGH)

    d_text = mm_nt(d_kv_b[0], w_xk) + mm_nt(d_kv_b[1], w_xv)
    d_gain = jnp.sum(d_text * text_hat, axis=0)
    d_hat = d_text * gain
    d_text_raw = text_inv * (d_hat - text_hat * jnp.mean(d_hat * text_hat, -1, keepdims=True))
    d_text_raw_b = bf(d_text_raw)
    d_cap_b = bf(gelu_pull(mm_nt(d_text_raw_b, w_cap2))[0])
    cap_shape = split_dp + (2, 1, cap_chunk, D)
    if cap_chunk == GL:
        cap_parts = [caption, cap_act_b, d_cap_b, d_text_raw_b]
        cap_sends = cap_grad(spot, cap_parts, place.n, 1, BF16).reshape(cap_shape)
        cap_keep = partial(cap_grad, spot, cap_parts, place.n, 0, F32)
    else:
        g_cap = jnp.concatenate(
            [
                mm_tn(caption, d_cap_b),
                mm_tn(cap_act_b, d_text_raw_b),
                jnp.zeros((place.n * cap_chunk - CAP_ROWS, D), F32),
            ],
            axis=0,
        ).reshape(split_dp + (2, 2, cap_chunk, D))
        cap_sends = bf(lax.dynamic_slice_in_dim(g_cap, 1 - c, 1, place.dp_bits + 1))
        cap_keep = partial(lax.dynamic_slice_in_dim, g_cap, c, 1, place.dp_bits + 1)

    d_rows_six = jnp.stack([total for _, total in d_mods])
    tables_grad = jnp.concatenate(
        [d_rows_six, d_shift_o[None], d_scale_o[None], d_gain[None], g_patch], axis=0
    )
    masks = [1, 2] + [n_mp << b for b in range(place.dp_bits)]
    d_silu = jnp.broadcast_to(d_silu.reshape(n_dp, 2, 1, 4 * D), (n_dp, 2, 2, 4 * D))
    d_silu = lax.all_to_all(d_silu.reshape(place.n, 4 * D), AXES, 0, 0).sum(0).reshape(4, D)
    cap_flow = Flow(
        place,
        cap_sends,
        [("abs", place.dp_bits, 2), ("abs", place.dp_bits - 1, place.x_mask)]
        + [("abs",) + pair_ for pair_ in far],
    )
    cap_flow.keep = cap_keep().reshape(cap_shape)
    d_time = d_silu * silu_grad(emb_mine) + d_emb
    d_hidden = mm_nt(d_time, wide(w_time[FREQ:]), HIGH)
    hidden_mine = lax.dynamic_slice_in_dim(time_hidden, canvas * 4, 4, 0)
    d_times = jnp.concatenate([d_time, d_hidden * silu_grad(hidden_mine)], axis=0)
    cap_far = [stage for stage in [("abs",) + pair_ for pair_ in far] if stage[1] != 0]
    cap_y, cap_x = ("abs", place.dp_bits, 2), ("abs", place.dp_bits - 1, place.x_mask)
    cap_flows = cap_flow.split(0, [[cap_y, cap_x] + cap_far, cap_far[:1] + [cap_y, cap_x] + cap_far[1:]])
    last = late_flows + cap_flows + [early]
    for flow in cap_flows:
        flow.land()
    ff_own = [flow.drain().reshape(dl, FFB)[:, : FF // 4] for flow in ffn_flows]
    part_sq = sum(jnp.sum(grad * grad) for grad in [g_block] + ff_own)
    row = lax.broadcasted_iota(jnp.int32, (8, 128), 0)
    scalars = jnp.where(row == 0, part_sq, loss)
    small = jnp.pad(tables_grad, ((0, -tables_grad.shape[0] % 8), (0, 0)))
    top = n_mp << place.dp_bits - 1
    joined, cap_own, small, d_times, scalars = finish(
        n_mp, last, top, masks, small, d_times[None], scalars
    )
    tables_grad = jnp.concatenate([small[: tables_grad.shape[0]], d_out_rows], axis=0)
    d_times = d_times.reshape(-1, 2, 4, D).transpose(1, 0, 2, 3).reshape(2, slots, D)
    g_time2 = mm_tn(wide(hidden_b), d_times[0], HIGH)
    g_time1 = mm_tn(wide(freq_b), d_times[1], HIGH)
    spots = -(-TIME_ROWS // owner_rows)
    g_time = jnp.concatenate(
        [g_time1, g_time2, jnp.zeros(((spots + 1) * owner_rows - TIME_ROWS, D), F32)], axis=0
    )
    g_time = lax.dynamic_slice_in_dim(
        g_time, jnp.minimum(place.me, spots) * owner_rows, owner_rows, 0
    )

    cap_own = cap_own.reshape(cap_chunk, D)
    g_cap = collect_rows(place, cap_own, owner_rows, TIME_ROWS, CAP_ROWS)
    g_cond = g_cap + g_block + g_time
    g_in, g_out = from_units(joined.transpose(1, 0, 2, 3).reshape(8, dl, D // 4))
    g_upper = jnp.stack(ff_own[1:], axis=1)
    g_lower = ff_own[0].T
    owned = (g_in, g_out, g_upper, g_lower, g_cond)

    squares, loss = scalars[0, 0], scalars[1, 0]
    squares = squares + jnp.sum(g_time1 * g_time1) + jnp.sum(g_time2 * g_time2)
    norm = jnp.sqrt(squares + jnp.sum(conv_grad * conv_grad) + jnp.sum(tables_grad * tables_grad))
    factor = CLIP / jnp.maximum(norm, CLIP)
    rate = STEP_SCALE * math.sqrt(PARAMS) / CLIP
    grads = owned + (conv_grad, tables_grad)
    weights = (in_proj, out_proj, w_up, w_down, cond, conv, tables)
    moments = (mom_in, mom_out, mom_up, mom_down, mom_cond, mom_conv, mom_tables)
    averages = (avg_in, avg_out, avg_up, avg_down, avg_cond, avg_conv, avg_tables)
    new = [
        update(weights[i], grads[i], moments[i], averages[i], factor, rate) for i in range(7)
    ]
    moments_out = [new[i][1] for i in range(5)] + [factor * conv_grad, new[6][1]]
    return (loss, norm, *[n[0] for n in new], *moments_out, *[n[2] for n in new])


def solution(mesh):
    tokens = P("dp", "mp", None)
    weights = (
        P("dp", None, "mp"),
        P(None, "mp", "dp"),
        P("dp", None, "mp"),
        P("mp", "dp"),
        P(("dp", "mp"), None),
        P(),
        P(),
    )
    in_specs = (tokens, tokens, tokens, P("dp"), P("dp", None), P("dp", None)) + weights * 3
    out_specs = (P(), P()) + weights * 3
    body = partial(local, mesh.shape["dp"], mesh.shape["mp"])
    return jax.shard_map(body, mesh=mesh, in_specs=in_specs, out_specs=out_specs, check_vma=False)
```

```python
from functools import partial
import math

import jax
import jax.numpy as jnp
from jax import lax
from jax.experimental import pallas as pl
from jax.experimental.pallas import tpu as pltpu
from jax.sharding import PartitionSpec as P

D = 1152
FF = 2880
CAPD = 2304
CIN = 32
FREQ = 256
SIDE = 32
TXT = 512
HEAD = 32
XHEAD = 72
XHEADS = 16
PARAMS = 34277760
FFB = 768
FFP = 4 * FFB
TIME_ROWS = FREQ + D
CAP_ROWS = CAPD + D
BLOCK_AT = TIME_ROWS + CAP_ROWS

HIGH = lax.Precision.HIGHEST
EPS = 1e-06
CLIP = 0.001
MOMENTUM = 0.9
AVERAGE_RATE = 0.1
STEP_SCALE = 0.01
TMAX = 1000.0
MASKED = -1e30
AXES = ("dp", "mp")
F32 = jnp.float32
BF16 = jnp.bfloat16


def bf(value):
    return value.astype(BF16)


def wide(value):
    return value.astype(F32)


def dot(left, right, dims, precision=None):
    return lax.dot_general(
        left, right, (dims, ((), ())), precision=precision, preferred_element_type=F32
    )


def mm(left, right, precision=None):
    return dot(left, right, ((1,), (0,)), precision)


def mm_nt(left, right, precision=None):
    return dot(left, right, ((1,), (1,)), precision)


def mm_tn(left, right, precision=None):
    return dot(left, right, ((0,), (0,)), precision)


class Place:
    def __init__(self, n_dp, n_mp):
        self.n_dp, self.n_mp, self.n = n_dp, n_mp, n_dp * n_mp
        self.dp, self.mp = lax.axis_index("dp"), lax.axis_index("mp")
        self.me = self.dp * n_mp + self.mp
        self.y, self.c = self.mp // 2, self.mp % 2
        self.dp_bits = int(math.log2(n_dp))

    def bit(self, mask):
        return (self.me // mask) % 2

    def swap(self, value, mask):
        return lax.ppermute(value, AXES, [(i, i ^ mask) for i in range(self.n)])

    @property
    def far_masks(self):
        return [self.n_mp << b for b in range(1, self.dp_bits)]

    @property
    def x_mask(self):
        return self.n_mp


def ordered(bit, mine, theirs, axis):
    low = jnp.where(bit == 0, mine, theirs)
    high = jnp.where(bit == 0, theirs, mine)
    return jnp.concatenate([low, high], axis=axis)


def gather_far(place, block, axis):
    block = jnp.expand_dims(block, axis)
    for mask in place.far_masks:
        block = ordered(place.bit(mask), block, place.swap(block, mask), axis)
    return block


def gather_near(place, block, order):
    held = {0: block}
    for mask in order:
        held.update({key | mask: place.swap(value, mask) for key, value in held.items()})
    return held


def near_bits(place, key):
    flip = [1 if key & mask else 0 for mask in (place.x_mask, 2, 1)]
    own = (place.bit(place.x_mask), place.y, place.c)
    return [jnp.where(f == 1, 1 - o, o) for f, o in zip(flip, own)]


def gather_rows_all(place, block, order):
    rows, cols = block.shape
    held = gather_near(place, gather_far(place, block, 0), order)
    half = place.n_dp // 2
    out = jnp.zeros((half, 2, 2, 2, rows, cols), block.dtype)
    for key, value in held.items():
        x, y, c = near_bits(place, key)
        out = lax.dynamic_update_slice(out, value[:, None, None, None], (0, x, y, c, 0, 0))
    return out.reshape(place.n * rows, cols)


def spread_table(place, owner_rows, low, chunk):
    rounds = -(-owner_rows // chunk) + 1
    tables = []
    for step in range(rounds):
        pairs = []
        for owner in range(place.n):
            target = (owner_rows * owner - low) // chunk + step
            start = low + chunk * target - owner_rows * owner
            if 0 <= target < place.n and -chunk < start < owner_rows:
                pairs.append((owner, target))
        tables.append(pairs)
    return tables


def chunk_of(place, rows, unit=16):
    chunk = -(-rows // place.n)
    return -(-chunk // unit) * unit


def spread_rows(place, held, low, rows):
    owner_rows = held.shape[0]
    chunk = chunk_of(place, rows)
    padded = jnp.pad(held, ((chunk, chunk), (0, 0)))
    first = (owner_rows * place.me - low) // chunk
    total = None
    for step, pairs in enumerate(spread_table(place, owner_rows, low, chunk)):
        start = low + chunk * (first + step) - owner_rows * place.me + chunk
        piece = lax.dynamic_slice_in_dim(padded, start, chunk, 0)
        got = lax.ppermute(piece, AXES, pairs)
        total = got if total is None else total + got
    return total


def collect_rows(place, block, owner_rows, low, rows):
    chunk = block.shape[0]
    first = (owner_rows * place.me - low) // chunk
    got = [
        wide(lax.ppermute(bf(block), AXES, [(target, owner) for owner, target in pairs]))
        for pairs in spread_table(place, owner_rows, low, chunk)
    ]
    start = owner_rows * place.me - low - chunk * first
    mine = lax.dynamic_slice_in_dim(jnp.concatenate(got, axis=0), start, owner_rows, 0)
    row = owner_rows * place.me + jnp.arange(owner_rows, dtype=jnp.int32)[:, None]
    return jnp.where((row >= low) & (row < low + rows), mine, 0.0)


def halve(place, grad, stages):
    for axis, mask in stages:
        bit = place.bit(mask)
        half = grad.shape[axis] // 2
        away = lax.dynamic_slice_in_dim(grad, (1 - bit) * half, half, axis)
        keep = lax.dynamic_slice_in_dim(grad, bit * half, half, axis)
        grad = keep + wide(place.swap(bf(away), mask))
    return grad


def layer_norm(value):
    centred = value - jnp.mean(value, -1, keepdims=True)
    inverse = lax.rsqrt(jnp.mean(centred * centred, -1, keepdims=True) + EPS)
    return centred * inverse, inverse


def layer_norm_back(grad, normed, inverse):
    along = jnp.mean(grad * normed, -1, keepdims=True)
    return inverse * (grad - jnp.mean(grad, -1, keepdims=True) - normed * along)


def silu_grad(value):
    gate = jax.nn.sigmoid(value)
    return gate * (1.0 + value * (1.0 - gate))


def time_embed(steps_t):
    half_size = FREQ // 2
    freqs = jnp.exp(-math.log(10000.0) * jnp.arange(half_size, dtype=F32) / half_size)
    angles = wide(steps_t)[:, None] * freqs[None, :]
    return jnp.concatenate([jnp.cos(angles), jnp.sin(angles)], axis=1)


def to_ff(value):
    blocks = value.reshape(value.shape[:-1] + (4, FF // 4))
    pad = [(0, 0)] * (blocks.ndim - 1) + [(0, FFB - FF // 4)]
    blocks = jnp.pad(blocks, pad)
    blocks = jnp.stack([blocks[..., m, :] for m in (0, 2, 1, 3)], axis=-2)
    return blocks.reshape(value.shape[:-1] + (FFP,))


def from_ff(value):
    blocks = value.reshape(value.shape[:-1] + (4, FFB))[..., : FF // 4]
    blocks = jnp.stack([blocks[..., m, :] for m in (0, 2, 1, 3)], axis=-2)
    return blocks.reshape(value.shape[:-1] + (FF,))


def unit_split(place, units):
    units = units.reshape((2, 4) + units.shape[1:])

    def part(number):
        return lax.dynamic_index_in_dim(units, number, 1, False)

    got = [part(place.mp)] + [place.swap(part(place.mp ^ m), m) for m in (1, 2, 3)]
    stacked = jnp.stack(got)
    return jnp.concatenate(
        [lax.dynamic_index_in_dim(stacked, place.mp ^ m, 0, False) for m in range(4)], axis=-1
    )


def unit_join(place, block):
    cols = D // 4

    def part(number):
        return lax.dynamic_slice_in_dim(block, number * cols, cols, 2)

    got = [part(place.mp)] + [place.swap(part(place.mp ^ m), m) for m in (1, 2, 3)]
    stacked = jnp.stack(got)
    order = [lax.dynamic_index_in_dim(stacked, place.mp ^ m, 0, False) for m in range(4)]
    return jnp.stack(order, axis=1).reshape((8,) + order[0].shape[1:])


def as_units(in_w, out_w):
    inp = [in_w[:, k] for k in range(6)]
    outp = [out_w[j].T for j in range(2)]
    return jnp.stack([inp[0], inp[1], inp[2], outp[0], inp[3], outp[1], inp[4], inp[5]])


def from_units(units):
    g_in = jnp.stack([units[u] for u in (0, 1, 2, 4, 6, 7)], axis=1)
    g_out = jnp.stack([units[3].T, units[5].T])
    return g_in, g_out


class Flow:
    def __init__(self, place, sends, stages):
        self.place, self.stages = place, list(stages)
        self.keep = None
        self.moving = place.swap(sends, 1)
        self.sends = None

    def launch(self):
        self.moving = self.place.swap(self.sends, self.mask)
        self.sends = None

    def part(self, take):
        return wide(take(self.keep)) + wide(take(self.moving))

    def land(self):
        if not self.stages:
            self.keep = self.part(lambda value: value)
            self.moving = None
            return
        kind, axis, self.mask = self.stages.pop(0)
        if kind == "rel":
            away = self.part(lambda value: lax.slice_in_dim(value, 1, 2, axis=axis))
            keep = self.part(lambda value: lax.slice_in_dim(value, 0, 1, axis=axis))
        else:
            bit = self.place.bit(self.mask)
            away = self.part(lambda value: lax.dynamic_slice_in_dim(value, 1 - bit, 1, axis))
            keep = self.part(lambda value: lax.dynamic_slice_in_dim(value, bit, 1, axis))
        self.sends, self.keep, self.moving = bf(away), keep, None

    def split(self, axis, orders):
        flows = []
        for i, order in enumerate(orders):
            flow = Flow.__new__(Flow)
            flow.place, flow.stages, flow.sends = self.place, list(order), None
            flow.keep = lax.slice_in_dim(self.keep, i, i + 1, axis=axis)
            flow.moving = lax.slice_in_dim(self.moving, i, i + 1, axis=axis)
            flows.append(flow)
        return flows

    def drain(self):
        while self.moving is not None:
            self.land()
            if self.sends is not None:
                self.launch()
        return self.keep


def tick(value, flows):
    moving = [flow for flow in flows if flow.moving is not None]
    value, landed = lax.optimization_barrier((value, [flow.moving for flow in moving]))
    for flow, arrived in zip(moving, landed):
        flow.moving = arrived
        flow.land()
    ready = [flow for flow in moving if flow.sends is not None]
    value, sends = lax.optimization_barrier((value, [flow.sends for flow in ready]))
    for flow, out in zip(ready, sends):
        flow.sends = out
        flow.launch()
    return value


CB = 256
ROW = SIDE
LIMIT = 48 * 1024 * 1024
QUICK = pl.CostEstimate(flops=2**20, bytes_accessed=2**16, transcendentals=0)


def whole_spec(shape):
    return pl.BlockSpec(shape, lambda *_: (0,) * len(shape))


def ffn_forward_kernel(
    x_ref, w0_ref, w1_ref, wd_ref, taps_ref, left_ref, right_ref, on_ref,
    u_ref, z_ref, g_ref, out_ref, act, act_l, act_r
):
    rows = g_ref.shape[0] // ROW
    zero = jnp.zeros((ROW, CB), F32)
    x = x_ref[...]
    u_ref[0] = mm(x, w0_ref[...].reshape(D, CB))
    u_ref[1] = mm(x, w1_ref[...].reshape(D, CB))
    on = on_ref[0, 0]
    for k in range(2):
        for ref in (act, act_l, act_r):
            ref[k, pl.ds(0, ROW)] = zero

    def fill(r, scale):
        for k in range(2):
            u = u_ref[k, pl.ds(pl.multiple_of(r * ROW, ROW), ROW)]
            a = u * jax.nn.sigmoid(u) * scale
            at = pl.ds(pl.multiple_of(r * ROW + ROW, ROW), ROW)
            act[k, at] = a
            act_l[k, at] = pltpu.roll(a, 1, 0) * left_ref[...]
            act_r[k, at] = pltpu.roll(a, ROW - 1, 0) * right_ref[...]

    @pl.loop(0, rows)
    def _(r):
        fill(r, 1.0)

    fill(rows, on)

    @pl.loop(0, rows)
    def _(r):
        z = []
        for k in range(2):
            total = jnp.broadcast_to(taps_ref[k, pl.ds(9, 1)], (ROW, CB))
            for dr in range(3):
                at = pl.ds(pl.multiple_of(r * ROW + dr * ROW, ROW), ROW)
                for dc, ref in enumerate((act_l, act, act_r)):
                    total = total + ref[k, at] * taps_ref[k, pl.ds(dr * 3 + dc, 1)]
            z_ref[k, pl.ds(pl.multiple_of(r * ROW, ROW), ROW)] = total
            z.append(total)
        gated = z[0] * (z[1] * jax.nn.sigmoid(z[1]))
        g_ref[pl.ds(pl.multiple_of(r * ROW, ROW), ROW)] = bf(gated)

    part = mm_nt(g_ref[...], wd_ref[...].reshape(D, CB))

    @pl.when(pl.program_id(0) == 0)
    def _():
        out_ref[...] = part

    @pl.when(pl.program_id(0) > 0)
    def _():
        out_ref[...] += part


def ff_spec(ffw, k):
    groups, blocks, rows, lanes = ffw.shape
    per = lanes // CB

    def index(j):
        at = j // per
        return (0, at % 2 * 2 + at // 2 if blocks == 4 else 0, k, j % per)

    return pl.BlockSpec((groups, 1, rows // 3, CB), index)


def ffn_forward(x_ext, ffw, taps, left_ok, right_ok, on):
    n_ext = x_ext.shape[0]
    n_tok = n_ext - ROW
    weight = partial(ff_spec, ffw)
    pads = pltpu.VMEM((2, n_ext + ROW, CB), F32)
    return pl.pallas_call(
        ffn_forward_kernel,
        grid=(FFP // CB,),
        in_specs=[
            whole_spec((n_ext, D)), weight(0), weight(1), weight(2),
            pl.BlockSpec((2, 10, CB), lambda j: (0, 0, j)),
            whole_spec((ROW, CB)), whole_spec((ROW, CB)),
            pl.BlockSpec((1, 1), lambda j: (0, 0), memory_space=pltpu.SMEM),
        ],
        out_specs=[
            pl.BlockSpec((2, n_ext, CB), lambda j: (0, 0, j)),
            pl.BlockSpec((2, n_tok, CB), lambda j: (0, 0, j)),
            pl.BlockSpec((n_tok, CB), lambda j: (0, j)),
            whole_spec((n_tok, D)),
        ],
        out_shape=[
            jax.ShapeDtypeStruct((2, n_ext, FFP), F32),
            jax.ShapeDtypeStruct((2, n_tok, FFP), F32),
            jax.ShapeDtypeStruct((n_tok, FFP), BF16),
            jax.ShapeDtypeStruct((n_tok, D), F32),
        ],
        scratch_shapes=[pads, pads, pads],
        compiler_params=pltpu.CompilerParams(
            dimension_semantics=("arbitrary",), vmem_limit_bytes=LIMIT
        ),
        cost_estimate=QUICK,
    )(x_ext, ffw, ffw, ffw, taps, left_ok, right_ok, on)


def ffn_backward_kernel(
    d_ref, wd_ref, w0_ref, w1_ref, u_ref, z_ref, zh_ref, taps_ref, left_ref, right_ref, on_ref,
    du_ref, dt_ref, dn_ref, dg_buf, dz, dz_l, dz_r, acc
):
    n_tok = z_ref.shape[1]
    rows = n_tok // ROW
    zero = jnp.zeros((ROW, CB), F32)
    dg_buf[...] = mm(d_ref[...], wd_ref[...].reshape(D, CB))
    for k in range(2):
        for ref in (dz, dz_l, dz_r):
            ref[k, pl.ds(0, ROW)] = zero
    acc[...] = jnp.zeros_like(acc)

    def fill(r, z0, z1, scale, count):
        dg = dg_buf[pl.ds(pl.multiple_of(r * ROW, ROW), ROW)]
        gate = jax.nn.sigmoid(z1)
        soft = z1 * gate
        at = pl.ds(pl.multiple_of(r * ROW + ROW, ROW), ROW)
        d_both = (dg * soft, dg * z0 * (gate + soft * (1.0 - gate)))
        for k in range(2):
            value = d_both[k] * scale
            dz[k, at] = value
            dz_l[k, at] = pltpu.roll(value * left_ref[...], ROW - 1, 0)
            dz_r[k, at] = pltpu.roll(value * right_ref[...], 1, 0)
            if count:
                acc[k, 9] += fold(value)

    def fold(value):
        return value[0:8] + value[8:16] + value[16:24] + value[24:32]

    @pl.loop(0, rows)
    def _(r):
        at = pl.ds(pl.multiple_of(r * ROW, ROW), ROW)
        fill(r, z_ref[0, at], z_ref[1, at], 1.0, True)

    fill(rows, zh_ref[0], zh_ref[1], on_ref[0, 0], False)

    def back(r, taps_on):
        at = pl.ds(pl.multiple_of(r * ROW, ROW), ROW)
        for k in range(2):
            u = u_ref[k, at]
            gate = jax.nn.sigmoid(u)
            a = u * gate
            total = zero
            for dr in range(3):
                near = pl.ds(pl.multiple_of(r * ROW + (2 - dr) * ROW, ROW), ROW)
                for dc, ref in enumerate((dz_l, dz, dz_r)):
                    value = ref[k, near]
                    total = total + value * taps_ref[k, pl.ds(dr * 3 + dc, 1)]
                    if dr in taps_on:
                        acc[k, dr * 3 + dc] += fold(value * a)
            du_ref[k, at] = bf(total * (gate + a * (1.0 - gate)))

    @pl.loop(0, rows - 1)
    def _(r):
        back(r, (0, 1, 2))

    back(rows - 1, (1, 2))
    for k in range(2):
        u = u_ref[k, pl.ds(n_tok, ROW)]
        a = u * jax.nn.sigmoid(u) * on_ref[0, 0]
        for dc, ref in enumerate((dz_l, dz, dz_r)):
            acc[k, 6 + dc] += fold(ref[k, pl.ds(n_tok, ROW)] * a)
        for t in range(10):
            dt_ref[k, pl.ds(t, 1)] = jnp.sum(acc[k, t], axis=0, keepdims=True)

    part = mm_nt(du_ref[0], w0_ref[...].reshape(D, CB))
    part = part + mm_nt(du_ref[1], w1_ref[...].reshape(D, CB))

    @pl.when(pl.program_id(0) == 0)
    def _():
        dn_ref[...] = part

    @pl.when(pl.program_id(0) > 0)
    def _():
        dn_ref[...] += part


def ffn_backward(d_ext, ffw, upper, z, z_halo, taps, left_ok, right_ok, on):
    n_ext = d_ext.shape[0]
    n_tok = n_ext - ROW
    pads = pltpu.VMEM((2, n_ext + ROW, CB), F32)
    return pl.pallas_call(
        ffn_backward_kernel,
        grid=(FFP // CB,),
        in_specs=[
            whole_spec((n_ext, D)),
            ff_spec(ffw, 2), ff_spec(ffw, 0), ff_spec(ffw, 1),
            pl.BlockSpec((2, n_ext, CB), lambda j: (0, 0, j)),
            pl.BlockSpec((2, n_tok, CB), lambda j: (0, 0, j)),
            pl.BlockSpec((2, ROW, CB), lambda j: (0, 0, j)),
            pl.BlockSpec((2, 10, CB), lambda j: (0, 0, j)),
            whole_spec((ROW, CB)), whole_spec((ROW, CB)),
            pl.BlockSpec((1, 1), lambda j: (0, 0), memory_space=pltpu.SMEM),
        ],
        out_specs=[
            pl.BlockSpec((2, n_tok, CB), lambda j: (0, 0, j)),
            pl.BlockSpec((2, 10, CB), lambda j: (0, 0, j)),
            whole_spec((n_tok, D)),
        ],
        out_shape=[
            jax.ShapeDtypeStruct((2, n_tok, FFP), BF16),
            jax.ShapeDtypeStruct((2, 10, FFP), F32),
            jax.ShapeDtypeStruct((n_tok, D), F32),
        ],
        scratch_shapes=[
            pltpu.VMEM((n_ext, CB), F32), pads, pads, pads, pltpu.VMEM((2, 10, 8, CB), F32)
        ],
        compiler_params=pltpu.CompilerParams(
            dimension_semantics=("arbitrary",), vmem_limit_bytes=LIMIT
        ),
        cost_estimate=QUICK,
    )(d_ext, ffw, ffw, ffw, upper, z, z_halo, taps, left_ok, right_ok, on)


def ff_grad_kernel(spot_ref, left_ref, right_ref, out_ref):
    out_ref[0, 0] = mm_tn(left_ref[...], right_ref[0]).astype(out_ref.dtype)


def ff_grad(spot, left, right, which, away, dtype):
    n_tok = left.shape[0]
    count = 1

    def lanes(k, r, spot_ref):
        return (which, 0, (spot_ref[1] + away) % 2 * 2 + (spot_ref[0] + r) % 2)

    return pl.pallas_call(
        ff_grad_kernel,
        grid_spec=pltpu.PrefetchScalarGridSpec(
            num_scalar_prefetch=1,
            grid=(count, 2),
            in_specs=[
                pl.BlockSpec((n_tok, D), lambda k, r, spot_ref: (0, 0)),
                pl.BlockSpec((1, n_tok, FFB), lanes),
            ],
            out_specs=pl.BlockSpec((1, 1, D, FFB), lambda k, r, spot_ref: (k, r, 0, 0)),
        ),
        out_shape=jax.ShapeDtypeStruct((count, 2, D, FFB), dtype),
        compiler_params=pltpu.CompilerParams(
            dimension_semantics=("arbitrary", "arbitrary"), vmem_limit_bytes=LIMIT
        ),
        cost_estimate=QUICK,
    )(spot, left, right)


def unit_grad_kernel(pairs, away, spot_ref, *refs):
    out_ref = refs[-1]
    unit = (spot_ref[0] + pl.program_id(0)) % 2 * 2 + (spot_ref[1] + away) % 2
    step = D // 3
    for number, (left, right) in enumerate(pairs):

        @pl.when(unit == number)
        def _():
            for i in range(3):
                rows = pl.ds(i * step, step)
                value = mm_tn(refs[left][:, rows], refs[right][...]).astype(out_ref.dtype)
                height = out_ref.shape[2]
                for block in range(i * step // height, -(-(i + 1) * step // height)):
                    low, high = max(block * height, i * step), min((block + 1) * height, (i + 1) * step)
                    out_ref[0, block, low - block * height : high - block * height] = value[
                        low - i * step : high - i * step
                    ]


def unit_grad(spot, arrays, pairs, away, dtype, blocks):
    n_tok = arrays[0].shape[0]
    return pl.pallas_call(
        partial(unit_grad_kernel, pairs, away),
        grid_spec=pltpu.PrefetchScalarGridSpec(
            num_scalar_prefetch=1,
            grid=(2,),
            in_specs=[pl.BlockSpec(a.shape, lambda r, spot_ref: (0, 0)) for a in arrays],
            out_specs=pl.BlockSpec((1, blocks, D // blocks, D), lambda r, spot_ref: (r, 0, 0, 0)),
        ),
        out_shape=jax.ShapeDtypeStruct((2, blocks, D // blocks, D), dtype),
        compiler_params=pltpu.CompilerParams(
            dimension_semantics=("arbitrary",), vmem_limit_bytes=LIMIT
        ),
        cost_estimate=QUICK,
    )(spot, *arrays)


class Course:
    def __init__(self, flow):
        shape = flow.keep.shape
        self.block = shape[-2:]
        self.count = math.prod(shape[:-2])
        self.sends = flow.sends.reshape((self.count,) + self.block)
        self.keep = flow.keep.reshape((self.count,) + self.block)
        self.first = flow.mask
        self.stages = [
            (kind, math.prod(shape[axis + 1 : -2]), mask) for kind, axis, mask in flow.stages
        ]

    def sizes(self):
        return [self.count >> i for i in range(len(self.stages) + 1)]


def finish_kernel(n_mp, courses, top, sum_masks, gather_masks, *refs):
    count = len(courses)
    dp, mp = lax.axis_index("dp"), lax.axis_index("mp")

    def bit(mask):
        return mp // mask % 2 if mask < n_mp else dp // (mask // n_mp) % 2

    def partner(mask):
        if mask < n_mp:
            return {"mp": mp + mask * (1 - 2 * bit(mask))}
        return {"dp": dp + mask // n_mp * (1 - 2 * bit(mask))}

    sends, keeps = refs[:count], refs[count : 2 * count]
    part_ref, mine_ref, scalar_ref, soon_ref = refs[2 * count : 2 * count + 4]
    join_ref, cap_ref, sum_ref, all_ref, total_ref, soon_out = refs[2 * count + 4 : 2 * count + 10]
    scratch = list(refs[2 * count + 10 :])
    soon_sem = scratch.pop()
    soon_got = scratch.pop()
    (
        send_sem, recv_sem, sum_send, sum_recv, all_send, all_recv, one_send, one_recv,
        join_send, join_recv
    ) = scratch[-10:]
    sum_got, sum_buf, owns, cap_owns, one_got, one_buf, join_buf = scratch[-17:-10]
    merges = [
        (owns, owns.at[3], scratch[-21], scratch[-20]),
        (cap_owns, cap_ref, scratch[-19], scratch[-18]),
    ]
    outs = [owns.at[0], owns.at[1], cap_owns.at[0], cap_owns.at[1], owns.at[2]]
    accs, gots, packs = [], [], []
    for course in courses:
        accs.append(scratch.pop(0))
        gots.append([scratch.pop(0) for _ in course.sizes()])
        packs.append([None] + [scratch.pop(0) for _ in course.sizes()[1:]])

    def across():
        return {"mp": mp + 1 - 2 * bit(1) + 2 * (1 - 2 * bit(2))}

    barrier = pltpu.get_barrier_semaphore()
    for target in [partner(mask) for mask in sum_masks] + [across()]:
        pl.semaphore_signal(
            barrier, inc=1, device_id=target, device_id_type=pl.DeviceIdType.MESH
        )
    pl.semaphore_wait(barrier, len(sum_masks) + 1)

    def copy(f, stage):
        course = courses[f]
        mask = course.first if stage == 0 else course.stages[stage - 1][2]
        return pltpu.make_async_remote_copy(
            src_ref=sends[f] if stage == 0 else packs[f][stage],
            dst_ref=gots[f][stage],
            send_sem=send_sem.at[f, stage],
            recv_sem=recv_sem.at[f, stage],
            device_id=partner(mask),
            device_id_type=pl.DeviceIdType.MESH,
        )

    def each_rows(rows, act):
        if rows % 16:
            act(slice(None))
        else:

            @pl.loop(0, rows // 16)
            def _(i):
                act(pl.ds(pl.multiple_of(i * 16, 16), 16))

    def spots(strides, at):
        found = [(at, 0)]
        for stride in strides:
            found = [
                (block + value * stride, slot * 2 + value)
                for block, slot in found for value in (0, 1)
            ]
        return found

    def absorb(f, stage, fixed, strides):
        course = courses[f]
        base = keeps[f] if stage == 0 else accs[f]
        got = gots[f][stage]
        rows = course.block[0]
        if stage == len(course.stages):

            def close(at):
                outs[f][at, :] = base[fixed, at, :] + wide(got[0, at, :])

            each_rows(rows, close)
            return None
        kind, cut, mask = course.stages[stage]
        own = bit(mask) if kind == "abs" else 0
        other = 1 - own
        place_of = strides.index(cut)
        weight = 1 << (len(strides) - 1 - place_of)
        rest = [stride for stride in strides if stride != cut]

        for number, (block, slot) in enumerate(spots(rest, fixed)):
            low = slot % weight
            slot = (slot // weight) * 2 * weight + low

            def act(at, block=block, slot=slot, number=number):
                packs[f][stage + 1][number, at, :] = bf(
                    base[block + other * cut, at, :] + wide(got[slot + other * weight, at, :])
                )

            each_rows(rows, act)
        copy(f, stage + 1).start()
        for number, (block, slot) in enumerate(spots(rest, fixed)):
            low = slot % weight
            slot = (slot // weight) * 2 * weight + low

            def act(at, block=block, slot=slot):
                accs[f][block + own * cut, at, :] = (
                    base[block + own * cut, at, :] + wide(got[slot + own * weight, at, :])
                )

            each_rows(rows, act)
        return fixed + own * cut, rest

    def sum_copy(stage):
        return pltpu.make_async_remote_copy(
            src_ref=part_ref if stage == 0 else sum_buf.at[stage - 1],
            dst_ref=sum_got.at[stage],
            send_sem=sum_send.at[stage],
            recv_sem=sum_recv.at[stage],
            device_id=partner(sum_masks[stage]),
            device_id_type=pl.DeviceIdType.MESH,
        )

    def all_copy(stage):
        held = canvas // (1 << stage) * (1 << stage)
        return pltpu.make_async_remote_copy(
            src_ref=mine_ref if stage == 0 else all_ref.at[pl.ds(held, 1 << stage)],
            dst_ref=all_ref.at[pl.ds(held, 1 << stage)],
            send_sem=all_send.at[stage],
            recv_sem=all_recv.at[stage],
            device_id=partner(gather_masks[stage]),
            device_id_type=pl.DeviceIdType.MESH,
        )

    def merge_copy(pair):
        return pltpu.make_async_remote_copy(
            src_ref=merges[pair][2],
            dst_ref=merges[pair][3],
            send_sem=send_sem.at[2 * pair, merge_at[pair] + 1],
            recv_sem=recv_sem.at[2 * pair, merge_at[pair] + 1],
            device_id=partner(top),
            device_id_type=pl.DeviceIdType.MESH,
        )

    def one_copy(stage):
        return pltpu.make_async_remote_copy(
            src_ref=one_buf.at[stage],
            dst_ref=one_got.at[stage],
            send_sem=one_send.at[stage],
            recv_sem=one_recv.at[stage],
            device_id=partner(sum_masks[stage]),
            device_id_type=pl.DeviceIdType.MESH,
        )

    def join_copy(number):
        return pltpu.make_async_remote_copy(
            src_ref=join_buf.at[number],
            dst_ref=join_ref.at[mp],
            send_sem=join_send.at[number],
            recv_sem=join_recv.at[number],
            device_id=across() if number == 2 else partner(number + 1),
            device_id_type=pl.DeviceIdType.MESH,
        )

    def lanes_of(number):
        cols = D // 4

        def cut(ref):
            value = ref[:, :cols]
            for m in range(1, 4):
                value = jnp.where(number == m, ref[:, m * cols : (m + 1) * cols], value)
            return value

        return cut

    def soon_copy():
        return pltpu.make_async_remote_copy(
            src_ref=soon_ref,
            dst_ref=soon_got,
            send_sem=soon_sem.at[0],
            recv_sem=soon_sem.at[1],
            device_id=partner(top),
            device_id_type=pl.DeviceIdType.MESH,
        )

    merge_at = [len(courses[0].stages), len(courses[2].stages)]
    canvas = dp * 2 + mp // 2
    soon_copy().start()
    sum_copy(0).start()
    all_copy(0).start()
    state = []
    turns = (0, 1, 4, 2, 3)
    join_turn = max(merge_at[0] + 1, len(courses[4].stages))
    lag = (0, 0, 1, 1, 0)
    for f, course in enumerate(courses):
        if not lag[f]:
            copy(f, 0).start()
        strides = [course.count >> (i + 1) for i in range(course.count.bit_length() - 1)]
        state.append((0, strides))
    all_ref[pl.ds(canvas, 1)] = mine_ref[...]
    high = bit(top) == 1
    for turn in range(max(len(sum_masks), *[len(course.stages) + 3 for course in courses])):
        for f in turns:
            stage = turn - lag[f]
            if stage == -1:
                copy(f, 0).start()
            elif stage <= len(courses[f].stages):
                copy(f, stage).wait_recv()
                state[f] = absorb(f, stage, *state[f])
            if f % 2 == 1 and stage == merge_at[f // 2]:
                both, _, pack, _ = merges[f // 2]
                pack[...] = bf(jnp.where(high, both[0], both[1]))
                merge_copy(f // 2).start()
        for pair, (both, own, pack, came) in enumerate(merges):
            if turn == merge_at[pair] + lag[2 * pair] + 1:
                merge_copy(pair).wait_recv()
                own[...] = jnp.where(high, both[1], both[0]) + wide(came[...])
        if turn == 1:
            soon_copy().wait_recv()
            soon_out[...] = soon_ref[...] + soon_got[...]
        if turn == join_turn:
            b0, b1 = bit(1), bit(2)
            for number, (f0, f1) in enumerate(((1, 0), (0, 1), (1, 1))):
                other = b0 + f0 * (1 - 2 * b0) + 2 * (b1 + f1 * (1 - 2 * b1))
                cut = lanes_of(other)
                join_buf[number, 0] = cut(owns.at[3])
                join_buf[number, 1] = cut(owns.at[2])
                join_copy(number).start()
            cut = lanes_of(mp)
            join_ref[mp, 0] = cut(owns.at[3])
            join_ref[mp, 1] = cut(owns.at[2])
        if turn < len(sum_masks):
            sum_copy(turn).wait_recv()
            total = (part_ref[...] if turn == 0 else sum_buf[turn - 1]) + sum_got[turn]
            if turn + 1 < len(sum_masks):
                sum_buf[turn] = total
                sum_copy(turn + 1).start()
            else:
                sum_ref[...] = total
        if turn < len(gather_masks):
            all_copy(turn).wait_recv()
            if turn + 1 < len(gather_masks):
                all_copy(turn + 1).start()
    square = jnp.sum(owns[2] * owns[2]) + jnp.sum(owns[3] * owns[3])
    square = square + jnp.sum(cap_ref[...] * cap_ref[...])
    row = lax.broadcasted_iota(jnp.int32, (8, 128), 0)
    one_buf[0] = scalar_ref[...] + jnp.where(row == 0, square, 0.0)
    one_copy(0).start()
    for stage in range(len(sum_masks)):
        one_copy(stage).wait_recv()
        total = one_buf[stage] + one_got[stage]
        if stage + 1 < len(sum_masks):
            one_buf[stage + 1] = total
            one_copy(stage + 1).start()
        else:
            total_ref[...] = total
    for number in range(3):
        join_copy(number).wait_recv()
        join_copy(number).wait_send()
    for stage in range(len(sum_masks)):
        one_copy(stage).wait_send()
        sum_copy(stage).wait_send()
    for stage in range(len(gather_masks)):
        all_copy(stage).wait_send()
    soon_copy().wait_send()
    for pair in range(2):
        merge_copy(pair).wait_send()
    for f, course in enumerate(courses):
        for stage in range(len(course.stages) + 1):
            copy(f, stage).wait_send()


def finish(n_mp, flows, top, masks, part, mine, scalars, soon):
    budget = 3000
    height = lambda flow: flow.keep.size // D // flow.keep.shape[-2] * (-(-flow.keep.shape[-2] // 16) * 16)
    while sum(height(flow) for flow in flows) > budget:
        flow = max(flows, key=height)
        flow.launch()
        flow.land()
    courses = [Course(flow) for flow in flows]
    canvases = 1 << len(masks) - 1
    scratch = []
    for course in courses:
        scratch.append(pltpu.VMEM((course.count,) + course.block, F32))
        scratch += [pltpu.VMEM((size,) + course.block, BF16) for size in course.sizes()]
        scratch += [pltpu.VMEM((size,) + course.block, BF16) for size in course.sizes()[1:]]
    most = max(len(course.stages) for course in courses) + 2
    late = courses[0].block
    for block in (late, courses[2].block):
        scratch += [pltpu.VMEM(block, BF16), pltpu.VMEM(block, BF16)]
    scratch += [
        pltpu.VMEM((len(masks),) + part.shape, F32),
        pltpu.VMEM((len(masks) - 1,) + part.shape, F32),
        pltpu.VMEM((4,) + late, F32),
        pltpu.VMEM((2,) + courses[2].block, F32),
        pltpu.VMEM((len(masks), 8, 128), F32),
        pltpu.VMEM((len(masks), 8, 128), F32),
        pltpu.VMEM((3, 2, late[0], D // 4), F32),
    ]
    scratch += [pltpu.SemaphoreType.DMA((len(courses), most))] * 2
    scratch += [pltpu.SemaphoreType.DMA((len(masks),))] * 6
    scratch += [pltpu.SemaphoreType.DMA((3,))] * 2
    scratch += [pltpu.VMEM(soon.shape, F32), pltpu.SemaphoreType.DMA((2,))]
    plan = [
        Plan(course.count, course.block, course.first, tuple(course.stages)) for course in courses
    ]
    vmem = pl.BlockSpec(memory_space=pltpu.VMEM)
    outs = [(4, 2, late[0], D // 4), courses[2].block, part.shape]
    outs += [(canvases,) + mine.shape[1:], (8, 128), soon.shape]
    return pl.pallas_call(
        partial(finish_kernel, n_mp, plan, top, masks, masks[1:]),
        in_specs=[pl.BlockSpec(memory_space=pl.ANY)] * len(courses) + [vmem] * (len(courses) + 4),
        out_specs=[vmem] * len(outs),
        out_shape=[jax.ShapeDtypeStruct(shape, F32) for shape in outs],
        scratch_shapes=scratch,
        compiler_params=pltpu.CompilerParams(
            collective_id=0, has_side_effects=True, vmem_limit_bytes=58 * 1024 * 1024
        ),
    )(*[course.sends for course in courses], *[course.keep for course in courses], part, mine, scalars, soon)


class Plan:
    def __init__(self, count, block, first, stages):
        self.count, self.block, self.first, self.stages = count, block, first, stages

    def sizes(self):
        return [self.count >> i for i in range(len(self.stages) + 1)]


def cap_grad_kernel(away, spot_ref, cap_ref, act_ref, dcap_ref, draw_ref, out_ref):
    block = pl.program_id(0) * 2 + (spot_ref[1] + away) % 2
    first, both = cap_ref.shape[1] // GL, (cap_ref.shape[1] + act_ref.shape[1]) // GL

    @pl.when(block < first)
    def _():
        rows = pl.ds(pl.multiple_of(block * GL, GL), GL)
        out_ref[0] = mm_tn(cap_ref[:, rows], dcap_ref[...]).astype(out_ref.dtype)

    @pl.when((block >= first) & (block < both))
    def _():
        rows = pl.ds(pl.multiple_of((block - first) * GL, GL), GL)
        out_ref[0] = mm_tn(act_ref[:, rows], draw_ref[...]).astype(out_ref.dtype)

    @pl.when(block >= both)
    def _():
        out_ref[0] = jnp.zeros((GL, D), out_ref.dtype)


def cap_grad(spot, arrays, blocks, away, dtype):
    return pl.pallas_call(
        partial(cap_grad_kernel, away),
        grid_spec=pltpu.PrefetchScalarGridSpec(
            num_scalar_prefetch=1,
            grid=(blocks // 2,),
            in_specs=[pl.BlockSpec(a.shape, lambda j, spot_ref: (0, 0)) for a in arrays],
            out_specs=pl.BlockSpec((1, GL, D), lambda j, spot_ref: (j, 0, 0)),
        ),
        out_shape=jax.ShapeDtypeStruct((blocks // 2, GL, D), dtype),
        compiler_params=pltpu.CompilerParams(
            dimension_semantics=("arbitrary",), vmem_limit_bytes=LIMIT
        ),
        cost_estimate=QUICK,
    )(spot, *arrays)


WIN = 256
QROWS = 512
BROWS = 256


def head_window(h):
    start = jnp.minimum(h * XHEAD // 128 * 128, D - WIN)
    lane = lax.broadcasted_iota(jnp.int32, (1, WIN), 1)
    mask = (lane >= h * XHEAD - start) & (lane < h * XHEAD - start + XHEAD)
    return pl.ds(pl.multiple_of(start, 128), WIN), mask


def cross_probs(q, keys, token_seg, text_seg):
    scores = mm_nt(q, keys) * XHEAD ** (-0.5)
    scores = jnp.where(token_seg == text_seg, scores, MASKED)
    top = jnp.max(scores, axis=-1, keepdims=True)
    probs = jnp.exp(scores - top)
    return probs * (1.0 / jnp.sum(probs, axis=-1, keepdims=True))


def cross_forward_kernel(q_ref, k_ref, v_ref, tok_ref, txt_ref, out_ref):
    win, mask = head_window(pl.program_id(0))
    keys, values = k_ref[:, win], v_ref[:, win]

    @pl.loop(0, q_ref.shape[0] // QROWS)
    def _(i):
        at = pl.ds(pl.multiple_of(i * QROWS, QROWS), QROWS)
        q = jnp.where(mask, q_ref[at, win], jnp.zeros((), BF16))
        probs = bf(cross_probs(q, keys, tok_ref[at, 0:1], txt_ref[...]))
        out_ref[at, win] = jnp.where(mask, bf(mm(probs, values)), out_ref[at, win])


def cross_forward(q, keys, values, token_seg, text_seg):
    n_tok = q.shape[0]
    n_txt = keys.shape[0]
    return pl.pallas_call(
        cross_forward_kernel,
        grid=(XHEADS,),
        in_specs=[
            whole_spec((n_tok, D)), whole_spec((n_txt, D)), whole_spec((n_txt, D)),
            whole_spec((n_tok, 1)), whole_spec((1, n_txt)),
        ],
        out_specs=whole_spec((n_tok, D)),
        out_shape=jax.ShapeDtypeStruct((n_tok, D), BF16),
        compiler_params=pltpu.CompilerParams(
            dimension_semantics=("arbitrary",), vmem_limit_bytes=LIMIT
        ),
        cost_estimate=QUICK,
    )(q, keys, values, token_seg, text_seg)


def cross_backward_kernel(
    q_ref, k_ref, v_ref, dc_ref, tok_ref, txt_ref, dq_ref, dk_ref, dv_ref, dk_acc, dv_acc
):
    win, mask = head_window(pl.program_id(0))
    keys, values = k_ref[:, win], v_ref[:, win]
    scale = XHEAD ** (-0.5)
    none = jnp.zeros((), BF16)
    dk_acc[...] = jnp.zeros_like(dk_acc)
    dv_acc[...] = jnp.zeros_like(dv_acc)

    @pl.loop(0, q_ref.shape[0] // BROWS)
    def _(i):
        at = pl.ds(pl.multiple_of(i * BROWS, BROWS), BROWS)
        q = jnp.where(mask, q_ref[at, win], none)
        dc = jnp.where(mask, dc_ref[at, win], none)
        probs = cross_probs(q, keys, tok_ref[at, 0:1], txt_ref[...])
        d_probs = mm_nt(dc, values)
        along = jnp.sum(probs * d_probs, axis=-1, keepdims=True)
        d_scores = bf(probs * (d_probs - along))
        dq_ref[at, win] = jnp.where(mask, bf(mm(d_scores, keys) * scale), dq_ref[at, win])
        dk_acc[...] += mm_tn(d_scores, q)
        dv_acc[...] += mm_tn(bf(probs), dc)

    dk_ref[:, win] = jnp.where(mask, dk_acc[...] * scale, dk_ref[:, win])
    dv_ref[:, win] = jnp.where(mask, dv_acc[...], dv_ref[:, win])


def cross_backward(q, keys, values, d_cross, token_seg, text_seg):
    n_tok = q.shape[0]
    n_txt = keys.shape[0]
    return pl.pallas_call(
        cross_backward_kernel,
        grid=(XHEADS,),
        in_specs=[
            whole_spec((n_tok, D)), whole_spec((n_txt, D)), whole_spec((n_txt, D)),
            whole_spec((n_tok, D)), whole_spec((n_tok, 1)), whole_spec((1, n_txt)),
        ],
        out_specs=[whole_spec((n_tok, D)), whole_spec((n_txt, D)), whole_spec((n_txt, D))],
        out_shape=[
            jax.ShapeDtypeStruct((n_tok, D), BF16),
            jax.ShapeDtypeStruct((n_txt, D), F32),
            jax.ShapeDtypeStruct((n_txt, D), F32),
        ],
        scratch_shapes=[pltpu.VMEM((n_txt, WIN), F32), pltpu.VMEM((n_txt, WIN), F32)],
        compiler_params=pltpu.CompilerParams(
            dimension_semantics=("arbitrary",), vmem_limit_bytes=LIMIT
        ),
        cost_estimate=QUICK,
    )(q, keys, values, d_cross, token_seg, text_seg)


GL = 128
GROUPS = D // GL


def parts(value):
    high = bf(value)
    return high, bf(value - wide(high))


def group_heads():
    row = lax.broadcasted_iota(jnp.int32, (GL, GL), 0) // HEAD
    col = lax.broadcasted_iota(jnp.int32, (GL, GL), 1) // HEAD
    return wide(row == col)


def both_segments(value, second):
    value = wide(value)
    late = value * second
    return bf(value - late), bf(late)


def state_kernel(k_ref, v_ref, sec_ref, kv_ref, ks_ref):
    same = group_heads()
    k0, k1 = both_segments(k_ref[...], sec_ref[...])
    kv_ref[0, 0] = mm_tn(k0, v_ref[...]) * same
    kv_ref[0, 1] = mm_tn(k1, v_ref[...]) * same
    ks_ref[0, 0] = jnp.broadcast_to(jnp.sum(wide(k0), axis=0, keepdims=True), (8, GL))
    ks_ref[0, 1] = jnp.broadcast_to(jnp.sum(wide(k1), axis=0, keepdims=True), (8, GL))


def attend(q_ref, sec_ref, kv_ref, ks_ref, same):
    q0, q1 = both_segments(q_ref[...], sec_ref[...])
    numer = 0.0
    denom = 1.0
    for i, q in enumerate((q0, q1)):
        for part in parts(kv_ref[0, i]):
            numer = numer + mm(q, part)
        sums = jnp.transpose(jnp.broadcast_to(ks_ref[0, i, 0:1], (GL, GL))) * same
        for part in parts(sums):
            denom = denom + mm(q, part)
    return q0, q1, numer, denom


def attend_kernel(q_ref, sec_ref, kv_ref, ks_ref, out_ref):
    _, _, numer, denom = attend(q_ref, sec_ref, kv_ref, ks_ref, group_heads())
    out_ref[...] = bf(numer / denom)


def attend_back_kernel(q_ref, da_ref, sec_ref, kv_ref, ks_ref, dq_ref, dkv_ref, dks_ref):
    same = group_heads()
    second = sec_ref[...]
    q0, q1, numer, denom = attend(q_ref, sec_ref, kv_ref, ks_ref, same)
    inverse = 1.0 / denom
    d_num = da_ref[...] * inverse
    high, low = parts(d_num * numer)
    ones = bf(same)
    d_den = -(mm(high, ones) + mm(low, ones)) * inverse
    d_parts = parts(d_num)
    back = []
    for i, q in enumerate((q0, q1)):
        total = 0.0
        grad = 0.0
        for part in d_parts:
            total = total + mm_tn(q, part)
        for part in parts(kv_ref[0, i]):
            for left in d_parts:
                grad = grad + mm_nt(left, part)
        dkv_ref[0, i] = total * same
        dks_ref[0, i] = jnp.broadcast_to(
            jnp.sum(wide(q) * d_den, axis=0, keepdims=True), (8, GL)
        )
        back.append(grad + d_den * ks_ref[0, i, 0:1])
    dq = jnp.where(second > 0, back[1], back[0])
    dq_ref[...] = bf(jnp.where(wide(q_ref[...]) > 0, dq, 0.0))


def state_back_kernel(k_ref, v_ref, sec_ref, dkv_ref, dks_ref, dk_ref, dv_ref):
    second = sec_ref[...] > 0
    k, v = k_ref[...], v_ref[...]
    dk, dv = [], []
    for i in range(2):
        grad_k = dks_ref[0, i, 0:1]
        grad_v = 0.0
        for part in parts(dkv_ref[0, i]):
            grad_k = grad_k + mm_nt(v, part)
            grad_v = grad_v + mm(k, part)
        dk.append(grad_k)
        dv.append(grad_v)
    dk_ref[...] = bf(jnp.where(wide(k) > 0, jnp.where(second, dk[1], dk[0]), 0.0))
    dv_ref[...] = bf(jnp.where(wide(v) > 0, jnp.where(second, dv[1], dv[0]), 0.0))


def by_group(kernel, n_tok, ins, outs, out_types):
    specs = dict(
        tok=pl.BlockSpec((n_tok, GL), lambda g: (0, g)),
        seg=whole_spec((n_tok, GL)),
        kv=pl.BlockSpec((1, 2, GL, GL), lambda g: (g, 0, 0, 0)),
        ks=pl.BlockSpec((1, 2, 8, GL), lambda g: (g, 0, 0, 0)),
    )
    shapes = dict(tok=(n_tok, D), kv=(GROUPS, 2, GL, GL), ks=(GROUPS, 2, 8, GL))
    return pl.pallas_call(
        kernel,
        grid=(GROUPS,),
        in_specs=[specs[i] for i in ins],
        out_specs=[specs[o] for o in outs],
        out_shape=[jax.ShapeDtypeStruct(shapes[o], t) for o, t in zip(outs, out_types)],
        compiler_params=pltpu.CompilerParams(
            dimension_semantics=("arbitrary",), vmem_limit_bytes=LIMIT
        ),
        cost_estimate=QUICK,
    )


def update(weight, grad, moment, average, factor, rate):
    clipped = factor * grad
    moment_new = MOMENTUM * moment + clipped
    weight_new = weight - rate * (clipped + MOMENTUM * moment_new)
    average_new = average + AVERAGE_RATE * (weight_new - average)
    return (weight_new, moment_new, average_new)


def local(
    n_dp, n_mp,
    latents, noise, captions, res_ids, timesteps, caption_lengths,
    in_proj, out_proj, w_up, w_down, cond, conv, tables,
    mom_in, mom_out, mom_up, mom_down, mom_cond, mom_conv, mom_tables,
    avg_in, avg_out, avg_up, avg_down, avg_cond, avg_conv, avg_tables,
):
    place = Place(n_dp, n_mp)
    y, c = place.y, place.c
    half_dp = n_dp // 2
    dl = D // n_dp
    spot = jnp.stack([y, c]).astype(jnp.int32)
    owner_rows = cond.shape[0]

    cond_b = bf(cond)
    units_b = unit_split(place, as_units(bf(in_proj), bf(out_proj)))
    cap_chunk = chunk_of(place, CAP_ROWS, GL if place.n <= 32 else 16)
    cap_mine = spread_rows(place, cond_b, TIME_ROWS, CAP_ROWS)
    packed = jnp.concatenate([units_b.reshape(-1, D), cap_mine], axis=0)
    ff_b = jnp.stack([bf(w_up[:, 0]), bf(w_up[:, 1]), bf(w_down).T])
    ff_b = jnp.pad(ff_b, ((0, 0), (0, 0), (0, FFB - ff_b.shape[2])))
    packed, ff_b, cond_time = lax.optimization_barrier((packed, ff_b, cond_b))
    got = lax.all_gather(packed, AXES, axis=0)
    by_place = got.reshape((n_dp, 2, 2) + packed.shape)
    w_q, w_k, w_v, w_o0, w_xq, w_o1, w_xk, w_xv = [
        by_place[:, i, j, part * dl : (part + 1) * dl].reshape(D, D)
        for part in (0, 1) for i in (0, 1) for j in (0, 1)
    ]
    cap_w = got[:, 2 * dl :].reshape(-1, D)
    w_cap1, w_cap2 = cap_w[:CAPD], cap_w[CAPD:CAP_ROWS]
    ffw = lax.all_gather(ff_b.reshape(3 * dl, FFB), AXES, axis=0)
    if dl % 16 == 0:
        ffw = ffw.reshape(n_dp, 4, 3 * dl, FFB)
    else:
        ffw = ffw.reshape(n_dp, 2, 2, 3, dl, FFB).transpose(3, 0, 4, 2, 1, 5)
        ffw = ffw.reshape(1, 1, 3 * D, FFP)

    spread_time = spread_rows(place, cond_time, 0, TIME_ROWS)
    w_time = gather_rows_all(place, spread_time, (place.x_mask, 2, 1))[:TIME_ROWS]
    facts = jnp.concatenate([timesteps, res_ids[:, None]], axis=1)
    for b in range(place.dp_bits):
        mask = n_mp << b
        facts = ordered(place.bit(mask), facts, place.swap(facts, mask), 0)
    steps_all = facts[:, :4].reshape(-1)
    count = jnp.sum(jnp.where(facts[:, 4] == 0, 4.0, 1.0))
    slots = steps_all.shape[0]

    resolution = lax.dynamic_index_in_dim(res_ids, y, 0, False)
    lengths = lax.dynamic_index_in_dim(caption_lengths, y, 0, False)
    steps_t = lax.dynamic_index_in_dim(timesteps, y, 0, False)
    pair = jnp.stack([latents, noise])
    quarters = jnp.stack([pair] + [place.swap(pair, mask) for mask in (1, 2, 3)])
    parts = [lax.dynamic_index_in_dim(quarters, (2 * c + j) ^ place.mp, 0, False) for j in (0, 1)]
    tokens = jnp.concatenate(
        [lax.dynamic_index_in_dim(part, y, 1, False) for part in parts], axis=1
    )
    n_tok = tokens.shape[1]
    rows = n_tok // SIDE
    grid = tokens.reshape(2, rows, SIDE, CIN)
    tokens = jnp.where(c == 1, grid[:, ::-1], grid).reshape(2, n_tok, CIN)
    clean, noisy = wide(tokens[0]), wide(tokens[1])
    col = jnp.arange(n_tok, dtype=jnp.int32)[:, None] % SIDE
    second = (col >= SIDE // 2) & (resolution == 0)
    seg0 = jnp.where(resolution == 0, 2 * c, 0)
    seg1 = jnp.where(resolution == 0, 2 * c + 1, 0)
    token_seg = jnp.where(second, seg1, seg0)

    def pick(table):
        first = lax.dynamic_index_in_dim(table, seg0, 0, True)
        other = lax.dynamic_index_in_dim(table, seg1, 0, True)
        return jnp.where(second, other, first)

    def by_segment(value):
        late = jnp.sum(jnp.where(second, value, 0.0), axis=0)
        early = jnp.sum(jnp.where(second, 0.0, value), axis=0)
        slot = jnp.arange(4, dtype=jnp.int32)[:, None]
        table = jnp.where(slot == seg0, early, 0.0) + jnp.where(slot == seg1, late, 0.0)
        return table, early + late

    sigma = pick(wide(steps_t)[:, None] / TMAX)
    mixed_in = (1.0 - sigma) * clean + sigma * noisy
    target = noisy - clean
    image_tokens = jnp.where(resolution == 0, (SIDE // 2) ** 2, SIDE * SIDE).astype(F32)
    loss_weight = 1.0 / (CIN * image_tokens * count)

    freq_b = bf(time_embed(steps_all))
    time_hidden = mm(freq_b, w_time[:FREQ])
    hidden_b = bf(jax.nn.silu(time_hidden))
    time_emb = mm(hidden_b, w_time[FREQ:])
    silu_b = bf(jax.nn.silu(time_emb))
    mod_mine = mm_nt(silu_b, cond_b).reshape(n_dp, 2, 1, 4 * owner_rows)
    mod_send = jnp.broadcast_to(mod_mine, (n_dp, 2, 2, 4 * owner_rows))
    mod_got = lax.all_to_all(mod_send.reshape(place.n, 4 * owner_rows), AXES, 0, 0)
    time_mod = mod_got.reshape(place.n, 4, owner_rows).transpose(1, 0, 2).reshape(4, -1)
    time_mod = time_mod[:, BLOCK_AT:].reshape(4, 6, D)
    mod_table = tables[None, :6] + time_mod
    mods = [pick(mod_table[:, k]) for k in range(6)]
    canvas = place.dp * 2 + y
    emb_mine = lax.dynamic_slice_in_dim(time_emb, canvas * 4, 4, 0)
    emb_tok = pick(emb_mine)

    own_cap = lax.dynamic_index_in_dim(captions, y, 0, False)
    their_cap = lax.dynamic_index_in_dim(captions, 1 - y, 0, False)
    caption = jnp.concatenate([own_cap, place.swap(their_cap, 2)], axis=0)
    quarter = own_cap.shape[0]
    within = jnp.arange(quarter, dtype=jnp.int32)
    text_at = jnp.concatenate([(place.mp ^ m) * quarter + within for m in (0, 2, 1, 3)])
    ends = jnp.cumsum(lengths)
    text_segment = jnp.sum((text_at[:, None] >= ends[None, :]).astype(jnp.int32), axis=1)
    cap_hidden = mm(caption, w_cap1)
    cap_act, gelu_pull = jax.vjp(partial(jax.nn.gelu, approximate=True), cap_hidden)
    cap_act_b = bf(cap_act)
    text_raw = mm(cap_act_b, w_cap2)
    gain = tables[8]
    text_inv = lax.rsqrt(jnp.mean(text_raw * text_raw, -1, keepdims=True) + EPS)
    text_hat = text_raw * text_inv
    text_b = bf(text_hat * gain)
    text_k = bf(mm(text_b, w_xk))
    text_v = bf(mm(text_b, w_xv))
    keys = jnp.concatenate([text_k, place.swap(text_k, 1)], axis=0)
    values = jnp.concatenate([text_v, place.swap(text_v, 1)], axis=0)

    embed = mm(mixed_in, tables[9 : 9 + CIN], HIGH)
    hat_a, inv_a = layer_norm(embed)
    normed_a = bf(hat_a * (1.0 + mods[1]) + mods[0])
    q = bf(jax.nn.relu(mm(normed_a, w_q)))
    k = bf(jax.nn.relu(mm(normed_a, w_k)))
    v = bf(jax.nn.relu(mm(normed_a, w_v)))
    whole_image = wide(resolution == 1)
    second_wide = jnp.broadcast_to(wide(second), (n_tok, GL))

    def shared(state, sums):
        first = jnp.concatenate([state[:, 0], sums[:, 0]], axis=1)
        first = first + whole_image * place.swap(first, 1)
        state = jnp.stack([first[:, :GL], state[:, 1]], axis=1)
        return state, jnp.stack([first[:, GL:], sums[:, 1]], axis=1)

    group_call = partial(by_group, n_tok=n_tok)
    state, key_sum = group_call(
        state_kernel, ins=("tok", "tok", "seg"), outs=("kv", "ks"), out_types=(F32, F32)
    )(k, v, second_wide)
    state, key_sum = shared(state, key_sum)
    (attn_b,) = group_call(
        attend_kernel, ins=("tok", "seg", "kv", "ks"), outs=("tok",), out_types=(BF16,)
    )(q, second_wide, state, key_sum)
    branch_a = mm_nt(attn_b, w_o0)
    state_a = embed + mods[2] * branch_a

    state_b = bf(state_a)
    xq = bf(mm(state_b, w_xq))
    cross_b = cross_forward(xq, keys, values, token_seg, text_segment[None, :])
    state_c = state_a + mm_nt(cross_b, w_o1)

    hat_f, inv_f = layer_norm(state_c)
    normed_f = bf(hat_f * (1.0 + mods[4]) + mods[3])
    taps = to_ff(conv)
    flipped = jnp.concatenate([taps[:, 6:9], taps[:, 3:6], taps[:, 0:3], taps[:, 9:]], axis=1)
    taps = jnp.where(c == 1, flipped, taps)
    column = jnp.arange(SIDE, dtype=jnp.int32)[:, None]
    middle = SIDE // 2
    left_ok = (column != 0) & ((resolution == 1) | (column != middle))
    right_ok = (column != SIDE - 1) & ((resolution == 1) | (column != middle - 1))
    left_ok = jnp.broadcast_to(wide(left_ok), (SIDE, CB))
    right_ok = jnp.broadcast_to(wide(right_ok), (SIDE, CB))
    halo_on = whole_image.reshape(1, 1)
    edge = n_tok - SIDE
    x_ext = jnp.concatenate([normed_f, place.swap(normed_f[edge:], 1)], axis=0)
    upper, z, gated_b, branch_f = ffn_forward(
        x_ext, ffw, taps, left_ok, right_ok, halo_on
    )
    z_halo = place.swap(z[:, edge:], 1)
    state_f = state_c + mods[5] * branch_f

    hat_o, inv_o = layer_norm(state_f)
    shift_o = tables[6] + emb_tok
    scale_o = tables[7] + emb_tok
    final = hat_o * (1.0 + scale_o) + shift_o
    out_rows = tables[9 + CIN :]
    output = mm_nt(final, out_rows, HIGH)
    error = output - target
    loss = jnp.sum(error * error) * loss_weight

    d_output = 2.0 * loss_weight * error
    d_final = mm(d_output, out_rows, HIGH)
    d_out_rows = mm_tn(d_output, final, HIGH)
    d_shift_seg, d_shift_o = by_segment(d_final)
    d_scale_seg, d_scale_o = by_segment(d_final * hat_o)
    d_emb_mine = d_shift_seg + d_scale_seg
    d_emb = d_emb_mine + place.swap(d_emb_mine, 1)
    d_state_f = layer_norm_back(d_final * (1.0 + scale_o), hat_o, inv_o)

    split_dp = (2,) * place.dp_bits
    far = [(b, n_mp << (place.dp_bits - 1 - b)) for b in range(place.dp_bits - 2, -1, -1)]

    def stages(lead, order):
        table = {
            "x": ("abs", lead + place.dp_bits - 1, place.x_mask),
            "y": ("rel", lead - 1, 2),
        }
        rest = [("abs", lead + axis, mask) for axis, mask in far]
        return [table[o] if o in table else rest.pop(0) for o in order] + rest

    def ff_flow(left, right, orders):
        shape = (1, 2) + split_dp + (dl, FFB)
        flows = []
        for i, order in enumerate(orders):
            away = ff_grad(spot, left, right, i, 1, BF16)
            flows.append(Flow(place, away.reshape(shape), stages(2, order)))
            left, right, away = lax.optimization_barrier((left, right, away))
        for i, flow in enumerate(flows):
            flow.keep = ff_grad(spot, left, right, i, 0, BF16).reshape(shape)
        return flows

    def unit_flow(arrays, pairs, order):
        shape = (2,) + split_dp + (dl, D)
        blocks = n_dp if dl % 16 == 0 else 1
        away = unit_grad(spot, arrays, pairs, 1, BF16, blocks)
        flow = Flow(place, away.reshape(shape), stages(1, order))
        arrays, away = lax.optimization_barrier((arrays, away))
        flow.keep = unit_grad(spot, arrays, pairs, 0, BF16, blocks).reshape(shape)
        return flow

    def settle(value, flows):
        value, keeps = lax.optimization_barrier((value, [flow.keep for flow in flows]))
        for flow, keep in zip(flows, keeps):
            flow.keep = keep
        return tick(value, flows)

    d_branch_f = bf(mods[5] * d_state_f)
    d_edge = place.swap(d_branch_f[edge:], 1)
    flow_dn, = ff_flow(d_branch_f, gated_b[None], ["yx"])
    d_ext = jnp.concatenate([d_branch_f, d_edge], axis=0)
    d_ext = settle(d_ext, [flow_dn])
    d_upper, d_taps, d_normed_f = tick(
        ffn_backward(d_ext, ffw, upper, z, z_halo, taps, left_ok, right_ok, halo_on), [flow_dn]
    )
    unflipped = jnp.concatenate(
        [d_taps[:, 6:9], d_taps[:, 3:6], d_taps[:, 0:3], d_taps[:, 9:]], axis=1
    )
    conv_grad = from_ff(jnp.where(c == 1, unflipped, d_taps))
    flow_up = ff_flow(normed_f, d_upper, ["xy", "yx"])
    ffn_flows = [flow_dn] + flow_up
    soon = jnp.concatenate([conv_grad.reshape(-1, D), d_out_rows], axis=0)
    soon_masks = [1, 2] + [n_mp << b for b in range(place.dp_bits)]
    soon_sent = place.swap(soon, soon_masks[0])
    d_normed_f, soon_sent = settle((d_normed_f, soon_sent), flow_up)
    soon = soon + soon_sent
    d_state_c = d_state_f + layer_norm_back(d_normed_f * (1.0 + mods[4]), hat_f, inv_f)
    d_mods = [None] * 6
    d_mods[5] = by_segment(d_state_f * branch_f)
    d_mods[3] = by_segment(d_normed_f)
    d_mods[4] = by_segment(d_normed_f * hat_f)

    d_branch_c = bf(d_state_c)
    d_cross = bf(mm(d_branch_c, w_o1))
    soon_sent = place.swap(soon, soon_masks[1])
    (d_xq_b, d_keys, d_values), soon_sent = tick(
        (
            cross_backward(xq, keys, values, d_cross, token_seg, text_segment[None, :]),
            soon_sent,
        ),
        ffn_flows,
    )
    soon = soon + soon_sent
    half_txt = TXT // 2
    d_kv = jnp.stack([d_keys, d_values])
    d_kv = d_kv[:, :half_txt] + place.swap(d_kv[:, half_txt:], 1)
    d_kv_b = bf(d_kv)
    early = unit_flow(
        [state_b, d_xq_b, d_branch_c, cross_b, text_b, d_kv_b[0], d_kv_b[1]],
        ((0, 1), (2, 3), (4, 5), (4, 6)),
        "yzx",
    )
    d_state_a = d_state_c + mm_nt(d_xq_b, w_xq)
    soon_sent = place.swap(soon, soon_masks[2])
    d_state_a, d_kv_b, soon_sent = settle((d_state_a, d_kv_b, soon_sent), [early])
    soon = soon + soon_sent

    d_branch_a = bf(mods[2] * d_state_a)
    d_mods[2] = by_segment(d_state_a * branch_a)
    d_attn = mm(d_branch_a, w_o0)
    soon_sent = place.swap(soon, soon_masks[3])
    (dq_b, d_state, d_sum), soon_sent = tick(
        (group_call(
            attend_back_kernel,
            ins=("tok", "tok", "seg", "kv", "ks"),
            outs=("tok", "kv", "ks"),
            out_types=(BF16, F32, F32),
        )(q, d_attn, second_wide, state, key_sum), soon_sent),
        ffn_flows,
    )
    soon = soon + soon_sent
    d_state, d_sum = shared(d_state, d_sum)
    dk_b, dv_b = group_call(
        state_back_kernel,
        ins=("tok", "tok", "seg", "kv", "ks"),
        outs=("tok", "tok"),
        out_types=(BF16, BF16),
    )(k, v, second_wide, d_state, d_sum)
    d_normed_a = mm_nt(dq_b, w_q) + mm_nt(dk_b, w_k) + mm_nt(dv_b, w_v)
    d_mods[0] = by_segment(d_normed_a)
    d_mods[1] = by_segment(d_normed_a * hat_a)

    d_mod = jnp.stack([table for table, _ in d_mods], axis=1).reshape(4, 6 * D)
    d_mod = jnp.pad(d_mod, ((0, 0), (BLOCK_AT, 0)))
    d_mod = d_mod.reshape(4, place.n, owner_rows).transpose(1, 0, 2)
    d_mod, dq_b, dk_b, dv_b = lax.optimization_barrier((d_mod, dq_b, dk_b, dv_b))
    d_mod = lax.all_to_all(d_mod, AXES, 0, 0)
    late = unit_flow(
        [normed_a, dq_b, dk_b, dv_b, d_branch_a, attn_b],
        ((0, 1), (0, 2), (0, 3), (4, 5)),
        "xy",
    )
    d_embed = d_state_a + layer_norm_back(d_normed_a * (1.0 + mods[1]), hat_a, inv_a)
    g_patch = mm_tn(mixed_in, d_embed, HIGH)
    d_mod, d_kv_b, g_patch, late.keep, late.moving = lax.optimization_barrier(
        (d_mod, d_kv_b, g_patch, late.keep, late.moving)
    )
    near_far = [stage for stage in stages(1, "") if stage[1] != 1]
    late_flows = late.split(
        1, [stages(1, order)[:2] + near_far for order in ("xy", "yx")]
    )
    d_mod, d_kv_b = tick((d_mod, d_kv_b), ffn_flows)
    for flow in late_flows:
        flow.land()
    d_mod = d_mod.reshape(slots // 4, 2, 4, owner_rows).sum(1).reshape(slots, owner_rows)
    d_silu = mm(d_mod, wide(cond_b), HIGH)
    g_block = mm_tn(d_mod, wide(silu_b), HIGH)

    d_text = mm_nt(d_kv_b[0], w_xk) + mm_nt(d_kv_b[1], w_xv)
    d_gain = jnp.sum(d_text * text_hat, axis=0)
    d_hat = d_text * gain
    d_text_raw = text_inv * (d_hat - text_hat * jnp.mean(d_hat * text_hat, -1, keepdims=True))
    d_text_raw_b = bf(d_text_raw)
    d_cap_b = bf(gelu_pull(mm_nt(d_text_raw_b, w_cap2))[0])
    cap_shape = split_dp + (2, 1, cap_chunk, D)
    if cap_chunk == GL:
        cap_parts = [caption, cap_act_b, d_cap_b, d_text_raw_b]
        cap_sends = cap_grad(spot, cap_parts, place.n, 1, BF16).reshape(cap_shape)
        cap_keep = partial(cap_grad, spot, cap_parts, place.n, 0, BF16)
    else:
        g_cap = jnp.concatenate(
            [
                mm_tn(caption, d_cap_b),
                mm_tn(cap_act_b, d_text_raw_b),
                jnp.zeros((place.n * cap_chunk - CAP_ROWS, D), F32),
            ],
            axis=0,
        ).reshape(split_dp + (2, 2, cap_chunk, D))
        cap_sends = bf(lax.dynamic_slice_in_dim(g_cap, 1 - c, 1, place.dp_bits + 1))
        cap_keep = partial(lax.dynamic_slice_in_dim, g_cap, c, 1, place.dp_bits + 1)

    for mask in soon_masks[4:-1]:
        soon = soon + place.swap(soon, mask)
    soon_rows = soon.shape[0]
    soon = jnp.pad(soon, ((0, -soon_rows % 8), (0, 0)))

    d_rows_six = jnp.stack([total for _, total in d_mods])
    tables_grad = jnp.concatenate(
        [d_rows_six, d_shift_o[None], d_scale_o[None], d_gain[None], g_patch], axis=0
    )
    masks = [1, 2] + [n_mp << b for b in range(place.dp_bits)]
    d_silu = jnp.broadcast_to(d_silu.reshape(n_dp, 2, 1, 4 * D), (n_dp, 2, 2, 4 * D))
    d_silu = lax.all_to_all(d_silu.reshape(place.n, 4 * D), AXES, 0, 0).sum(0).reshape(4, D)
    cap_flow = Flow(
        place,
        cap_sends,
        [("abs", place.dp_bits, 2), ("abs", place.dp_bits - 1, place.x_mask)]
        + [("abs",) + pair_ for pair_ in far],
    )
    cap_flow.keep = cap_keep().reshape(cap_shape)
    d_time = d_silu * silu_grad(emb_mine) + d_emb
    d_hidden = mm_nt(d_time, wide(w_time[FREQ:]), HIGH)
    hidden_mine = lax.dynamic_slice_in_dim(time_hidden, canvas * 4, 4, 0)
    d_times = jnp.concatenate([d_time, d_hidden * silu_grad(hidden_mine)], axis=0)
    cap_far = [stage for stage in [("abs",) + pair_ for pair_ in far] if stage[1] != 0]
    cap_y, cap_x = ("abs", place.dp_bits, 2), ("abs", place.dp_bits - 1, place.x_mask)
    cap_flows = cap_flow.split(0, [[cap_y, cap_x] + cap_far, cap_far[:1] + [cap_y, cap_x] + cap_far[1:]])
    last = late_flows + cap_flows + [early]
    for flow in cap_flows:
        flow.land()
    d_times, early.moving = lax.optimization_barrier((d_times, early.moving))
    early.land()
    ff_own = [flow.drain().reshape(dl, FFB)[:, : FF // 4] for flow in ffn_flows]
    part_sq = sum(jnp.sum(grad * grad) for grad in [g_block] + ff_own)
    row = lax.broadcasted_iota(jnp.int32, (8, 128), 0)
    scalars = jnp.where(row == 0, part_sq, loss)
    small = jnp.pad(tables_grad, ((0, -tables_grad.shape[0] % 8), (0, 0)))
    top = n_mp << place.dp_bits - 1
    joined, cap_own, small, d_times, scalars, soon = finish(
        n_mp, last, top, masks, small, d_times[None], scalars, soon
    )
    conv_grad = soon[: conv_grad.size // D].reshape(conv_grad.shape)
    d_out_rows = soon[conv_grad.size // D : soon_rows]
    tables_grad = jnp.concatenate([small[: tables_grad.shape[0]], d_out_rows], axis=0)
    d_times = d_times.reshape(-1, 2, 4, D).transpose(1, 0, 2, 3).reshape(2, slots, D)
    g_time2 = mm_tn(wide(hidden_b), d_times[0], HIGH)
    g_time1 = mm_tn(wide(freq_b), d_times[1], HIGH)
    spots = -(-TIME_ROWS // owner_rows)
    g_time = jnp.concatenate(
        [g_time1, g_time2, jnp.zeros(((spots + 1) * owner_rows - TIME_ROWS, D), F32)], axis=0
    )
    g_time = lax.dynamic_slice_in_dim(
        g_time, jnp.minimum(place.me, spots) * owner_rows, owner_rows, 0
    )

    cap_own = cap_own.reshape(cap_chunk, D)
    g_cap = collect_rows(place, cap_own, owner_rows, TIME_ROWS, CAP_ROWS)
    g_cond = g_cap + g_block + g_time
    g_in, g_out = from_units(joined.transpose(1, 0, 2, 3).reshape(8, dl, D // 4))
    g_upper = jnp.stack(ff_own[1:], axis=1)
    g_lower = ff_own[0].T
    owned = (g_in, g_out, g_upper, g_lower, g_cond)

    squares, loss = scalars[0, 0], scalars[1, 0]
    squares = squares + jnp.sum(g_time1 * g_time1) + jnp.sum(g_time2 * g_time2)
    norm = jnp.sqrt(squares + jnp.sum(conv_grad * conv_grad) + jnp.sum(tables_grad * tables_grad))
    factor = CLIP / jnp.maximum(norm, CLIP)
    rate = STEP_SCALE * math.sqrt(PARAMS) / CLIP
    grads = owned + (conv_grad, tables_grad)
    weights = (in_proj, out_proj, w_up, w_down, cond, conv, tables)
    moments = (mom_in, mom_out, mom_up, mom_down, mom_cond, mom_conv, mom_tables)
    averages = (avg_in, avg_out, avg_up, avg_down, avg_cond, avg_conv, avg_tables)
    new = [
        update(weights[i], grads[i], moments[i], averages[i], factor, rate) for i in range(7)
    ]
    moments_out = [new[i][1] for i in range(5)] + [factor * conv_grad, new[6][1]]
    return (loss, norm, *[n[0] for n in new], *moments_out, *[n[2] for n in new])


def solution(mesh):
    tokens = P("dp", "mp", None)
    weights = (
        P("dp", None, "mp"),
        P(None, "mp", "dp"),
        P("dp", None, "mp"),
        P("mp", "dp"),
        P(("dp", "mp"), None),
        P(),
        P(),
    )
    in_specs = (tokens, tokens, tokens, P("dp"), P("dp", None), P("dp", None)) + weights * 3
    out_specs = (P(), P()) + weights * 3
    body = partial(local, mesh.shape["dp"], mesh.shape["mp"])
    return jax.shard_map(body, mesh=mesh, in_specs=in_specs, out_specs=out_specs, check_vma=False)
```

```python
from functools import partial
import math

import jax
import jax.numpy as jnp
from jax import lax
from jax.experimental import pallas as pl
from jax.experimental.pallas import tpu as pltpu
from jax.sharding import PartitionSpec as P

D = 1152
FF = 2880
CAPD = 2304
CIN = 32
FREQ = 256
SIDE = 32
TXT = 512
HEAD = 32
XHEAD = 72
XHEADS = 16
PARAMS = 34277760
FFB = 768
FFP = 4 * FFB
TIME_ROWS = FREQ + D
CAP_ROWS = CAPD + D
BLOCK_AT = TIME_ROWS + CAP_ROWS

HIGH = lax.Precision.HIGHEST
EPS = 1e-06
CLIP = 0.001
MOMENTUM = 0.9
AVERAGE_RATE = 0.1
STEP_SCALE = 0.01
TMAX = 1000.0
MASKED = -1e30
AXES = ("dp", "mp")
F32 = jnp.float32
BF16 = jnp.bfloat16


def bf(value):
    return value.astype(BF16)


def wide(value):
    return value.astype(F32)


def dot(left, right, dims, precision=None):
    return lax.dot_general(
        left, right, (dims, ((), ())), precision=precision, preferred_element_type=F32
    )


def mm(left, right, precision=None):
    return dot(left, right, ((1,), (0,)), precision)


def mm_nt(left, right, precision=None):
    return dot(left, right, ((1,), (1,)), precision)


def mm_tn(left, right, precision=None):
    return dot(left, right, ((0,), (0,)), precision)


class Place:
    def __init__(self, n_dp, n_mp):
        self.n_dp, self.n_mp, self.n = n_dp, n_mp, n_dp * n_mp
        self.dp, self.mp = lax.axis_index("dp"), lax.axis_index("mp")
        self.me = self.dp * n_mp + self.mp
        self.y, self.c = self.mp // 2, self.mp % 2
        self.dp_bits = int(math.log2(n_dp))

    def bit(self, mask):
        return (self.me // mask) % 2

    def swap(self, value, mask):
        return lax.ppermute(value, AXES, [(i, i ^ mask) for i in range(self.n)])

    @property
    def far_masks(self):
        return [self.n_mp << b for b in range(1, self.dp_bits)]

    @property
    def x_mask(self):
        return self.n_mp


def ordered(bit, mine, theirs, axis):
    low = jnp.where(bit == 0, mine, theirs)
    high = jnp.where(bit == 0, theirs, mine)
    return jnp.concatenate([low, high], axis=axis)


def gather_far(place, block, axis):
    block = jnp.expand_dims(block, axis)
    for mask in place.far_masks:
        block = ordered(place.bit(mask), block, place.swap(block, mask), axis)
    return block


def gather_near(place, block, order):
    held = {0: block}
    for mask in order:
        held.update({key | mask: place.swap(value, mask) for key, value in held.items()})
    return held


def near_bits(place, key):
    flip = [1 if key & mask else 0 for mask in (place.x_mask, 2, 1)]
    own = (place.bit(place.x_mask), place.y, place.c)
    return [jnp.where(f == 1, 1 - o, o) for f, o in zip(flip, own)]


def gather_rows_all(place, block, order):
    rows, cols = block.shape
    held = gather_near(place, gather_far(place, block, 0), order)
    half = place.n_dp // 2
    out = jnp.zeros((half, 2, 2, 2, rows, cols), block.dtype)
    for key, value in held.items():
        x, y, c = near_bits(place, key)
        out = lax.dynamic_update_slice(out, value[:, None, None, None], (0, x, y, c, 0, 0))
    return out.reshape(place.n * rows, cols)


def spread_table(place, owner_rows, low, chunk):
    rounds = -(-owner_rows // chunk) + 1
    tables = []
    for step in range(rounds):
        pairs = []
        for owner in range(place.n):
            target = (owner_rows * owner - low) // chunk + step
            start = low + chunk * target - owner_rows * owner
            if 0 <= target < place.n and -chunk < start < owner_rows:
                pairs.append((owner, target))
        tables.append(pairs)
    return tables


def chunk_of(place, rows, unit=16):
    chunk = -(-rows // place.n)
    return -(-chunk // unit) * unit


def spread_rows(place, held, low, rows):
    owner_rows = held.shape[0]
    chunk = chunk_of(place, rows)
    padded = jnp.pad(held, ((chunk, chunk), (0, 0)))
    first = (owner_rows * place.me - low) // chunk
    total = None
    for step, pairs in enumerate(spread_table(place, owner_rows, low, chunk)):
        start = low + chunk * (first + step) - owner_rows * place.me + chunk
        piece = lax.dynamic_slice_in_dim(padded, start, chunk, 0)
        got = lax.ppermute(piece, AXES, pairs)
        total = got if total is None else total + got
    return total


def collect_rows(place, block, owner_rows, low, rows):
    chunk = block.shape[0]
    first = (owner_rows * place.me - low) // chunk
    got = [
        wide(lax.ppermute(bf(block), AXES, [(target, owner) for owner, target in pairs]))
        for pairs in spread_table(place, owner_rows, low, chunk)
    ]
    start = owner_rows * place.me - low - chunk * first
    mine = lax.dynamic_slice_in_dim(jnp.concatenate(got, axis=0), start, owner_rows, 0)
    row = owner_rows * place.me + jnp.arange(owner_rows, dtype=jnp.int32)[:, None]
    return jnp.where((row >= low) & (row < low + rows), mine, 0.0)


def halve(place, grad, stages):
    for axis, mask in stages:
        bit = place.bit(mask)
        half = grad.shape[axis] // 2
        away = lax.dynamic_slice_in_dim(grad, (1 - bit) * half, half, axis)
        keep = lax.dynamic_slice_in_dim(grad, bit * half, half, axis)
        grad = keep + wide(place.swap(bf(away), mask))
    return grad


def layer_norm(value):
    centred = value - jnp.mean(value, -1, keepdims=True)
    inverse = lax.rsqrt(jnp.mean(centred * centred, -1, keepdims=True) + EPS)
    return centred * inverse, inverse


def layer_norm_back(grad, normed, inverse):
    along = jnp.mean(grad * normed, -1, keepdims=True)
    return inverse * (grad - jnp.mean(grad, -1, keepdims=True) - normed * along)


def silu_grad(value):
    gate = jax.nn.sigmoid(value)
    return gate * (1.0 + value * (1.0 - gate))


def time_embed(steps_t):
    half_size = FREQ // 2
    freqs = jnp.exp(-math.log(10000.0) * jnp.arange(half_size, dtype=F32) / half_size)
    angles = wide(steps_t)[:, None] * freqs[None, :]
    return jnp.concatenate([jnp.cos(angles), jnp.sin(angles)], axis=1)


def to_ff(value):
    blocks = value.reshape(value.shape[:-1] + (4, FF // 4))
    pad = [(0, 0)] * (blocks.ndim - 1) + [(0, FFB - FF // 4)]
    blocks = jnp.pad(blocks, pad)
    blocks = jnp.stack([blocks[..., m, :] for m in (0, 2, 1, 3)], axis=-2)
    return blocks.reshape(value.shape[:-1] + (FFP,))


def from_ff(value):
    blocks = value.reshape(value.shape[:-1] + (4, FFB))[..., : FF // 4]
    blocks = jnp.stack([blocks[..., m, :] for m in (0, 2, 1, 3)], axis=-2)
    return blocks.reshape(value.shape[:-1] + (FF,))


def unit_split(place, units):
    units = units.reshape((2, 4) + units.shape[1:])

    def part(number):
        return lax.dynamic_index_in_dim(units, number, 1, False)

    got = [part(place.mp)] + [place.swap(part(place.mp ^ m), m) for m in (1, 2, 3)]
    stacked = jnp.stack(got)
    return jnp.concatenate(
        [lax.dynamic_index_in_dim(stacked, place.mp ^ m, 0, False) for m in range(4)], axis=-1
    )


def unit_join(place, block):
    cols = D // 4

    def part(number):
        return lax.dynamic_slice_in_dim(block, number * cols, cols, 2)

    got = [part(place.mp)] + [place.swap(part(place.mp ^ m), m) for m in (1, 2, 3)]
    stacked = jnp.stack(got)
    order = [lax.dynamic_index_in_dim(stacked, place.mp ^ m, 0, False) for m in range(4)]
    return jnp.stack(order, axis=1).reshape((8,) + order[0].shape[1:])


def as_units(in_w, out_w):
    inp = [in_w[:, k] for k in range(6)]
    outp = [out_w[j].T for j in range(2)]
    return jnp.stack([inp[0], inp[1], inp[2], outp[0], inp[3], outp[1], inp[4], inp[5]])


def from_units(units):
    g_in = jnp.stack([units[u] for u in (0, 1, 2, 4, 6, 7)], axis=1)
    g_out = jnp.stack([units[3].T, units[5].T])
    return g_in, g_out


class Flow:
    def __init__(self, place, sends, stages):
        self.place, self.stages = place, list(stages)
        self.keep = None
        self.moving = place.swap(sends, 1)
        self.sends = None

    def launch(self):
        self.moving = self.place.swap(self.sends, self.mask)
        self.sends = None

    def part(self, take):
        return wide(take(self.keep)) + wide(take(self.moving))

    def land(self):
        if not self.stages:
            self.keep = self.part(lambda value: value)
            self.moving = None
            return
        kind, axis, self.mask = self.stages.pop(0)
        if kind == "rel":
            away = self.part(lambda value: lax.slice_in_dim(value, 1, 2, axis=axis))
            keep = self.part(lambda value: lax.slice_in_dim(value, 0, 1, axis=axis))
        else:
            bit = self.place.bit(self.mask)
            away = self.part(lambda value: lax.dynamic_slice_in_dim(value, 1 - bit, 1, axis))
            keep = self.part(lambda value: lax.dynamic_slice_in_dim(value, bit, 1, axis))
        self.sends, self.keep, self.moving = bf(away), keep, None

    def split(self, axis, orders):
        flows = []
        for i, order in enumerate(orders):
            flow = Flow.__new__(Flow)
            flow.place, flow.stages, flow.sends = self.place, list(order), None
            flow.keep = lax.slice_in_dim(self.keep, i, i + 1, axis=axis)
            flow.moving = lax.slice_in_dim(self.moving, i, i + 1, axis=axis)
            flows.append(flow)
        return flows

    def drain(self):
        while self.moving is not None:
            self.land()
            if self.sends is not None:
                self.launch()
        return self.keep


def tick(value, flows):
    moving = [flow for flow in flows if flow.moving is not None]
    value, landed = lax.optimization_barrier((value, [flow.moving for flow in moving]))
    for flow, arrived in zip(moving, landed):
        flow.moving = arrived
        flow.land()
    ready = [flow for flow in moving if flow.sends is not None]
    value, sends = lax.optimization_barrier((value, [flow.sends for flow in ready]))
    for flow, out in zip(ready, sends):
        flow.sends = out
        flow.launch()
    return value


CB = 256
ROW = SIDE
LIMIT = 48 * 1024 * 1024
QUICK = pl.CostEstimate(flops=2**20, bytes_accessed=2**16, transcendentals=0)


def whole_spec(shape):
    return pl.BlockSpec(shape, lambda *_: (0,) * len(shape))


def ffn_forward_kernel(
    x_ref, w0_ref, w1_ref, wd_ref, taps_ref, left_ref, right_ref, on_ref,
    u_ref, z_ref, g_ref, out_ref, act, act_l, act_r
):
    rows = g_ref.shape[0] // ROW
    zero = jnp.zeros((ROW, CB), F32)
    x = x_ref[...]
    u_ref[0] = mm(x, w0_ref[...].reshape(D, CB))
    u_ref[1] = mm(x, w1_ref[...].reshape(D, CB))
    on = on_ref[0, 0]
    for k in range(2):
        for ref in (act, act_l, act_r):
            ref[k, pl.ds(0, ROW)] = zero

    def fill(r, scale):
        for k in range(2):
            u = u_ref[k, pl.ds(pl.multiple_of(r * ROW, ROW), ROW)]
            a = u * jax.nn.sigmoid(u) * scale
            at = pl.ds(pl.multiple_of(r * ROW + ROW, ROW), ROW)
            act[k, at] = a
            act_l[k, at] = pltpu.roll(a, 1, 0) * left_ref[...]
            act_r[k, at] = pltpu.roll(a, ROW - 1, 0) * right_ref[...]

    @pl.loop(0, rows, unroll=2)
    def _(r):
        fill(r, 1.0)

    fill(rows, on)

    @pl.loop(0, rows, unroll=2)
    def _(r):
        z = []
        for k in range(2):
            total = jnp.broadcast_to(taps_ref[k, pl.ds(9, 1)], (ROW, CB))
            for dr in range(3):
                at = pl.ds(pl.multiple_of(r * ROW + dr * ROW, ROW), ROW)
                for dc, ref in enumerate((act_l, act, act_r)):
                    total = total + ref[k, at] * taps_ref[k, pl.ds(dr * 3 + dc, 1)]
            z_ref[k, pl.ds(pl.multiple_of(r * ROW, ROW), ROW)] = total
            z.append(total)
        gated = z[0] * (z[1] * jax.nn.sigmoid(z[1]))
        g_ref[pl.ds(pl.multiple_of(r * ROW, ROW), ROW)] = bf(gated)

    part = mm_nt(g_ref[...], wd_ref[...].reshape(D, CB))

    @pl.when(pl.program_id(0) == 0)
    def _():
        out_ref[...] = part

    @pl.when(pl.program_id(0) > 0)
    def _():
        out_ref[...] += part


def ff_spec(ffw, k):
    groups, blocks, rows, lanes = ffw.shape
    per = lanes // CB

    def index(j):
        at = j // per
        return (0, at % 2 * 2 + at // 2 if blocks == 4 else 0, k, j % per)

    return pl.BlockSpec((groups, 1, rows // 3, CB), index)


def ffn_forward(x_ext, ffw, taps, left_ok, right_ok, on):
    n_ext = x_ext.shape[0]
    n_tok = n_ext - ROW
    weight = partial(ff_spec, ffw)
    pads = pltpu.VMEM((2, n_ext + ROW, CB), F32)
    return pl.pallas_call(
        ffn_forward_kernel,
        grid=(FFP // CB,),
        in_specs=[
            whole_spec((n_ext, D)), weight(0), weight(1), weight(2),
            pl.BlockSpec((2, 10, CB), lambda j: (0, 0, j)),
            whole_spec((ROW, CB)), whole_spec((ROW, CB)),
            pl.BlockSpec((1, 1), lambda j: (0, 0), memory_space=pltpu.SMEM),
        ],
        out_specs=[
            pl.BlockSpec((2, n_ext, CB), lambda j: (0, 0, j)),
            pl.BlockSpec((2, n_tok, CB), lambda j: (0, 0, j)),
            pl.BlockSpec((n_tok, CB), lambda j: (0, j)),
            whole_spec((n_tok, D)),
        ],
        out_shape=[
            jax.ShapeDtypeStruct((2, n_ext, FFP), F32),
            jax.ShapeDtypeStruct((2, n_tok, FFP), F32),
            jax.ShapeDtypeStruct((n_tok, FFP), BF16),
            jax.ShapeDtypeStruct((n_tok, D), F32),
        ],
        scratch_shapes=[pads, pads, pads],
        compiler_params=pltpu.CompilerParams(
            dimension_semantics=("arbitrary",), vmem_limit_bytes=LIMIT
        ),
        cost_estimate=QUICK,
    )(x_ext, ffw, ffw, ffw, taps, left_ok, right_ok, on)


def ffn_backward_kernel(
    d_ref, wd_ref, w0_ref, w1_ref, u_ref, z_ref, zh_ref, taps_ref, left_ref, right_ref, on_ref,
    du_ref, dt_ref, dn_ref, dg_buf, dz, dz_l, dz_r, acc
):
    n_tok = z_ref.shape[1]
    rows = n_tok // ROW
    zero = jnp.zeros((ROW, CB), F32)
    dg_buf[...] = mm(d_ref[...], wd_ref[...].reshape(D, CB))
    for k in range(2):
        for ref in (dz, dz_l, dz_r):
            ref[k, pl.ds(0, ROW)] = zero
    acc[...] = jnp.zeros_like(acc)

    def fill(r, z0, z1, scale, count):
        dg = dg_buf[pl.ds(pl.multiple_of(r * ROW, ROW), ROW)]
        gate = jax.nn.sigmoid(z1)
        soft = z1 * gate
        at = pl.ds(pl.multiple_of(r * ROW + ROW, ROW), ROW)
        d_both = (dg * soft, dg * z0 * (gate + soft * (1.0 - gate)))
        for k in range(2):
            value = d_both[k] * scale
            dz[k, at] = value
            dz_l[k, at] = pltpu.roll(value * left_ref[...], ROW - 1, 0)
            dz_r[k, at] = pltpu.roll(value * right_ref[...], 1, 0)
            if count:
                acc[k, 9] += fold(value)

    def fold(value):
        return value[0:8] + value[8:16] + value[16:24] + value[24:32]

    @pl.loop(0, rows, unroll=2)
    def _(r):
        at = pl.ds(pl.multiple_of(r * ROW, ROW), ROW)
        fill(r, z_ref[0, at], z_ref[1, at], 1.0, True)

    fill(rows, zh_ref[0], zh_ref[1], on_ref[0, 0], False)

    def back(r, taps_on):
        at = pl.ds(pl.multiple_of(r * ROW, ROW), ROW)
        for k in range(2):
            u = u_ref[k, at]
            gate = jax.nn.sigmoid(u)
            a = u * gate
            total = zero
            for dr in range(3):
                near = pl.ds(pl.multiple_of(r * ROW + (2 - dr) * ROW, ROW), ROW)
                for dc, ref in enumerate((dz_l, dz, dz_r)):
                    value = ref[k, near]
                    total = total + value * taps_ref[k, pl.ds(dr * 3 + dc, 1)]
                    if dr in taps_on:
                        acc[k, dr * 3 + dc] += fold(value * a)
            du_ref[k, at] = bf(total * (gate + a * (1.0 - gate)))

    @pl.loop(0, rows - 1, unroll=3)
    def _(r):
        back(r, (0, 1, 2))

    back(rows - 1, (1, 2))
    for k in range(2):
        u = u_ref[k, pl.ds(n_tok, ROW)]
        a = u * jax.nn.sigmoid(u) * on_ref[0, 0]
        for dc, ref in enumerate((dz_l, dz, dz_r)):
            acc[k, 6 + dc] += fold(ref[k, pl.ds(n_tok, ROW)] * a)
        for t in range(10):
            dt_ref[k, pl.ds(t, 1)] = jnp.sum(acc[k, t], axis=0, keepdims=True)

    part = mm_nt(du_ref[0], w0_ref[...].reshape(D, CB))
    part = part + mm_nt(du_ref[1], w1_ref[...].reshape(D, CB))

    @pl.when(pl.program_id(0) == 0)
    def _():
        dn_ref[...] = part

    @pl.when(pl.program_id(0) > 0)
    def _():
        dn_ref[...] += part


def ffn_backward(d_ext, ffw, upper, z, z_halo, taps, left_ok, right_ok, on):
    n_ext = d_ext.shape[0]
    n_tok = n_ext - ROW
    pads = pltpu.VMEM((2, n_ext + ROW, CB), F32)
    return pl.pallas_call(
        ffn_backward_kernel,
        grid=(FFP // CB,),
        in_specs=[
            whole_spec((n_ext, D)),
            ff_spec(ffw, 2), ff_spec(ffw, 0), ff_spec(ffw, 1),
            pl.BlockSpec((2, n_ext, CB), lambda j: (0, 0, j)),
            pl.BlockSpec((2, n_tok, CB), lambda j: (0, 0, j)),
            pl.BlockSpec((2, ROW, CB), lambda j: (0, 0, j)),
            pl.BlockSpec((2, 10, CB), lambda j: (0, 0, j)),
            whole_spec((ROW, CB)), whole_spec((ROW, CB)),
            pl.BlockSpec((1, 1), lambda j: (0, 0), memory_space=pltpu.SMEM),
        ],
        out_specs=[
            pl.BlockSpec((2, n_tok, CB), lambda j: (0, 0, j)),
            pl.BlockSpec((2, 10, CB), lambda j: (0, 0, j)),
            whole_spec((n_tok, D)),
        ],
        out_shape=[
            jax.ShapeDtypeStruct((2, n_tok, FFP), BF16),
            jax.ShapeDtypeStruct((2, 10, FFP), F32),
            jax.ShapeDtypeStruct((n_tok, D), F32),
        ],
        scratch_shapes=[
            pltpu.VMEM((n_ext, CB), F32), pads, pads, pads, pltpu.VMEM((2, 10, 8, CB), F32)
        ],
        compiler_params=pltpu.CompilerParams(
            dimension_semantics=("arbitrary",), vmem_limit_bytes=LIMIT
        ),
        cost_estimate=QUICK,
    )(d_ext, ffw, ffw, ffw, upper, z, z_halo, taps, left_ok, right_ok, on)


def ff_grad_kernel(spot_ref, left_ref, right_ref, out_ref):
    out_ref[0, 0] = mm_tn(left_ref[...], right_ref[0]).astype(out_ref.dtype)


def ff_grad(spot, left, right, which, away, dtype):
    n_tok = left.shape[0]
    count = 1

    def lanes(k, r, spot_ref):
        return (which, 0, (spot_ref[1] + away) % 2 * 2 + (spot_ref[0] + r) % 2)

    return pl.pallas_call(
        ff_grad_kernel,
        grid_spec=pltpu.PrefetchScalarGridSpec(
            num_scalar_prefetch=1,
            grid=(count, 2),
            in_specs=[
                pl.BlockSpec((n_tok, D), lambda k, r, spot_ref: (0, 0)),
                pl.BlockSpec((1, n_tok, FFB), lanes),
            ],
            out_specs=pl.BlockSpec((1, 1, D, FFB), lambda k, r, spot_ref: (k, r, 0, 0)),
        ),
        out_shape=jax.ShapeDtypeStruct((count, 2, D, FFB), dtype),
        compiler_params=pltpu.CompilerParams(
            dimension_semantics=("arbitrary", "arbitrary"), vmem_limit_bytes=LIMIT
        ),
        cost_estimate=QUICK,
    )(spot, left, right)


def unit_grad_kernel(pairs, away, spot_ref, *refs):
    out_ref = refs[-1]
    unit = (spot_ref[0] + pl.program_id(0)) % 2 * 2 + (spot_ref[1] + away) % 2
    step = D // 3
    for number, (left, right) in enumerate(pairs):

        @pl.when(unit == number)
        def _():
            for i in range(3):
                rows = pl.ds(i * step, step)
                value = mm_tn(refs[left][:, rows], refs[right][...]).astype(out_ref.dtype)
                height = out_ref.shape[2]
                for block in range(i * step // height, -(-(i + 1) * step // height)):
                    low, high = max(block * height, i * step), min((block + 1) * height, (i + 1) * step)
                    out_ref[0, block, low - block * height : high - block * height] = value[
                        low - i * step : high - i * step
                    ]


def unit_grad(spot, arrays, pairs, away, dtype, blocks):
    n_tok = arrays[0].shape[0]
    return pl.pallas_call(
        partial(unit_grad_kernel, pairs, away),
        grid_spec=pltpu.PrefetchScalarGridSpec(
            num_scalar_prefetch=1,
            grid=(2,),
            in_specs=[pl.BlockSpec(a.shape, lambda r, spot_ref: (0, 0)) for a in arrays],
            out_specs=pl.BlockSpec((1, blocks, D // blocks, D), lambda r, spot_ref: (r, 0, 0, 0)),
        ),
        out_shape=jax.ShapeDtypeStruct((2, blocks, D // blocks, D), dtype),
        compiler_params=pltpu.CompilerParams(
            dimension_semantics=("arbitrary",), vmem_limit_bytes=LIMIT
        ),
        cost_estimate=QUICK,
    )(spot, *arrays)


class Course:
    def __init__(self, flow):
        shape = flow.keep.shape
        self.block = shape[-2:]
        self.count = math.prod(shape[:-2])
        self.sends = flow.sends.reshape((self.count,) + self.block)
        self.keep = flow.keep.reshape((self.count,) + self.block)
        self.first = flow.mask
        self.stages = [
            (kind, math.prod(shape[axis + 1 : -2]), mask) for kind, axis, mask in flow.stages
        ]

    def sizes(self):
        return [self.count >> i for i in range(len(self.stages) + 1)]


def finish_kernel(n_mp, courses, top, sum_masks, gather_masks, *refs):
    count = len(courses)
    dp, mp = lax.axis_index("dp"), lax.axis_index("mp")

    def bit(mask):
        return mp // mask % 2 if mask < n_mp else dp // (mask // n_mp) % 2

    def partner(mask):
        if mask < n_mp:
            return {"mp": mp + mask * (1 - 2 * bit(mask))}
        return {"dp": dp + mask // n_mp * (1 - 2 * bit(mask))}

    sends, keeps = refs[:count], refs[count : 2 * count]
    part_ref, mine_ref, scalar_ref, soon_ref = refs[2 * count : 2 * count + 4]
    join_ref, cap_ref, sum_ref, all_ref, total_ref, soon_out = refs[2 * count + 4 : 2 * count + 10]
    scratch = list(refs[2 * count + 10 :])
    soon_sem = scratch.pop()
    soon_got = scratch.pop()
    (
        send_sem, recv_sem, sum_send, sum_recv, all_send, all_recv, one_send, one_recv,
        join_send, join_recv
    ) = scratch[-10:]
    sum_got, sum_buf, owns, cap_owns, one_got, one_buf, join_buf = scratch[-17:-10]
    merges = [
        (owns, owns.at[3], scratch[-21], scratch[-20]),
        (cap_owns, cap_ref, scratch[-19], scratch[-18]),
    ]
    outs = [owns.at[0], owns.at[1], cap_owns.at[0], cap_owns.at[1], owns.at[2]]
    accs, gots, packs = [], [], []
    for course in courses:
        accs.append(scratch.pop(0))
        gots.append([scratch.pop(0) for _ in course.sizes()])
        packs.append([None] + [scratch.pop(0) for _ in course.sizes()[1:]])

    def across():
        return {"mp": mp + 1 - 2 * bit(1) + 2 * (1 - 2 * bit(2))}

    barrier = pltpu.get_barrier_semaphore()
    for target in [partner(mask) for mask in sum_masks] + [across()]:
        pl.semaphore_signal(
            barrier, inc=1, device_id=target, device_id_type=pl.DeviceIdType.MESH
        )
    pl.semaphore_wait(barrier, len(sum_masks) + 1)

    def copy(f, stage):
        course = courses[f]
        mask = course.first if stage == 0 else course.stages[stage - 1][2]
        return pltpu.make_async_remote_copy(
            src_ref=sends[f] if stage == 0 else packs[f][stage],
            dst_ref=gots[f][stage],
            send_sem=send_sem.at[f, stage],
            recv_sem=recv_sem.at[f, stage],
            device_id=partner(mask),
            device_id_type=pl.DeviceIdType.MESH,
        )

    def each_rows(rows, act):
        if rows % 16:
            act(slice(None))
        else:

            @pl.loop(0, rows // 16)
            def _(i):
                act(pl.ds(pl.multiple_of(i * 16, 16), 16))

    def spots(strides, at):
        found = [(at, 0)]
        for stride in strides:
            found = [
                (block + value * stride, slot * 2 + value)
                for block, slot in found for value in (0, 1)
            ]
        return found

    def absorb(f, stage, fixed, strides):
        course = courses[f]
        base = keeps[f] if stage == 0 else accs[f]
        got = gots[f][stage]
        rows = course.block[0]
        if stage == len(course.stages):

            def close(at):
                outs[f][at, :] = base[fixed, at, :] + wide(got[0, at, :])

            each_rows(rows, close)
            return None
        kind, cut, mask = course.stages[stage]
        own = bit(mask) if kind == "abs" else 0
        other = 1 - own
        place_of = strides.index(cut)
        weight = 1 << (len(strides) - 1 - place_of)
        rest = [stride for stride in strides if stride != cut]

        for number, (block, slot) in enumerate(spots(rest, fixed)):
            low = slot % weight
            slot = (slot // weight) * 2 * weight + low

            def act(at, block=block, slot=slot, number=number):
                packs[f][stage + 1][number, at, :] = bf(
                    base[block + other * cut, at, :] + wide(got[slot + other * weight, at, :])
                )

            each_rows(rows, act)
        copy(f, stage + 1).start()
        for number, (block, slot) in enumerate(spots(rest, fixed)):
            low = slot % weight
            slot = (slot // weight) * 2 * weight + low

            def act(at, block=block, slot=slot):
                accs[f][block + own * cut, at, :] = (
                    base[block + own * cut, at, :] + wide(got[slot + own * weight, at, :])
                )

            each_rows(rows, act)
        return fixed + own * cut, rest

    def sum_copy(stage):
        return pltpu.make_async_remote_copy(
            src_ref=part_ref if stage == 0 else sum_buf.at[stage - 1],
            dst_ref=sum_got.at[stage],
            send_sem=sum_send.at[stage],
            recv_sem=sum_recv.at[stage],
            device_id=partner(sum_masks[stage]),
            device_id_type=pl.DeviceIdType.MESH,
        )

    def all_copy(stage):
        held = canvas // (1 << stage) * (1 << stage)
        return pltpu.make_async_remote_copy(
            src_ref=mine_ref if stage == 0 else all_ref.at[pl.ds(held, 1 << stage)],
            dst_ref=all_ref.at[pl.ds(held, 1 << stage)],
            send_sem=all_send.at[stage],
            recv_sem=all_recv.at[stage],
            device_id=partner(gather_masks[stage]),
            device_id_type=pl.DeviceIdType.MESH,
        )

    def merge_copy(pair):
        return pltpu.make_async_remote_copy(
            src_ref=merges[pair][2],
            dst_ref=merges[pair][3],
            send_sem=send_sem.at[2 * pair, merge_at[pair] + 1],
            recv_sem=recv_sem.at[2 * pair, merge_at[pair] + 1],
            device_id=partner(top),
            device_id_type=pl.DeviceIdType.MESH,
        )

    def one_copy(stage):
        return pltpu.make_async_remote_copy(
            src_ref=one_buf.at[stage],
            dst_ref=one_got.at[stage],
            send_sem=one_send.at[stage],
            recv_sem=one_recv.at[stage],
            device_id=partner(sum_masks[stage]),
            device_id_type=pl.DeviceIdType.MESH,
        )

    def join_copy(number):
        return pltpu.make_async_remote_copy(
            src_ref=join_buf.at[number],
            dst_ref=join_ref.at[mp],
            send_sem=join_send.at[number],
            recv_sem=join_recv.at[number],
            device_id=across() if number == 2 else partner(number + 1),
            device_id_type=pl.DeviceIdType.MESH,
        )

    def lanes_of(number):
        cols = D // 4

        def cut(ref):
            value = ref[:, :cols]
            for m in range(1, 4):
                value = jnp.where(number == m, ref[:, m * cols : (m + 1) * cols], value)
            return value

        return cut

    def soon_copy():
        return pltpu.make_async_remote_copy(
            src_ref=soon_ref,
            dst_ref=soon_got,
            send_sem=soon_sem.at[0],
            recv_sem=soon_sem.at[1],
            device_id=partner(top),
            device_id_type=pl.DeviceIdType.MESH,
        )

    merge_at = [len(courses[0].stages), len(courses[2].stages)]
    canvas = dp * 2 + mp // 2
    soon_copy().start()
    sum_copy(0).start()
    all_copy(0).start()
    state = []
    turns = (0, 1, 4, 2, 3)
    join_turn = max(merge_at[0] + 1, len(courses[4].stages))
    lag = (0, 0, 1, 1, 0)
    for f, course in enumerate(courses):
        if not lag[f]:
            copy(f, 0).start()
        strides = [course.count >> (i + 1) for i in range(course.count.bit_length() - 1)]
        state.append((0, strides))
    all_ref[pl.ds(canvas, 1)] = mine_ref[...]
    high = bit(top) == 1
    for turn in range(max(len(sum_masks), *[len(course.stages) + 3 for course in courses])):
        for f in turns:
            stage = turn - lag[f]
            if stage == -1:
                copy(f, 0).start()
            elif stage <= len(courses[f].stages):
                copy(f, stage).wait_recv()
                state[f] = absorb(f, stage, *state[f])
            if f % 2 == 1 and stage == merge_at[f // 2]:
                both, _, pack, _ = merges[f // 2]
                pack[...] = bf(jnp.where(high, both[0], both[1]))
                merge_copy(f // 2).start()
        for pair, (both, own, pack, came) in enumerate(merges):
            if turn == merge_at[pair] + lag[2 * pair] + 1:
                merge_copy(pair).wait_recv()
                own[...] = jnp.where(high, both[1], both[0]) + wide(came[...])
        if turn == 1:
            soon_copy().wait_recv()
            soon_out[...] = soon_ref[...] + soon_got[...]
        if turn == join_turn:
            b0, b1 = bit(1), bit(2)
            for number, (f0, f1) in enumerate(((1, 0), (0, 1), (1, 1))):
                other = b0 + f0 * (1 - 2 * b0) + 2 * (b1 + f1 * (1 - 2 * b1))
                cut = lanes_of(other)
                join_buf[number, 0] = cut(owns.at[3])
                join_buf[number, 1] = cut(owns.at[2])
                join_copy(number).start()
            cut = lanes_of(mp)
            join_ref[mp, 0] = cut(owns.at[3])
            join_ref[mp, 1] = cut(owns.at[2])
        if turn < len(sum_masks):
            sum_copy(turn).wait_recv()
            total = (part_ref[...] if turn == 0 else sum_buf[turn - 1]) + sum_got[turn]
            if turn + 1 < len(sum_masks):
                sum_buf[turn] = total
                sum_copy(turn + 1).start()
            else:
                sum_ref[...] = total
        if turn < len(gather_masks):
            all_copy(turn).wait_recv()
            if turn + 1 < len(gather_masks):
                all_copy(turn + 1).start()
    square = jnp.sum(owns[2] * owns[2]) + jnp.sum(owns[3] * owns[3])
    square = square + jnp.sum(cap_ref[...] * cap_ref[...])
    row = lax.broadcasted_iota(jnp.int32, (8, 128), 0)
    one_buf[0] = scalar_ref[...] + jnp.where(row == 0, square, 0.0)
    one_copy(0).start()
    for stage in range(len(sum_masks)):
        one_copy(stage).wait_recv()
        total = one_buf[stage] + one_got[stage]
        if stage + 1 < len(sum_masks):
            one_buf[stage + 1] = total
            one_copy(stage + 1).start()
        else:
            total_ref[...] = total
    for number in range(3):
        join_copy(number).wait_recv()
        join_copy(number).wait_send()
    for stage in range(len(sum_masks)):
        one_copy(stage).wait_send()
        sum_copy(stage).wait_send()
    for stage in range(len(gather_masks)):
        all_copy(stage).wait_send()
    soon_copy().wait_send()
    for pair in range(2):
        merge_copy(pair).wait_send()
    for f, course in enumerate(courses):
        for stage in range(len(course.stages) + 1):
            copy(f, stage).wait_send()


def finish(n_mp, flows, top, masks, part, mine, scalars, soon):
    budget = 3000
    height = lambda flow: flow.keep.size // D // flow.keep.shape[-2] * (-(-flow.keep.shape[-2] // 16) * 16)
    while sum(height(flow) for flow in flows) > budget:
        flow = max(flows, key=height)
        flow.launch()
        flow.land()
    courses = [Course(flow) for flow in flows]
    canvases = 1 << len(masks) - 1
    scratch = []
    for course in courses:
        scratch.append(pltpu.VMEM((course.count,) + course.block, F32))
        scratch += [pltpu.VMEM((size,) + course.block, BF16) for size in course.sizes()]
        scratch += [pltpu.VMEM((size,) + course.block, BF16) for size in course.sizes()[1:]]
    most = max(len(course.stages) for course in courses) + 2
    late = courses[0].block
    for block in (late, courses[2].block):
        scratch += [pltpu.VMEM(block, BF16), pltpu.VMEM(block, BF16)]
    scratch += [
        pltpu.VMEM((len(masks),) + part.shape, F32),
        pltpu.VMEM((len(masks) - 1,) + part.shape, F32),
        pltpu.VMEM((4,) + late, F32),
        pltpu.VMEM((2,) + courses[2].block, F32),
        pltpu.VMEM((len(masks), 8, 128), F32),
        pltpu.VMEM((len(masks), 8, 128), F32),
        pltpu.VMEM((3, 2, late[0], D // 4), F32),
    ]
    scratch += [pltpu.SemaphoreType.DMA((len(courses), most))] * 2
    scratch += [pltpu.SemaphoreType.DMA((len(masks),))] * 6
    scratch += [pltpu.SemaphoreType.DMA((3,))] * 2
    scratch += [pltpu.VMEM(soon.shape, F32), pltpu.SemaphoreType.DMA((2,))]
    plan = [
        Plan(course.count, course.block, course.first, tuple(course.stages)) for course in courses
    ]
    vmem = pl.BlockSpec(memory_space=pltpu.VMEM)
    outs = [(4, 2, late[0], D // 4), courses[2].block, part.shape]
    outs += [(canvases,) + mine.shape[1:], (8, 128), soon.shape]
    return pl.pallas_call(
        partial(finish_kernel, n_mp, plan, top, masks, masks[1:]),
        in_specs=[pl.BlockSpec(memory_space=pl.ANY)] * len(courses) + [vmem] * (len(courses) + 4),
        out_specs=[vmem] * len(outs),
        out_shape=[jax.ShapeDtypeStruct(shape, F32) for shape in outs],
        scratch_shapes=scratch,
        compiler_params=pltpu.CompilerParams(
            collective_id=0, has_side_effects=True, vmem_limit_bytes=58 * 1024 * 1024
        ),
    )(*[course.sends for course in courses], *[course.keep for course in courses], part, mine, scalars, soon)


class Plan:
    def __init__(self, count, block, first, stages):
        self.count, self.block, self.first, self.stages = count, block, first, stages

    def sizes(self):
        return [self.count >> i for i in range(len(self.stages) + 1)]


def cap_grad_kernel(away, spot_ref, cap_ref, act_ref, dcap_ref, draw_ref, out_ref):
    block = pl.program_id(0) * 2 + (spot_ref[1] + away) % 2
    first, both = cap_ref.shape[1] // GL, (cap_ref.shape[1] + act_ref.shape[1]) // GL

    @pl.when(block < first)
    def _():
        rows = pl.ds(pl.multiple_of(block * GL, GL), GL)
        out_ref[0] = mm_tn(cap_ref[:, rows], dcap_ref[...]).astype(out_ref.dtype)

    @pl.when((block >= first) & (block < both))
    def _():
        rows = pl.ds(pl.multiple_of((block - first) * GL, GL), GL)
        out_ref[0] = mm_tn(act_ref[:, rows], draw_ref[...]).astype(out_ref.dtype)

    @pl.when(block >= both)
    def _():
        out_ref[0] = jnp.zeros((GL, D), out_ref.dtype)


def cap_grad(spot, arrays, blocks, away, dtype):
    return pl.pallas_call(
        partial(cap_grad_kernel, away),
        grid_spec=pltpu.PrefetchScalarGridSpec(
            num_scalar_prefetch=1,
            grid=(blocks // 2,),
            in_specs=[pl.BlockSpec(a.shape, lambda j, spot_ref: (0, 0)) for a in arrays],
            out_specs=pl.BlockSpec((1, GL, D), lambda j, spot_ref: (j, 0, 0)),
        ),
        out_shape=jax.ShapeDtypeStruct((blocks // 2, GL, D), dtype),
        compiler_params=pltpu.CompilerParams(
            dimension_semantics=("arbitrary",), vmem_limit_bytes=LIMIT
        ),
        cost_estimate=QUICK,
    )(spot, *arrays)


WIN = 256
QROWS = 512
BROWS = 512


def head_window(h):
    start = jnp.minimum(h * XHEAD // 128 * 128, D - WIN)
    lane = lax.broadcasted_iota(jnp.int32, (1, WIN), 1)
    mask = (lane >= h * XHEAD - start) & (lane < h * XHEAD - start + XHEAD)
    return pl.ds(pl.multiple_of(start, 128), WIN), mask


def cross_probs(q, keys, token_seg, text_seg):
    scores = mm_nt(q, keys) * XHEAD ** (-0.5)
    scores = jnp.where(token_seg == text_seg, scores, MASKED)
    top = jnp.max(scores, axis=-1, keepdims=True)
    probs = jnp.exp(scores - top)
    return probs * (1.0 / jnp.sum(probs, axis=-1, keepdims=True))


def cross_forward_kernel(q_ref, k_ref, v_ref, tok_ref, txt_ref, out_ref):
    win, mask = head_window(pl.program_id(0))
    keys, values = k_ref[:, win], v_ref[:, win]

    @pl.loop(0, q_ref.shape[0] // QROWS)
    def _(i):
        at = pl.ds(pl.multiple_of(i * QROWS, QROWS), QROWS)
        q = jnp.where(mask, q_ref[at, win], jnp.zeros((), BF16))
        probs = bf(cross_probs(q, keys, tok_ref[at, 0:1], txt_ref[...]))
        out_ref[at, win] = jnp.where(mask, bf(mm(probs, values)), out_ref[at, win])


def cross_forward(q, keys, values, token_seg, text_seg):
    n_tok = q.shape[0]
    n_txt = keys.shape[0]
    return pl.pallas_call(
        cross_forward_kernel,
        grid=(XHEADS,),
        in_specs=[
            whole_spec((n_tok, D)), whole_spec((n_txt, D)), whole_spec((n_txt, D)),
            whole_spec((n_tok, 1)), whole_spec((1, n_txt)),
        ],
        out_specs=whole_spec((n_tok, D)),
        out_shape=jax.ShapeDtypeStruct((n_tok, D), BF16),
        compiler_params=pltpu.CompilerParams(
            dimension_semantics=("arbitrary",), vmem_limit_bytes=LIMIT
        ),
        cost_estimate=QUICK,
    )(q, keys, values, token_seg, text_seg)


def cross_backward_kernel(
    q_ref, k_ref, v_ref, dc_ref, tok_ref, txt_ref, dq_ref, dk_ref, dv_ref, dk_acc, dv_acc
):
    win, mask = head_window(pl.program_id(0))
    keys, values = k_ref[:, win], v_ref[:, win]
    scale = XHEAD ** (-0.5)
    none = jnp.zeros((), BF16)
    dk_acc[...] = jnp.zeros_like(dk_acc)
    dv_acc[...] = jnp.zeros_like(dv_acc)

    @pl.loop(0, q_ref.shape[0] // BROWS)
    def _(i):
        at = pl.ds(pl.multiple_of(i * BROWS, BROWS), BROWS)
        q = jnp.where(mask, q_ref[at, win], none)
        dc = jnp.where(mask, dc_ref[at, win], none)
        probs = cross_probs(q, keys, tok_ref[at, 0:1], txt_ref[...])
        d_probs = mm_nt(dc, values)
        along = jnp.sum(probs * d_probs, axis=-1, keepdims=True)
        d_scores = bf(probs * (d_probs - along))
        dq_ref[at, win] = jnp.where(mask, bf(mm(d_scores, keys) * scale), dq_ref[at, win])
        dk_acc[...] += mm_tn(d_scores, q)
        dv_acc[...] += mm_tn(bf(probs), dc)

    dk_ref[:, win] = jnp.where(mask, dk_acc[...] * scale, dk_ref[:, win])
    dv_ref[:, win] = jnp.where(mask, dv_acc[...], dv_ref[:, win])


def cross_backward(q, keys, values, d_cross, token_seg, text_seg):
    n_tok = q.shape[0]
    n_txt = keys.shape[0]
    return pl.pallas_call(
        cross_backward_kernel,
        grid=(XHEADS,),
        in_specs=[
            whole_spec((n_tok, D)), whole_spec((n_txt, D)), whole_spec((n_txt, D)),
            whole_spec((n_tok, D)), whole_spec((n_tok, 1)), whole_spec((1, n_txt)),
        ],
        out_specs=[whole_spec((n_tok, D)), whole_spec((n_txt, D)), whole_spec((n_txt, D))],
        out_shape=[
            jax.ShapeDtypeStruct((n_tok, D), BF16),
            jax.ShapeDtypeStruct((n_txt, D), F32),
            jax.ShapeDtypeStruct((n_txt, D), F32),
        ],
        scratch_shapes=[pltpu.VMEM((n_txt, WIN), F32), pltpu.VMEM((n_txt, WIN), F32)],
        compiler_params=pltpu.CompilerParams(
            dimension_semantics=("arbitrary",), vmem_limit_bytes=LIMIT
        ),
        cost_estimate=QUICK,
    )(q, keys, values, d_cross, token_seg, text_seg)


GL = 128
GROUPS = D // GL


def parts(value):
    high = bf(value)
    return high, bf(value - wide(high))


def group_heads():
    row = lax.broadcasted_iota(jnp.int32, (GL, GL), 0) // HEAD
    col = lax.broadcasted_iota(jnp.int32, (GL, GL), 1) // HEAD
    return wide(row == col)


def both_segments(value, second):
    value = wide(value)
    late = value * second
    return bf(value - late), bf(late)


def state_kernel(k_ref, v_ref, sec_ref, kv_ref, ks_ref):
    same = group_heads()
    k0, k1 = both_segments(k_ref[...], sec_ref[...])
    kv_ref[0, 0] = mm_tn(k0, v_ref[...]) * same
    kv_ref[0, 1] = mm_tn(k1, v_ref[...]) * same
    ks_ref[0, 0] = jnp.broadcast_to(jnp.sum(wide(k0), axis=0, keepdims=True), (8, GL))
    ks_ref[0, 1] = jnp.broadcast_to(jnp.sum(wide(k1), axis=0, keepdims=True), (8, GL))


def attend(q_ref, sec_ref, kv_ref, ks_ref, same):
    q0, q1 = both_segments(q_ref[...], sec_ref[...])
    numer = 0.0
    denom = 1.0
    for i, q in enumerate((q0, q1)):
        for part in parts(kv_ref[0, i]):
            numer = numer + mm(q, part)
        sums = jnp.transpose(jnp.broadcast_to(ks_ref[0, i, 0:1], (GL, GL))) * same
        for part in parts(sums):
            denom = denom + mm(q, part)
    return q0, q1, numer, denom


def attend_kernel(q_ref, sec_ref, kv_ref, ks_ref, out_ref):
    _, _, numer, denom = attend(q_ref, sec_ref, kv_ref, ks_ref, group_heads())
    out_ref[...] = bf(numer / denom)


def attend_back_kernel(q_ref, da_ref, sec_ref, kv_ref, ks_ref, dq_ref, dkv_ref, dks_ref):
    same = group_heads()
    second = sec_ref[...]
    q0, q1, numer, denom = attend(q_ref, sec_ref, kv_ref, ks_ref, same)
    inverse = 1.0 / denom
    d_num = da_ref[...] * inverse
    high, low = parts(d_num * numer)
    ones = bf(same)
    d_den = -(mm(high, ones) + mm(low, ones)) * inverse
    d_parts = parts(d_num)
    back = []
    for i, q in enumerate((q0, q1)):
        total = 0.0
        grad = 0.0
        for part in d_parts:
            total = total + mm_tn(q, part)
        for part in parts(kv_ref[0, i]):
            for left in d_parts:
                grad = grad + mm_nt(left, part)
        dkv_ref[0, i] = total * same
        dks_ref[0, i] = jnp.broadcast_to(
            jnp.sum(wide(q) * d_den, axis=0, keepdims=True), (8, GL)
        )
        back.append(grad + d_den * ks_ref[0, i, 0:1])
    dq = jnp.where(second > 0, back[1], back[0])
    dq_ref[...] = bf(jnp.where(wide(q_ref[...]) > 0, dq, 0.0))


def state_back_kernel(k_ref, v_ref, sec_ref, dkv_ref, dks_ref, dk_ref, dv_ref):
    second = sec_ref[...] > 0
    k, v = k_ref[...], v_ref[...]
    dk, dv = [], []
    for i in range(2):
        grad_k = dks_ref[0, i, 0:1]
        grad_v = 0.0
        for part in parts(dkv_ref[0, i]):
            grad_k = grad_k + mm_nt(v, part)
            grad_v = grad_v + mm(k, part)
        dk.append(grad_k)
        dv.append(grad_v)
    dk_ref[...] = bf(jnp.where(wide(k) > 0, jnp.where(second, dk[1], dk[0]), 0.0))
    dv_ref[...] = bf(jnp.where(wide(v) > 0, jnp.where(second, dv[1], dv[0]), 0.0))


def by_group(kernel, n_tok, ins, outs, out_types):
    specs = dict(
        tok=pl.BlockSpec((n_tok, GL), lambda g: (0, g)),
        seg=whole_spec((n_tok, GL)),
        kv=pl.BlockSpec((1, 2, GL, GL), lambda g: (g, 0, 0, 0)),
        ks=pl.BlockSpec((1, 2, 8, GL), lambda g: (g, 0, 0, 0)),
    )
    shapes = dict(tok=(n_tok, D), kv=(GROUPS, 2, GL, GL), ks=(GROUPS, 2, 8, GL))
    return pl.pallas_call(
        kernel,
        grid=(GROUPS,),
        in_specs=[specs[i] for i in ins],
        out_specs=[specs[o] for o in outs],
        out_shape=[jax.ShapeDtypeStruct(shapes[o], t) for o, t in zip(outs, out_types)],
        compiler_params=pltpu.CompilerParams(
            dimension_semantics=("arbitrary",), vmem_limit_bytes=LIMIT
        ),
        cost_estimate=QUICK,
    )


def update(weight, grad, moment, average, factor, rate):
    clipped = factor * grad
    moment_new = MOMENTUM * moment + clipped
    weight_new = weight - rate * (clipped + MOMENTUM * moment_new)
    average_new = average + AVERAGE_RATE * (weight_new - average)
    return (weight_new, moment_new, average_new)


def local(
    n_dp, n_mp,
    latents, noise, captions, res_ids, timesteps, caption_lengths,
    in_proj, out_proj, w_up, w_down, cond, conv, tables,
    mom_in, mom_out, mom_up, mom_down, mom_cond, mom_conv, mom_tables,
    avg_in, avg_out, avg_up, avg_down, avg_cond, avg_conv, avg_tables,
):
    place = Place(n_dp, n_mp)
    y, c = place.y, place.c
    half_dp = n_dp // 2
    dl = D // n_dp
    spot = jnp.stack([y, c]).astype(jnp.int32)
    owner_rows = cond.shape[0]

    cond_b = bf(cond)
    units_b = unit_split(place, as_units(bf(in_proj), bf(out_proj)))
    cap_chunk = chunk_of(place, CAP_ROWS, GL if place.n <= 32 else 16)
    cap_mine = spread_rows(place, cond_b, TIME_ROWS, CAP_ROWS)
    packed = jnp.concatenate([units_b.reshape(-1, D), cap_mine], axis=0)
    ff_b = jnp.stack([bf(w_up[:, 0]), bf(w_up[:, 1]), bf(w_down).T])
    ff_b = jnp.pad(ff_b, ((0, 0), (0, 0), (0, FFB - ff_b.shape[2])))
    packed, ff_b, cond_time = lax.optimization_barrier((packed, ff_b, cond_b))
    got = lax.all_gather(packed, AXES, axis=0)
    by_place = got.reshape((n_dp, 2, 2) + packed.shape)
    w_q, w_k, w_v, w_o0, w_xq, w_o1, w_xk, w_xv = [
        by_place[:, i, j, part * dl : (part + 1) * dl].reshape(D, D)
        for part in (0, 1) for i in (0, 1) for j in (0, 1)
    ]
    cap_w = got[:, 2 * dl :].reshape(-1, D)
    w_cap1, w_cap2 = cap_w[:CAPD], cap_w[CAPD:CAP_ROWS]
    ffw = lax.all_gather(ff_b.reshape(3 * dl, FFB), AXES, axis=0)
    if dl % 16 == 0:
        ffw = ffw.reshape(n_dp, 4, 3 * dl, FFB)
    else:
        ffw = ffw.reshape(n_dp, 2, 2, 3, dl, FFB).transpose(3, 0, 4, 2, 1, 5)
        ffw = ffw.reshape(1, 1, 3 * D, FFP)

    spread_time = spread_rows(place, cond_time, 0, TIME_ROWS)
    w_time = gather_rows_all(place, spread_time, (place.x_mask, 2, 1))[:TIME_ROWS]
    facts = jnp.concatenate([timesteps, res_ids[:, None]], axis=1)
    for b in range(place.dp_bits):
        mask = n_mp << b
        facts = ordered(place.bit(mask), facts, place.swap(facts, mask), 0)
    steps_all = facts[:, :4].reshape(-1)
    count = jnp.sum(jnp.where(facts[:, 4] == 0, 4.0, 1.0))
    slots = steps_all.shape[0]

    resolution = lax.dynamic_index_in_dim(res_ids, y, 0, False)
    lengths = lax.dynamic_index_in_dim(caption_lengths, y, 0, False)
    steps_t = lax.dynamic_index_in_dim(timesteps, y, 0, False)
    pair = jnp.stack([latents, noise])
    quarters = jnp.stack([pair] + [place.swap(pair, mask) for mask in (1, 2, 3)])
    parts = [lax.dynamic_index_in_dim(quarters, (2 * c + j) ^ place.mp, 0, False) for j in (0, 1)]
    tokens = jnp.concatenate(
        [lax.dynamic_index_in_dim(part, y, 1, False) for part in parts], axis=1
    )
    n_tok = tokens.shape[1]
    rows = n_tok // SIDE
    grid = tokens.reshape(2, rows, SIDE, CIN)
    tokens = jnp.where(c == 1, grid[:, ::-1], grid).reshape(2, n_tok, CIN)
    clean, noisy = wide(tokens[0]), wide(tokens[1])
    col = jnp.arange(n_tok, dtype=jnp.int32)[:, None] % SIDE
    second = (col >= SIDE // 2) & (resolution == 0)
    seg0 = jnp.where(resolution == 0, 2 * c, 0)
    seg1 = jnp.where(resolution == 0, 2 * c + 1, 0)
    token_seg = jnp.where(second, seg1, seg0)

    def pick(table):
        first = lax.dynamic_index_in_dim(table, seg0, 0, True)
        other = lax.dynamic_index_in_dim(table, seg1, 0, True)
        return jnp.where(second, other, first)

    def by_segment(value):
        late = jnp.sum(jnp.where(second, value, 0.0), axis=0)
        early = jnp.sum(jnp.where(second, 0.0, value), axis=0)
        slot = jnp.arange(4, dtype=jnp.int32)[:, None]
        table = jnp.where(slot == seg0, early, 0.0) + jnp.where(slot == seg1, late, 0.0)
        return table, early + late

    sigma = pick(wide(steps_t)[:, None] / TMAX)
    mixed_in = (1.0 - sigma) * clean + sigma * noisy
    target = noisy - clean
    image_tokens = jnp.where(resolution == 0, (SIDE // 2) ** 2, SIDE * SIDE).astype(F32)
    loss_weight = 1.0 / (CIN * image_tokens * count)

    freq_b = bf(time_embed(steps_all))
    time_hidden = mm(freq_b, w_time[:FREQ])
    hidden_b = bf(jax.nn.silu(time_hidden))
    time_emb = mm(hidden_b, w_time[FREQ:])
    silu_b = bf(jax.nn.silu(time_emb))
    mod_mine = mm_nt(silu_b, cond_b).reshape(n_dp, 2, 1, 4 * owner_rows)
    mod_send = jnp.broadcast_to(mod_mine, (n_dp, 2, 2, 4 * owner_rows))
    mod_got = lax.all_to_all(mod_send.reshape(place.n, 4 * owner_rows), AXES, 0, 0)
    time_mod = mod_got.reshape(place.n, 4, owner_rows).transpose(1, 0, 2).reshape(4, -1)
    time_mod = time_mod[:, BLOCK_AT:].reshape(4, 6, D)
    mod_table = tables[None, :6] + time_mod
    mods = [pick(mod_table[:, k]) for k in range(6)]
    canvas = place.dp * 2 + y
    emb_mine = lax.dynamic_slice_in_dim(time_emb, canvas * 4, 4, 0)
    emb_tok = pick(emb_mine)

    own_cap = lax.dynamic_index_in_dim(captions, y, 0, False)
    their_cap = lax.dynamic_index_in_dim(captions, 1 - y, 0, False)
    caption = jnp.concatenate([own_cap, place.swap(their_cap, 2)], axis=0)
    quarter = own_cap.shape[0]
    within = jnp.arange(quarter, dtype=jnp.int32)
    text_at = jnp.concatenate([(place.mp ^ m) * quarter + within for m in (0, 2, 1, 3)])
    ends = jnp.cumsum(lengths)
    text_segment = jnp.sum((text_at[:, None] >= ends[None, :]).astype(jnp.int32), axis=1)
    cap_hidden = mm(caption, w_cap1)
    cap_act, gelu_pull = jax.vjp(partial(jax.nn.gelu, approximate=True), cap_hidden)
    cap_act_b = bf(cap_act)
    text_raw = mm(cap_act_b, w_cap2)
    gain = tables[8]
    text_inv = lax.rsqrt(jnp.mean(text_raw * text_raw, -1, keepdims=True) + EPS)
    text_hat = text_raw * text_inv
    text_b = bf(text_hat * gain)
    text_k = bf(mm(text_b, w_xk))
    text_v = bf(mm(text_b, w_xv))
    keys = jnp.concatenate([text_k, place.swap(text_k, 1)], axis=0)
    values = jnp.concatenate([text_v, place.swap(text_v, 1)], axis=0)

    embed = mm(mixed_in, tables[9 : 9 + CIN], HIGH)
    hat_a, inv_a = layer_norm(embed)
    normed_a = bf(hat_a * (1.0 + mods[1]) + mods[0])
    q = bf(jax.nn.relu(mm(normed_a, w_q)))
    k = bf(jax.nn.relu(mm(normed_a, w_k)))
    v = bf(jax.nn.relu(mm(normed_a, w_v)))
    whole_image = wide(resolution == 1)
    second_wide = jnp.broadcast_to(wide(second), (n_tok, GL))

    def shared(state, sums):
        first = jnp.concatenate([state[:, 0], sums[:, 0]], axis=1)
        first = first + whole_image * place.swap(first, 1)
        state = jnp.stack([first[:, :GL], state[:, 1]], axis=1)
        return state, jnp.stack([first[:, GL:], sums[:, 1]], axis=1)

    group_call = partial(by_group, n_tok=n_tok)
    state, key_sum = group_call(
        state_kernel, ins=("tok", "tok", "seg"), outs=("kv", "ks"), out_types=(F32, F32)
    )(k, v, second_wide)
    state, key_sum = shared(state, key_sum)
    (attn_b,) = group_call(
        attend_kernel, ins=("tok", "seg", "kv", "ks"), outs=("tok",), out_types=(BF16,)
    )(q, second_wide, state, key_sum)
    branch_a = mm_nt(attn_b, w_o0)
    state_a = embed + mods[2] * branch_a

    state_b = bf(state_a)
    xq = bf(mm(state_b, w_xq))
    cross_b = cross_forward(xq, keys, values, token_seg, text_segment[None, :])
    state_c = state_a + mm_nt(cross_b, w_o1)

    hat_f, inv_f = layer_norm(state_c)
    normed_f = bf(hat_f * (1.0 + mods[4]) + mods[3])
    taps = to_ff(conv)
    flipped = jnp.concatenate([taps[:, 6:9], taps[:, 3:6], taps[:, 0:3], taps[:, 9:]], axis=1)
    taps = jnp.where(c == 1, flipped, taps)
    column = jnp.arange(SIDE, dtype=jnp.int32)[:, None]
    middle = SIDE // 2
    left_ok = (column != 0) & ((resolution == 1) | (column != middle))
    right_ok = (column != SIDE - 1) & ((resolution == 1) | (column != middle - 1))
    left_ok = jnp.broadcast_to(wide(left_ok), (SIDE, CB))
    right_ok = jnp.broadcast_to(wide(right_ok), (SIDE, CB))
    halo_on = whole_image.reshape(1, 1)
    edge = n_tok - SIDE
    x_ext = jnp.concatenate([normed_f, place.swap(normed_f[edge:], 1)], axis=0)
    upper, z, gated_b, branch_f = ffn_forward(
        x_ext, ffw, taps, left_ok, right_ok, halo_on
    )
    z_halo = place.swap(z[:, edge:], 1)
    state_f = state_c + mods[5] * branch_f

    hat_o, inv_o = layer_norm(state_f)
    shift_o = tables[6] + emb_tok
    scale_o = tables[7] + emb_tok
    final = hat_o * (1.0 + scale_o) + shift_o
    out_rows = tables[9 + CIN :]
    output = mm_nt(final, out_rows, HIGH)
    error = output - target
    loss = jnp.sum(error * error) * loss_weight

    d_output = 2.0 * loss_weight * error
    d_final = mm(d_output, out_rows, HIGH)
    d_out_rows = mm_tn(d_output, final, HIGH)
    d_shift_seg, d_shift_o = by_segment(d_final)
    d_scale_seg, d_scale_o = by_segment(d_final * hat_o)
    d_emb_mine = d_shift_seg + d_scale_seg
    d_emb = d_emb_mine + place.swap(d_emb_mine, 1)
    d_state_f = layer_norm_back(d_final * (1.0 + scale_o), hat_o, inv_o)

    split_dp = (2,) * place.dp_bits
    far = [(b, n_mp << (place.dp_bits - 1 - b)) for b in range(place.dp_bits - 2, -1, -1)]

    def stages(lead, order):
        table = {
            "x": ("abs", lead + place.dp_bits - 1, place.x_mask),
            "y": ("rel", lead - 1, 2),
        }
        rest = [("abs", lead + axis, mask) for axis, mask in far]
        return [table[o] if o in table else rest.pop(0) for o in order] + rest

    def ff_flow(left, right, orders):
        shape = (1, 2) + split_dp + (dl, FFB)
        flows = []
        for i, order in enumerate(orders):
            away = ff_grad(spot, left, right, i, 1, BF16)
            flows.append(Flow(place, away.reshape(shape), stages(2, order)))
            left, right, away = lax.optimization_barrier((left, right, away))
        for i, flow in enumerate(flows):
            flow.keep = ff_grad(spot, left, right, i, 0, BF16).reshape(shape)
        return flows

    def unit_flow(arrays, pairs, order):
        shape = (2,) + split_dp + (dl, D)
        blocks = n_dp if dl % 16 == 0 else 1
        away = unit_grad(spot, arrays, pairs, 1, BF16, blocks)
        flow = Flow(place, away.reshape(shape), stages(1, order))
        arrays, away = lax.optimization_barrier((arrays, away))
        flow.keep = unit_grad(spot, arrays, pairs, 0, BF16, blocks).reshape(shape)
        return flow

    def settle(value, flows):
        value, keeps = lax.optimization_barrier((value, [flow.keep for flow in flows]))
        for flow, keep in zip(flows, keeps):
            flow.keep = keep
        return tick(value, flows)

    d_branch_f = bf(mods[5] * d_state_f)
    d_edge = place.swap(d_branch_f[edge:], 1)
    flow_dn, = ff_flow(d_branch_f, gated_b[None], ["yx"])
    d_ext = jnp.concatenate([d_branch_f, d_edge], axis=0)
    d_ext = settle(d_ext, [flow_dn])
    d_upper, d_taps, d_normed_f = tick(
        ffn_backward(d_ext, ffw, upper, z, z_halo, taps, left_ok, right_ok, halo_on), [flow_dn]
    )
    unflipped = jnp.concatenate(
        [d_taps[:, 6:9], d_taps[:, 3:6], d_taps[:, 0:3], d_taps[:, 9:]], axis=1
    )
    conv_grad = from_ff(jnp.where(c == 1, unflipped, d_taps))
    flow_up = ff_flow(normed_f, d_upper, ["xy", "yx"])
    ffn_flows = [flow_dn] + flow_up
    soon = jnp.concatenate([conv_grad.reshape(-1, D), d_out_rows], axis=0)
    soon_masks = [1, 2] + [n_mp << b for b in range(place.dp_bits)]
    soon_sent = place.swap(soon, soon_masks[0])
    d_normed_f, soon_sent = settle((d_normed_f, soon_sent), flow_up)
    soon = soon + soon_sent
    d_state_c = d_state_f + layer_norm_back(d_normed_f * (1.0 + mods[4]), hat_f, inv_f)
    d_mods = [None] * 6
    d_mods[5] = by_segment(d_state_f * branch_f)
    d_mods[3] = by_segment(d_normed_f)
    d_mods[4] = by_segment(d_normed_f * hat_f)

    d_branch_c = bf(d_state_c)
    d_cross = bf(mm(d_branch_c, w_o1))
    soon_sent = place.swap(soon, soon_masks[1])
    (d_xq_b, d_keys, d_values), soon_sent = tick(
        (
            cross_backward(xq, keys, values, d_cross, token_seg, text_segment[None, :]),
            soon_sent,
        ),
        ffn_flows,
    )
    soon = soon + soon_sent
    half_txt = TXT // 2
    d_kv = jnp.stack([d_keys, d_values])
    d_kv = d_kv[:, :half_txt] + place.swap(d_kv[:, half_txt:], 1)
    d_kv_b = bf(d_kv)
    early = unit_flow(
        [state_b, d_xq_b, d_branch_c, cross_b, text_b, d_kv_b[0], d_kv_b[1]],
        ((0, 1), (2, 3), (4, 5), (4, 6)),
        "yzx",
    )
    d_state_a = d_state_c + mm_nt(d_xq_b, w_xq)
    soon_sent = place.swap(soon, soon_masks[2])
    d_state_a, d_kv_b, soon_sent = settle((d_state_a, d_kv_b, soon_sent), [early])
    soon = soon + soon_sent

    d_branch_a = bf(mods[2] * d_state_a)
    d_mods[2] = by_segment(d_state_a * branch_a)
    d_attn = mm(d_branch_a, w_o0)
    soon_sent = place.swap(soon, soon_masks[3])
    (dq_b, d_state, d_sum), soon_sent = tick(
        (group_call(
            attend_back_kernel,
            ins=("tok", "tok", "seg", "kv", "ks"),
            outs=("tok", "kv", "ks"),
            out_types=(BF16, F32, F32),
        )(q, d_attn, second_wide, state, key_sum), soon_sent),
        ffn_flows,
    )
    soon = soon + soon_sent
    d_state, d_sum = shared(d_state, d_sum)
    dk_b, dv_b = group_call(
        state_back_kernel,
        ins=("tok", "tok", "seg", "kv", "ks"),
        outs=("tok", "tok"),
        out_types=(BF16, BF16),
    )(k, v, second_wide, d_state, d_sum)
    d_normed_a = mm_nt(dq_b, w_q) + mm_nt(dk_b, w_k) + mm_nt(dv_b, w_v)
    d_mods[0] = by_segment(d_normed_a)
    d_mods[1] = by_segment(d_normed_a * hat_a)

    d_mod = jnp.stack([table for table, _ in d_mods], axis=1).reshape(4, 6 * D)
    d_mod = jnp.pad(d_mod, ((0, 0), (BLOCK_AT, 0)))
    d_mod = d_mod.reshape(4, place.n, owner_rows).transpose(1, 0, 2)
    d_mod, dq_b, dk_b, dv_b = lax.optimization_barrier((d_mod, dq_b, dk_b, dv_b))
    d_mod = lax.all_to_all(d_mod, AXES, 0, 0)
    late = unit_flow(
        [normed_a, dq_b, dk_b, dv_b, d_branch_a, attn_b],
        ((0, 1), (0, 2), (0, 3), (4, 5)),
        "xy",
    )
    d_embed = d_state_a + layer_norm_back(d_normed_a * (1.0 + mods[1]), hat_a, inv_a)
    g_patch = mm_tn(mixed_in, d_embed, HIGH)
    d_mod, d_kv_b, g_patch, late.keep, late.moving = lax.optimization_barrier(
        (d_mod, d_kv_b, g_patch, late.keep, late.moving)
    )
    near_far = [stage for stage in stages(1, "") if stage[1] != 1]
    late_flows = late.split(
        1, [stages(1, order)[:2] + near_far for order in ("xy", "yx")]
    )
    d_mod, d_kv_b = tick((d_mod, d_kv_b), ffn_flows)
    for flow in late_flows:
        flow.land()
    d_mod = d_mod.reshape(slots // 4, 2, 4, owner_rows).sum(1).reshape(slots, owner_rows)
    d_silu = mm(d_mod, wide(cond_b), HIGH)
    g_block = mm_tn(d_mod, wide(silu_b), HIGH)

    d_text = mm_nt(d_kv_b[0], w_xk) + mm_nt(d_kv_b[1], w_xv)
    d_gain = jnp.sum(d_text * text_hat, axis=0)
    d_hat = d_text * gain
    d_text_raw = text_inv * (d_hat - text_hat * jnp.mean(d_hat * text_hat, -1, keepdims=True))
    d_text_raw_b = bf(d_text_raw)
    d_cap_b = bf(gelu_pull(mm_nt(d_text_raw_b, w_cap2))[0])
    cap_shape = split_dp + (2, 1, cap_chunk, D)
    if cap_chunk == GL:
        cap_parts = [caption, cap_act_b, d_cap_b, d_text_raw_b]
        cap_sends = cap_grad(spot, cap_parts, place.n, 1, BF16).reshape(cap_shape)
        cap_keep = partial(cap_grad, spot, cap_parts, place.n, 0, BF16)
    else:
        g_cap = jnp.concatenate(
            [
                mm_tn(caption, d_cap_b),
                mm_tn(cap_act_b, d_text_raw_b),
                jnp.zeros((place.n * cap_chunk - CAP_ROWS, D), F32),
            ],
            axis=0,
        ).reshape(split_dp + (2, 2, cap_chunk, D))
        cap_sends = bf(lax.dynamic_slice_in_dim(g_cap, 1 - c, 1, place.dp_bits + 1))
        cap_keep = partial(lax.dynamic_slice_in_dim, g_cap, c, 1, place.dp_bits + 1)

    for mask in soon_masks[4:-1]:
        soon = soon + place.swap(soon, mask)
    soon_rows = soon.shape[0]
    soon = jnp.pad(soon, ((0, -soon_rows % 8), (0, 0)))

    d_rows_six = jnp.stack([total for _, total in d_mods])
    tables_grad = jnp.concatenate(
        [d_rows_six, d_shift_o[None], d_scale_o[None], d_gain[None], g_patch], axis=0
    )
    masks = [1, 2] + [n_mp << b for b in range(place.dp_bits)]
    d_silu = jnp.broadcast_to(d_silu.reshape(n_dp, 2, 1, 4 * D), (n_dp, 2, 2, 4 * D))
    d_silu = lax.all_to_all(d_silu.reshape(place.n, 4 * D), AXES, 0, 0).sum(0).reshape(4, D)
    cap_flow = Flow(
        place,
        cap_sends,
        [("abs", place.dp_bits, 2), ("abs", place.dp_bits - 1, place.x_mask)]
        + [("abs",) + pair_ for pair_ in far],
    )
    cap_flow.keep = cap_keep().reshape(cap_shape)
    d_time = d_silu * silu_grad(emb_mine) + d_emb
    d_hidden = mm_nt(d_time, wide(w_time[FREQ:]), HIGH)
    hidden_mine = lax.dynamic_slice_in_dim(time_hidden, canvas * 4, 4, 0)
    d_times = jnp.concatenate([d_time, d_hidden * silu_grad(hidden_mine)], axis=0)
    cap_far = [stage for stage in [("abs",) + pair_ for pair_ in far] if stage[1] != 0]
    cap_y, cap_x = ("abs", place.dp_bits, 2), ("abs", place.dp_bits - 1, place.x_mask)
    cap_flows = cap_flow.split(0, [[cap_y, cap_x] + cap_far, cap_far[:1] + [cap_y, cap_x] + cap_far[1:]])
    last = late_flows + cap_flows + [early]
    for flow in cap_flows:
        flow.land()
    d_times, early.moving = lax.optimization_barrier((d_times, early.moving))
    early.land()
    ff_own = [flow.drain().reshape(dl, FFB)[:, : FF // 4] for flow in ffn_flows]
    part_sq = sum(jnp.sum(grad * grad) for grad in [g_block] + ff_own)
    row = lax.broadcasted_iota(jnp.int32, (8, 128), 0)
    scalars = jnp.where(row == 0, part_sq, loss)
    small = jnp.pad(tables_grad, ((0, -tables_grad.shape[0] % 8), (0, 0)))
    top = n_mp << place.dp_bits - 1
    joined, cap_own, small, d_times, scalars, soon = finish(
        n_mp, last, top, masks, small, d_times[None], scalars, soon
    )
    conv_grad = soon[: conv_grad.size // D].reshape(conv_grad.shape)
    d_out_rows = soon[conv_grad.size // D : soon_rows]
    tables_grad = jnp.concatenate([small[: tables_grad.shape[0]], d_out_rows], axis=0)
    d_times = d_times.reshape(-1, 2, 4, D).transpose(1, 0, 2, 3).reshape(2, slots, D)
    g_time2 = mm_tn(wide(hidden_b), d_times[0], HIGH)
    g_time1 = mm_tn(wide(freq_b), d_times[1], HIGH)
    spots = -(-TIME_ROWS // owner_rows)
    g_time = jnp.concatenate(
        [g_time1, g_time2, jnp.zeros(((spots + 1) * owner_rows - TIME_ROWS, D), F32)], axis=0
    )
    g_time = lax.dynamic_slice_in_dim(
        g_time, jnp.minimum(place.me, spots) * owner_rows, owner_rows, 0
    )

    cap_own = cap_own.reshape(cap_chunk, D)
    g_cap = collect_rows(place, cap_own, owner_rows, TIME_ROWS, CAP_ROWS)
    g_cond = g_cap + g_block + g_time
    g_in, g_out = from_units(joined.transpose(1, 0, 2, 3).reshape(8, dl, D // 4))
    g_upper = jnp.stack(ff_own[1:], axis=1)
    g_lower = ff_own[0].T
    owned = (g_in, g_out, g_upper, g_lower, g_cond)

    squares, loss = scalars[0, 0], scalars[1, 0]
    squares = squares + jnp.sum(g_time1 * g_time1) + jnp.sum(g_time2 * g_time2)
    norm = jnp.sqrt(squares + jnp.sum(conv_grad * conv_grad) + jnp.sum(tables_grad * tables_grad))
    factor = CLIP / jnp.maximum(norm, CLIP)
    rate = STEP_SCALE * math.sqrt(PARAMS) / CLIP
    grads = owned + (conv_grad, tables_grad)
    weights = (in_proj, out_proj, w_up, w_down, cond, conv, tables)
    moments = (mom_in, mom_out, mom_up, mom_down, mom_cond, mom_conv, mom_tables)
    averages = (avg_in, avg_out, avg_up, avg_down, avg_cond, avg_conv, avg_tables)
    new = [
        update(weights[i], grads[i], moments[i], averages[i], factor, rate) for i in range(7)
    ]
    moments_out = [new[i][1] for i in range(5)] + [factor * conv_grad, new[6][1]]
    return (loss, norm, *[n[0] for n in new], *moments_out, *[n[2] for n in new])


def solution(mesh):
    tokens = P("dp", "mp", None)
    weights = (
        P("dp", None, "mp"),
        P(None, "mp", "dp"),
        P("dp", None, "mp"),
        P("mp", "dp"),
        P(("dp", "mp"), None),
        P(),
        P(),
    )
    in_specs = (tokens, tokens, tokens, P("dp"), P("dp", None), P("dp", None)) + weights * 3
    out_specs = (P(), P()) + weights * 3
    body = partial(local, mesh.shape["dp"], mesh.shape["mp"])
    return jax.shard_map(body, mesh=mesh, in_specs=in_specs, out_specs=out_specs, check_vma=False)
```
